256 devices in a mesh: lat: 8 (over x, core), lon: 32 (over y, z).
Axes of the slice: x: 4, y: 4, z: 8, core: 2. Of those that a mesh axis runs over, the one named last changes fastest.
Arguments:
- fields: float32 [256, 512, 320], P('lat', 'lon'), may hold values from -6 to 6
- wind_east: float32 [256, 512, 64], P('lat', 'lon'), may hold values from -0.45 to 0.45
- wind_north: float32 [256, 512, 64], P('lat', 'lon'), may hold values from -0.45 to 0.45
- owner: int32 [8, 128], P('lat', 'lon'), may hold values from 0 to 31, as said below
- counts: int32 [8, 128], P('lat', 'lon'), may hold values from 8 to 128
- w_in: bfloat16 [32, 320, 512], P('lon'), may hold values from -0.3125 to 0.3125
- w_two: bfloat16 [32, 512, 512], P('lon'), may hold values from -0.25 to 0.25
- w_three: bfloat16 [32, 512, 512], P('lon'), may hold values from -0.25 to 0.25
- w_out: bfloat16 [32, 512, 320], P('lon'), may hold values from -0.25 to 0.25
Outputs:
- updated: float32 [256, 512, 320], P('lat', 'lon')
The draws below stay inside these ranges and needn't reach their ends.
Inputs may be any that keep to these rules, and one draw needn't show every extreme that they name: `owner`: each entry is the lon index whose scheme takes the block. Every device sends at most 1 block to any one device of its lat slab, and every device takes exactly 4 blocks.
All inputs are finite; a program needn't handle non-finite values.
Results may differ from the reference program's by a relative error of at most 0.003.
Values may be sent and summed in bfloat16 or wider, within the bound.
A program may use at most 64 MiB of HBM per device.

```python
import jax
import jax.numpy as jnp
from jax import lax

FIELDS = 5
LEVELS = 64
HIDDEN_SIZE = 512
COLS = 128
STEPS = 2
SWEEPS = 2
CLAT = 32
CLON = 16
FEAT = 320
BLK_DEV = 4
EXPERTS = 32
NLAT = 256
NLON = 512
LAT_SLABS = 8
OWNED = 128
N_LAT = 8
N_LON = 32


def draw_owner(key, part):
    key = jax.random.fold_in(key, 11)

    def one_slab(slab_key):
        key_sigma, key_tau, key_rho = jax.random.split(slab_key, 3)
        sigma = jax.random.permutation(key_sigma, N_LON)
        offsets = jax.random.permutation(key_tau, N_LON)
        orders = jax.vmap(lambda inner_key: jax.random.permutation(inner_key, BLK_DEV))(jax.random.split(key_rho, N_LON))
        stride = jnp.arange(BLK_DEV, dtype=jnp.int32)
        target = sigma[(offsets[:, None] + stride[None, :]) % N_LON]
        inverse = jnp.argsort(orders, axis=1)
        return jnp.take_along_axis(target, inverse, axis=1).reshape(-1)
    return jax.vmap(one_slab)(jax.random.split(key, N_LAT)).astype(jnp.int32)


def place_ends(array, stream_key, smallest, high):
    place = [jax.random.randint(jax.random.fold_in(stream_key, axis), (), 0, length) for axis, length in enumerate(array.shape)]
    longest = array.shape.index(max(array.shape))
    neighbour = place[:longest] + [(place[longest] + 1) % array.shape[longest]] + place[longest + 1:]
    return array.at[tuple(place)].set(smallest).at[tuple(neighbour)].set(high)


def levels(rng, shape, cuts, least, top_value):
    level, own = 1.0, jax.random.fold_in(rng, 6)
    for axis_at, blocks in cuts:
        heights = jnp.exp(jax.random.uniform(jax.random.fold_in(own, axis_at), (blocks,), jnp.float32, least / len(cuts), top_value / len(cuts)))
        level = level * jnp.repeat(heights, shape[axis_at] // blocks).reshape([-1 if axis == axis_at else 1 for axis in range(len(shape))])
    return level


def gaussian(own_key, extent, width, limit, cuts=(), held_as=jnp.bfloat16):
    gain = levels(own_key, extent, cuts, -0.22, 0.18) if cuts else 1.0
    drawn = jax.random.normal(own_key, extent, jnp.float32) * width * gain
    return jnp.minimum(jnp.maximum(drawn, -limit), limit).astype(held_as)


def setup_inputs(seed: int = 0) -> dict:
    key_of = jax.random.split(jax.random.key(seed), 10)
    return {
        "fields": gaussian(key_of[0], (NLAT, NLON, FEAT), 1.0, 6.0, ((0, 8), (1, 32)), jnp.float32),
        "wind_east": jnp.clip(jax.random.uniform(key_of[1], (NLAT, NLON, LEVELS), jnp.float32, -0.45, 0.45) * levels(key_of[1], (NLAT, NLON, LEVELS), ((0, 8), (1, 32)), -0.4, 0.0), -0.45, 0.45),
        "wind_north": jnp.clip(jax.random.uniform(key_of[2], (NLAT, NLON, LEVELS), jnp.float32, -0.45, 0.45) * levels(key_of[2], (NLAT, NLON, LEVELS), ((0, 8), (1, 32)), -0.4, 0.0), -0.45, 0.45),
        "owner": draw_owner(jax.random.fold_in(key_of[9], 71), 0),
        "counts": place_ends(jax.random.randint(key_of[4], (LAT_SLABS, OWNED), 8, 129), jax.random.fold_in(key_of[4], 1), 8, 128).astype(jnp.int32),
        "w_in": gaussian(key_of[5], (EXPERTS, FEAT, HIDDEN_SIZE), FEAT ** -0.5, 0.3125, ((0, 32),)),
        "w_two": gaussian(key_of[6], (EXPERTS, HIDDEN_SIZE, HIDDEN_SIZE), HIDDEN_SIZE ** -0.5, 0.25, ((0, 32),)),
        "w_three": gaussian(key_of[7], (EXPERTS, HIDDEN_SIZE, HIDDEN_SIZE), HIDDEN_SIZE ** -0.5, 0.25, ((0, 32),)),
        "w_out": gaussian(key_of[8], (EXPERTS, HIDDEN_SIZE, FEAT), HIDDEN_SIZE ** -0.5, 0.25, ((0, 32),)),
    }


def advect(fields_now, east_face, north_eff):
    shaped = fields_now.reshape(NLAT, NLON, FIELDS, LEVELS)
    east_pos = jnp.maximum(east_face, 0.0)[:, :, None, :]
    east_neg = jnp.minimum(east_face, 0.0)[:, :, None, :]
    north_pos = jnp.maximum(north_eff, 0.0)[:, :, None, :]
    north_neg = jnp.minimum(north_eff, 0.0)[:, :, None, :]
    eastern = jnp.roll(shaped, -1, axis=1)
    flux_east = east_pos * shaped + east_neg * eastern
    flux_west = jnp.roll(flux_east, 1, axis=1)
    northern = jnp.concatenate([shaped[1:], jnp.zeros_like(shaped[:1])], axis=0)
    flux_north = north_pos * shaped + north_neg * northern
    flux_south = jnp.concatenate([jnp.zeros_like(flux_north[:1]), flux_north[:-1]], axis=0)
    result = shaped - (flux_east - flux_west) - (flux_north - flux_south)
    return result.reshape(NLAT, NLON, FEAT)


def column_net(blocks, schemes, w_in, w_two, w_three, w_out):
    def single(pair):
        block, scheme = pair
        hidden_one = jax.nn.silu(jnp.dot(block, w_in[scheme], preferred_element_type=jnp.float32)).astype(jnp.bfloat16)
        hidden_two = jax.nn.silu(jnp.dot(hidden_one, w_two[scheme], preferred_element_type=jnp.float32)).astype(jnp.bfloat16)
        hidden_three = jax.nn.silu(jnp.dot(hidden_two, w_three[scheme], preferred_element_type=jnp.float32)).astype(jnp.bfloat16)
        return jnp.dot(hidden_three, w_out[scheme], preferred_element_type=jnp.float32).astype(jnp.bfloat16)
    return lax.map(single, (blocks, schemes), batch_size=32)


def reference(fields, wind_east, wind_north, owner, counts, w_in, w_two, w_three, w_out):
    row_index = jnp.arange(NLAT, dtype=jnp.int32)
    east_face = 0.5 * (wind_east + jnp.roll(wind_east, -1, axis=1))
    north_next = jnp.concatenate([wind_north[1:], jnp.zeros_like(wind_north[:1])], axis=0)
    north_eff = 0.5 * (wind_north + north_next) * (row_index < NLAT - 1).astype(jnp.float32)[:, None, None]
    cell_index = jnp.arange(COLS, dtype=jnp.int32)
    live_mask = (cell_index[None, :] < counts.reshape(-1)[:, None]).astype(jnp.float32)[:, :, None]
    schemes = owner.reshape(-1)
    current = fields
    for step_index in range(STEPS):
        for sweep_index in range(SWEEPS):
            current = advect(current, east_face, north_eff)
        column = current.astype(jnp.bfloat16).reshape(N_LAT, CLAT, N_LON, CLON, FEAT)
        blocks = column.transpose(0, 2, 1, 3, 4).reshape(N_LAT * N_LON * BLK_DEV, COLS, FEAT)
        tendency = column_net(blocks, schemes, w_in, w_two, w_three, w_out)
        added = tendency.astype(jnp.float32) * live_mask
        spread = added.reshape(N_LAT, N_LON, CLAT, CLON, FEAT).transpose(0, 2, 1, 3, 4).reshape(NLAT, NLON, FEAT)
        current = current + spread
    return current
```

```python
import functools

import jax
import jax.numpy as jnp
from jax import lax
from jax.experimental import pallas as pl
from jax.experimental.pallas import tpu as pltpu
from jax.sharding import PartitionSpec as P

F32 = jnp.float32
BF16 = jnp.bfloat16
MESH = pl.DeviceIdType.MESH

STEPS = 2
COLS = 128
ROWS = 32
WIDE = 16
FEAT = 320
LEVELS = 64
HID = 512
BLKS = 4
GROUPS = 4
EXT_R = ROWS + 4
EXT_C = 24
CELLS = ROWS * WIDE
GROUP_ROWS = CELLS // GROUPS
TILES = ((0, 128), (128, 256), (256, 320))


def silu(x):
    half = 0.5 * x
    return half + half * jnp.tanh(half)


def roll(x, shift):
    return pltpu.roll(x, shift % x.shape[0], axis=0)


def kernel(
    n_lat,
    n_lon,
    fields,
    wind_east,
    wind_north,
    owner,
    counts,
    w_in,
    w_two,
    w_three,
    w_out,
    out,
    x,
    z,
    wind,
    raw_east,
    raw_north,
    coef,
    side_out,
    side_in,
    wside_out,
    wside_in,
    corner_out,
    corner_in,
    cur_bf,
    send_one,
    recv_one,
    send_two,
    recv_two,
    send_three,
    recv_three,
    send_four,
    recv_four,
    perm,
    perm_t,
    result,
    v_in,
    v_two,
    v_three,
    v_out,
    load_sem,
    halo_send,
    halo_recv,
    wind_send,
    wind_recv,
    ex_send,
    ex_recv,
    out_sem,
):
    near = n_lon // GROUPS
    piece = COLS // n_lon
    msg = BLKS * piece
    me_lat = lax.axis_index("lat")
    me = lax.axis_index("lon")
    my_group = me // near
    my_near = me % near
    north = lax.rem(me_lat + 1, n_lat)
    south = lax.rem(me_lat + n_lat - 1, n_lat)
    east = lax.rem(me + 1, n_lon)
    west = lax.rem(me + n_lon - 1, n_lon)
    corners = ((south, west), (south, east), (north, west), (north, east))

    def peer(group_step, near_step):
        group = lax.rem(my_group + group_step, GROUPS)
        return group * near + lax.rem(my_near + near_step, near)

    loads = [
        pltpu.make_async_copy(wind_east, raw_east, load_sem.at[0]),
        pltpu.make_async_copy(wind_north, raw_north, load_sem.at[1]),
        pltpu.make_async_copy(
            fields, x.at[0, pl.ds(2, ROWS), pl.ds(0, WIDE), :], load_sem.at[2]
        ),
        pltpu.make_async_copy(w_in, v_in, load_sem.at[3]),
        pltpu.make_async_copy(w_two, v_two, load_sem.at[4]),
        pltpu.make_async_copy(w_three, v_three, load_sem.at[5]),
        pltpu.make_async_copy(w_out, v_out, load_sem.at[6]),
    ]
    for load in loads:
        load.start()

    barrier = pltpu.get_barrier_semaphore()

    def greet(step, carry):
        pl.semaphore_signal(
            barrier,
            inc=1,
            device_id=(me_lat, lax.rem(me + step, n_lon)),
            device_id_type=MESH,
        )
        return carry

    lax.fori_loop(1, n_lon, greet, 0)
    for there in ((south, me), (north, me)) + corners:
        pl.semaphore_signal(barrier, inc=1, device_id=there, device_id_type=MESH)

    def clear(r, carry):
        x[0, r, pl.ds(WIDE, 8), :] = jnp.zeros((8, FEAT), F32)
        x[1, r, pl.ds(WIDE, 8), :] = jnp.zeros((8, FEAT), F32)
        wind[r, pl.ds(WIDE, 8), :] = jnp.zeros((8, 2 * LEVELS), F32)
        return carry

    lax.fori_loop(0, EXT_R, clear, 0)

    loads[0].wait()
    loads[1].wait()

    def join(r, carry):
        wind[r + 2, pl.ds(0, WIDE), :] = jnp.concatenate([raw_east[r], raw_north[r]], axis=-1)
        return carry

    lax.fori_loop(0, ROWS, join, 0)
    loads[2].wait()

    def remote(src, dst, send, recv, where):
        return pltpu.make_async_remote_copy(
            src_ref=src,
            dst_ref=dst,
            send_sem=send,
            recv_sem=recv,
            device_id=where,
            device_id_type=MESH,
        )

    def halo_copies(step):
        grid = x.at[step]
        inner = pl.ds(0, WIDE)
        copies = [
            remote(
                grid.at[pl.ds(2, 2), inner, :],
                grid.at[pl.ds(ROWS + 2, 2), inner, :],
                halo_send.at[step, 0],
                halo_recv.at[step, 0],
                (south, me),
            ),
            remote(
                grid.at[pl.ds(ROWS, 2), inner, :],
                grid.at[pl.ds(0, 2), inner, :],
                halo_send.at[step, 1],
                halo_recv.at[step, 1],
                (north, me),
            ),
        ]
        for side, there in enumerate((west, east)):
            copies.append(
                remote(
                    side_out.at[step, side],
                    side_in.at[step, side],
                    halo_send.at[step, 2 + side],
                    halo_recv.at[step, 2 + side],
                    (me_lat, there),
                )
            )
        for at, there in enumerate(corners):
            copies.append(
                remote(
                    corner_out.at[step, at],
                    corner_in.at[step, at],
                    halo_send.at[step, 4 + at],
                    halo_recv.at[step, 4 + at],
                    there,
                )
            )
        return copies

    def wind_copies():
        inner = pl.ds(0, WIDE)
        copies = [
            remote(
                wind.at[pl.ds(2, 2), inner, :],
                wind.at[pl.ds(ROWS + 2, 2), inner, :],
                wind_send.at[0],
                wind_recv.at[0],
                (south, me),
            ),
            remote(
                wind.at[pl.ds(ROWS, 2), inner, :],
                wind.at[pl.ds(0, 2), inner, :],
                wind_send.at[1],
                wind_recv.at[1],
                (north, me),
            ),
        ]
        for side, there in enumerate((west, east)):
            copies.append(
                remote(
                    wside_out.at[side],
                    wside_in.at[side],
                    wind_send.at[2 + side],
                    wind_recv.at[2 + side],
                    (me_lat, there),
                )
            )
        return copies

    corner_cells = ((2, 0), (2, WIDE - 1), (ROWS + 1, 0), (ROWS + 1, WIDE - 1))
    corner_slots = ((ROWS + 2, 16), (ROWS + 2, 23), (1, 16), (1, 23))
    side_cells = ((0, 1), (WIDE - 2, WIDE - 1))
    side_slots = ((16, 17), (22, 23))

    def stage_halo(step):
        for side in range(2):
            for at in range(2):
                side_out[step, side, at] = x[step, pl.ds(2, ROWS), side_cells[side][at], :]
        for at, (r, c) in enumerate(corner_cells):
            corner_out[step, at, pl.ds(0, 1), :] = x[step, r, pl.ds(c, 1), :]

    def place_halo(step):
        for side in range(2):
            for at in range(2):
                x[step, pl.ds(2, ROWS), side_slots[side][at], :] = side_in[step, side, at]
        for at, (r, c) in enumerate(corner_slots):
            x[step, r, pl.ds(c, 1), :] = corner_in[step, at, pl.ds(0, 1), :]

    corner_out[...] = jnp.zeros_like(corner_out)
    stage_halo(0)
    for side in range(2):
        for at in range(2):
            wside_out[side, at] = wind[pl.ds(2, ROWS), side_cells[side][at], :]
    for at, (r, c) in enumerate(corner_cells):
        corner_out[0, at, pl.ds(1, 1), pl.ds(0, 128)] = wind[r, pl.ds(c, 1), :]

    pl.semaphore_wait(barrier, n_lon - 1 + 6)

    winds = wind_copies()
    first = halo_copies(0)
    for copy in winds + first:
        copy.start()

    row_i = lax.broadcasted_iota(jnp.int32, (GROUP_ROWS, GROUP_ROWS), 0)
    col_i = lax.broadcasted_iota(jnp.int32, (GROUP_ROWS, GROUP_ROWS), 1)

    def slot_of(cell):
        blk = cell // (2 * WIDE)
        at = cell % (2 * WIDE)
        return (at // piece) * msg + blk * piece + at % piece

    shuffle = jnp.where(row_i == slot_of(col_i), 1.0, 0.0).astype(BF16)
    unshuffle = jnp.where(slot_of(row_i) == col_i, 1.0, 0.0).astype(BF16)

    for copy in winds + first:
        copy.wait_recv()
    for side in range(2):
        for at in range(2):
            wind[pl.ds(2, ROWS), side_slots[side][at], :] = wside_in[side, at]
    for at, (r, c) in enumerate(corner_slots):
        wind[r, pl.ds(c, 1), :] = corner_in[0, at, pl.ds(1, 1), pl.ds(0, 128)]
    place_halo(0)

    first_row = me_lat * ROWS
    last_face = n_lat * ROWS - 1
    low_half = lax.broadcasted_iota(jnp.int32, (EXT_C, 128), 1) < LEVELS

    def both(row):
        turned = pltpu.roll(row, LEVELS, axis=1)
        return jnp.where(low_half, row, turned), jnp.where(low_half, turned, row)

    def face_north(r, here, above):
        j = first_row + r - 2
        keep = jnp.where((j >= 0) & (j < last_face), 0.5, 0.0)
        return (here + above) * keep

    def make_coef(r, carry):
        _, n_low = both(wind[r - 1])
        e_here, n_here = both(wind[r])
        _, n_high = both(wind[r + 1])
        e_face = 0.5 * (e_here + roll(e_here, -1))
        w_face = roll(e_face, 1)
        n_face = face_north(r, n_here, n_high)
        s_face = face_north(r - 1, n_low, n_here)
        coef[0, r] = (
            1.0
            - jnp.maximum(e_face, 0.0)
            + jnp.minimum(w_face, 0.0)
            - jnp.maximum(n_face, 0.0)
            + jnp.minimum(s_face, 0.0)
        )
        coef[1, r] = -jnp.minimum(e_face, 0.0)
        coef[2, r] = jnp.maximum(w_face, 0.0)
        coef[3, r] = -jnp.minimum(n_face, 0.0)
        coef[4, r] = jnp.maximum(s_face, 0.0)
        return carry

    lax.fori_loop(1, EXT_R - 1, make_coef, 0)

    def advected(grid, r, lo, hi):
        w = hi - lo
        lanes = pl.ds(lo, w)
        first_lanes = pl.ds(0, w)
        q = grid[r, :, lanes]
        return (
            coef[0, r, :, first_lanes] * q
            + coef[1, r, :, first_lanes] * roll(q, -1)
            + coef[2, r, :, first_lanes] * roll(q, 1)
            + coef[3, r, :, first_lanes] * grid[r + 1, :, lanes]
            + coef[4, r, :, first_lanes] * grid[r - 1, :, lanes]
        )

    def owner_lanes(blk):
        return jnp.broadcast_to(owner[0, blk].astype(F32), (WIDE, 64)).astype(BF16)

    def exchange(step, phase, send, recv, group_step):
        def one(near_step, carry):
            there = peer(group_step, near_step)

            @pl.when(there != me)
            def _():
                remote(
                    send.at[step, there],
                    recv.at[step, me],
                    ex_send.at[step, phase],
                    ex_recv.at[step, phase, my_group],
                    (me_lat, there),
                ).start()

            @pl.when(there == me)
            def _():
                pltpu.make_async_copy(
                    send.at[step, me], recv.at[step, me], ex_recv.at[step, phase, my_group]
                ).start()

            return carry

        lax.fori_loop(0, near, one, 0)

    def arrived(step, phase, recv, group):
        part = recv.at[step, pl.ds(group * near, near)]
        pltpu.make_async_copy(part, part, ex_recv.at[step, phase, group]).wait()

    def group_at(group_step):
        return lax.rem(my_group + group_step, GROUPS)

    for step in range(STEPS):
        if step:
            stage_halo(step)
            copies = halo_copies(step)
            for copy in copies:
                copy.start()
            for copy in copies:
                copy.wait_recv()
            place_halo(step)

        def sweep_one(r, carry):
            for lo, hi in TILES:
                z[r, :, pl.ds(lo, hi - lo)] = advected(x.at[step], r, lo, hi)
            return carry

        lax.fori_loop(1, EXT_R - 1, sweep_one, 0)

        def sweep_two(r, carry):
            j = r - 2
            slot = (j % 8 // 2) * 8 + (j // 8) * 2 + j % 2
            for lo, hi in TILES:
                new = advected(z, r, lo, hi)[:WIDE]
                if step + 1 < STEPS:
                    x[step + 1, r, pl.ds(0, WIDE), pl.ds(lo, hi - lo)] = new
                else:
                    result[j, :, pl.ds(lo, hi - lo)] = new
                cur_bf[slot, :, pl.ds(lo, hi - lo)] = new.astype(BF16)
            if step == 0:
                cur_bf[slot, :, pl.ds(FEAT, 64)] = owner_lanes(j // 8)
            return carry

        lax.fori_loop(2, ROWS + 2, sweep_two, 0)

        def spread(group_step, carry):
            group = group_at(group_step)
            cells = cur_bf[pl.ds(group * 8, 8)].reshape(GROUP_ROWS, 384)
            moved = jnp.dot(shuffle, cells, preferred_element_type=F32).astype(BF16)
            send_one[step, pl.ds(group * near, near)] = moved.reshape(near, msg, 384)
            exchange(step, 0, send_one, recv_one, group_step)
            return carry

        lax.fori_loop(0, GROUPS, spread, 0)
        for group in range(GROUPS):
            arrived(step, 0, recv_one, group)

        if step == 0:
            lane = lax.broadcasted_iota(jnp.int32, (CELLS, 128), 1)
            tail = recv_one[0, :, :, pl.ds(256, 128)].reshape(CELLS, 128).astype(F32)
            scheme = (lane - 64).astype(F32)
            hit = jnp.where((lane >= 64) & (tail == scheme), 1.0, 0.0)
            q_i = lax.broadcasted_iota(jnp.int32, (CELLS, CELLS), 0)
            p_i = lax.broadcasted_iota(jnp.int32, (CELLS, CELLS), 1)
            before = (p_i // piece < q_i // piece) & (p_i % piece == 0)
            ahead = jnp.dot(
                jnp.where(before, 1.0, 0.0).astype(BF16),
                hit.astype(BF16),
                preferred_element_type=F32,
            )
            place = jnp.sum(hit * (scheme * msg + ahead * piece), axis=1, keepdims=True)
            part = lax.broadcasted_iota(jnp.int32, (CELLS, 1), 0) % piece
            place = place + part.astype(F32)
            picked = jnp.where(p_i.astype(F32) == place, 1.0, 0.0)
            perm_t[...] = picked.astype(BF16)
            perm[...] = picked.T.astype(BF16)

        def deliver(group_step, carry):
            group = group_at(group_step)
            rows = perm[pl.ds(group * GROUP_ROWS, GROUP_ROWS), :]
            held = recv_one[step, :, :, pl.ds(0, FEAT)].reshape(CELLS, FEAT)
            moved = jnp.dot(rows, held, preferred_element_type=F32).astype(BF16)
            send_two[step, pl.ds(group * near, near)] = moved.reshape(near, msg, FEAT)
            exchange(step, 1, send_two, recv_two, group_step)
            return carry

        lax.fori_loop(0, GROUPS, deliver, 0)

        if step == 0:
            for load in loads[3:]:
                load.wait()

        def physics(at, carry):
            group_step = lax.rem(GROUPS - at, GROUPS)
            group = group_at(group_step)
            arrived(step, 1, recv_two, group)
            column = recv_two[step, pl.ds(group * near, near)].reshape(GROUP_ROWS, FEAT)
            hidden = jnp.dot(column, v_in[0], preferred_element_type=F32)
            hidden = silu(hidden).astype(BF16)
            hidden = jnp.dot(hidden, v_two[0], preferred_element_type=F32)
            hidden = silu(hidden).astype(BF16)
            hidden = jnp.dot(hidden, v_three[0], preferred_element_type=F32)
            hidden = silu(hidden).astype(BF16)
            tendency = jnp.dot(hidden, v_out[0], preferred_element_type=F32).astype(BF16)
            send_three[step, pl.ds(group * near, near)] = tendency.reshape(near, msg, FEAT)
            exchange(step, 2, send_three, recv_three, group_step)
            return carry

        lax.fori_loop(0, GROUPS, physics, 0)
        for group in range(GROUPS):
            arrived(step, 2, recv_three, group)

        def homeward(group_step, carry):
            group = group_at(group_step)
            rows = perm_t[pl.ds(group * GROUP_ROWS, GROUP_ROWS), :]
            held = recv_three[step].reshape(CELLS, FEAT)
            moved = jnp.dot(rows, held, preferred_element_type=F32).astype(BF16)
            send_four[step, pl.ds(group * near, near)] = moved.reshape(near, msg, FEAT)
            exchange(step, 3, send_four, recv_four, group_step)
            return carry

        lax.fori_loop(0, GROUPS, homeward, 0)

        def add_home(at, carry):
            group = group_at(lax.rem(GROUPS - at, GROUPS))
            arrived(step, 3, recv_four, group)
            pieces = recv_four[step, pl.ds(group * near, near)].reshape(GROUP_ROWS, FEAT)
            home = jnp.dot(unshuffle, pieces, preferred_element_type=F32)
            for blk in range(BLKS):
                for odd in range(2):
                    j = 8 * blk + 2 * group + odd
                    lo = (2 * blk + odd) * WIDE
                    cell = (2 * group + odd) * WIDE + lax.broadcasted_iota(
                        jnp.int32, (WIDE, FEAT), 0
                    )
                    added = jnp.where(cell < counts[0, blk], home[lo : lo + WIDE], 0.0)
                    if step + 1 < STEPS:
                        x[step + 1, j + 2, pl.ds(0, WIDE), :] += added
                    else:
                        result[j] += added
            return carry

        lax.fori_loop(0, GROUPS, add_home, 0)

    finish = pltpu.make_async_copy(result, out, out_sem.at[0])
    finish.start()
    for copy in winds:
        copy.wait_send()
    for step in range(STEPS):
        for copy in halo_copies(step):
            copy.wait_send()
        for phase, send in enumerate((send_one, send_two, send_three, send_four)):
            sent = send.at[step, pl.ds(0, n_lon - 1)]
            pltpu.make_async_copy(sent, sent, ex_send.at[step, phase]).wait()
    finish.wait()


def solution(mesh):
    n_lat, n_lon = mesh.shape["lat"], mesh.shape["lon"]
    msg = BLKS * COLS // n_lon
    any_spec = pl.BlockSpec(memory_space=pl.ANY)
    smem = pl.BlockSpec(memory_space=pltpu.SMEM)
    dma = pltpu.SemaphoreType.DMA
    vmem = pltpu.VMEM
    scratch = [
        vmem((STEPS, EXT_R, EXT_C, FEAT), F32),
        vmem((EXT_R, EXT_C, FEAT), F32),
        vmem((EXT_R, EXT_C, 2 * LEVELS), F32),
        vmem((ROWS, WIDE, LEVELS), F32),
        vmem((ROWS, WIDE, LEVELS), F32),
        vmem((5, EXT_R, EXT_C, 128), F32),
        vmem((STEPS, 2, 2, ROWS, FEAT), F32),
        vmem((STEPS, 2, 2, ROWS, FEAT), F32),
        vmem((2, 2, ROWS, 128), F32),
        vmem((2, 2, ROWS, 128), F32),
        vmem((STEPS, 4, 8, FEAT), F32),
        vmem((STEPS, 4, 8, FEAT), F32),
        vmem((ROWS, WIDE, 384), BF16),
        vmem((STEPS, n_lon, msg, 384), BF16),
        vmem((STEPS, n_lon, msg, 384), BF16),
    ]
    scratch += [vmem((STEPS, n_lon, msg, FEAT), BF16)] * 6
    scratch += [
        vmem((CELLS, CELLS), BF16),
        vmem((CELLS, CELLS), BF16),
        vmem((ROWS, WIDE, FEAT), F32),
        vmem((1, FEAT, HID), BF16),
        vmem((1, HID, HID), BF16),
        vmem((1, HID, HID), BF16),
        vmem((1, HID, FEAT), BF16),
        dma((7,)),
        dma((STEPS, 8)),
        dma((STEPS, 8)),
        dma((4,)),
        dma((4,)),
        dma((STEPS, 4)),
        dma((STEPS, 4, GROUPS)),
        dma((1,)),
    ]

    call = pl.pallas_call(
        functools.partial(kernel, n_lat, n_lon),
        out_shape=jax.ShapeDtypeStruct((ROWS, WIDE, FEAT), F32),
        in_specs=[any_spec] * 3 + [smem] * 2 + [any_spec] * 4,
        out_specs=any_spec,
        scratch_shapes=scratch,
        compiler_params=pltpu.CompilerParams(
            collective_id=0, has_side_effects=True, vmem_limit_bytes=40 * 1024 * 1024
        ),
        name="coupled_steps",
    )

    return jax.shard_map(
        call,
        mesh=mesh,
        in_specs=(
            P("lat", "lon", None),
            P("lat", "lon", None),
            P("lat", "lon", None),
            P("lat", "lon"),
            P("lat", "lon"),
            P("lon", None, None),
            P("lon", None, None),
            P("lon", None, None),
            P("lon", None, None),
        ),
        out_specs=P("lat", "lon", None),
        check_vma=False,
    )
```

```python
import functools

import jax
import jax.numpy as jnp
from jax import lax
from jax.experimental import pallas as pl
from jax.experimental.pallas import tpu as pltpu
from jax.sharding import PartitionSpec as P

F32 = jnp.float32
BF16 = jnp.bfloat16
MESH = pl.DeviceIdType.MESH

STEPS = 2
COLS = 128
ROWS = 32
WIDE = 16
FEAT = 320
LEVELS = 64
HID = 512
BLKS = 4
GROUPS = 4
EXT_R = ROWS + 4
EXT_C = 24
CELLS = ROWS * WIDE
GROUP_ROWS = CELLS // GROUPS
TILES = ((0, 128), (128, 256), (256, 320))


def silu(x):
    half = 0.5 * x
    return half + half * jnp.tanh(half)


def roll(x, shift):
    return pltpu.roll(x, shift % x.shape[0], axis=0)


def kernel(
    n_lat,
    n_lon,
    fields,
    wind_east,
    wind_north,
    owner,
    counts,
    w_in,
    w_two,
    w_three,
    w_out,
    out,
    x,
    z,
    wind,
    raw_east,
    raw_north,
    coef,
    side_out,
    side_in,
    wside_out,
    wside_in,
    corner_out,
    corner_in,
    cur_bf,
    send_one,
    recv_one,
    send_two,
    recv_two,
    send_three,
    recv_three,
    send_four,
    recv_four,
    perm,
    perm_t,
    result,
    v_in,
    v_two,
    v_three,
    v_out,
    load_sem,
    halo_send,
    halo_recv,
    wind_send,
    wind_recv,
    ex_send,
    ex_recv,
    out_sem,
):
    near = n_lon // GROUPS
    piece = COLS // n_lon
    msg = BLKS * piece
    me_lat = lax.axis_index("lat")
    me = lax.axis_index("lon")
    my_group = me // near
    my_near = me % near
    north = lax.rem(me_lat + 1, n_lat)
    south = lax.rem(me_lat + n_lat - 1, n_lat)
    east = lax.rem(me + 1, n_lon)
    west = lax.rem(me + n_lon - 1, n_lon)
    corners = ((south, west), (south, east), (north, west), (north, east))

    def far_first(turn, count):
        return lax.rem(count // 2 + (1 - 2 * (turn % 2)) * ((turn + 1) // 2) + count, count)

    def peer(group_step, near_step):
        group = lax.rem(my_group + group_step, GROUPS)
        return group * near + lax.rem(my_near + near_step, near)

    loads = [
        pltpu.make_async_copy(wind_east, raw_east, load_sem.at[0]),
        pltpu.make_async_copy(wind_north, raw_north, load_sem.at[1]),
        pltpu.make_async_copy(
            fields, x.at[0, pl.ds(2, ROWS), pl.ds(0, WIDE), :], load_sem.at[2]
        ),
        pltpu.make_async_copy(w_in, v_in, load_sem.at[3]),
        pltpu.make_async_copy(w_two, v_two, load_sem.at[4]),
        pltpu.make_async_copy(w_three, v_three, load_sem.at[5]),
        pltpu.make_async_copy(w_out, v_out, load_sem.at[6]),
    ]
    for load in loads:
        load.start()

    barrier = pltpu.get_barrier_semaphore()

    def greet(step, carry):
        pl.semaphore_signal(
            barrier,
            inc=1,
            device_id=(me_lat, lax.rem(me + step, n_lon)),
            device_id_type=MESH,
        )
        return carry

    lax.fori_loop(1, n_lon, greet, 0)
    for there in ((south, me), (north, me)) + corners:
        pl.semaphore_signal(barrier, inc=1, device_id=there, device_id_type=MESH)

    def clear(r, carry):
        x[0, r, pl.ds(WIDE, 8), :] = jnp.zeros((8, FEAT), F32)
        x[1, r, pl.ds(WIDE, 8), :] = jnp.zeros((8, FEAT), F32)
        wind[r, pl.ds(WIDE, 8), :] = jnp.zeros((8, 2 * LEVELS), F32)
        return carry

    lax.fori_loop(0, EXT_R, clear, 0)

    loads[0].wait()
    loads[1].wait()

    def join(r, carry):
        wind[r + 2, pl.ds(0, WIDE), :] = jnp.concatenate([raw_east[r], raw_north[r]], axis=-1)
        return carry

    lax.fori_loop(0, ROWS, join, 0)
    loads[2].wait()

    def remote(src, dst, send, recv, where):
        return pltpu.make_async_remote_copy(
            src_ref=src,
            dst_ref=dst,
            send_sem=send,
            recv_sem=recv,
            device_id=where,
            device_id_type=MESH,
        )

    def halo_copies(step):
        grid = x.at[step]
        inner = pl.ds(0, WIDE)
        copies = [
            remote(
                grid.at[pl.ds(2, 2), inner, :],
                grid.at[pl.ds(ROWS + 2, 2), inner, :],
                halo_send.at[step, 0],
                halo_recv.at[step, 0],
                (south, me),
            ),
            remote(
                grid.at[pl.ds(ROWS, 2), inner, :],
                grid.at[pl.ds(0, 2), inner, :],
                halo_send.at[step, 1],
                halo_recv.at[step, 1],
                (north, me),
            ),
        ]
        for side, there in enumerate((west, east)):
            copies.append(
                remote(
                    side_out.at[step, side],
                    side_in.at[step, side],
                    halo_send.at[step, 2 + side],
                    halo_recv.at[step, 2 + side],
                    (me_lat, there),
                )
            )
        for at, there in enumerate(corners):
            copies.append(
                remote(
                    corner_out.at[step, at],
                    corner_in.at[step, at],
                    halo_send.at[step, 4 + at],
                    halo_recv.at[step, 4 + at],
                    there,
                )
            )
        return copies

    def wind_copies():
        inner = pl.ds(0, WIDE)
        copies = [
            remote(
                wind.at[pl.ds(2, 2), inner, :],
                wind.at[pl.ds(ROWS + 2, 2), inner, :],
                wind_send.at[0],
                wind_recv.at[0],
                (south, me),
            ),
            remote(
                wind.at[pl.ds(ROWS, 2), inner, :],
                wind.at[pl.ds(0, 2), inner, :],
                wind_send.at[1],
                wind_recv.at[1],
                (north, me),
            ),
        ]
        for side, there in enumerate((west, east)):
            copies.append(
                remote(
                    wside_out.at[side],
                    wside_in.at[side],
                    wind_send.at[2 + side],
                    wind_recv.at[2 + side],
                    (me_lat, there),
                )
            )
        return copies

    corner_cells = ((2, 0), (2, WIDE - 1), (ROWS + 1, 0), (ROWS + 1, WIDE - 1))
    corner_slots = ((ROWS + 2, 16), (ROWS + 2, 23), (1, 16), (1, 23))
    side_cells = ((0, 1), (WIDE - 2, WIDE - 1))
    side_slots = ((16, 17), (22, 23))

    def stage_halo(step):
        for side in range(2):
            for at in range(2):
                side_out[step, side, at] = x[step, pl.ds(2, ROWS), side_cells[side][at], :]
        for at, (r, c) in enumerate(corner_cells):
            corner_out[step, at, pl.ds(0, 1), :] = x[step, r, pl.ds(c, 1), :]

    def place_halo(step):
        for side in range(2):
            for at in range(2):
                x[step, pl.ds(2, ROWS), side_slots[side][at], :] = side_in[step, side, at]
        for at, (r, c) in enumerate(corner_slots):
            x[step, r, pl.ds(c, 1), :] = corner_in[step, at, pl.ds(0, 1), :]

    corner_out[...] = jnp.zeros_like(corner_out)
    stage_halo(0)
    for side in range(2):
        for at in range(2):
            wside_out[side, at] = wind[pl.ds(2, ROWS), side_cells[side][at], :]
    for at, (r, c) in enumerate(corner_cells):
        corner_out[0, at, pl.ds(1, 1), pl.ds(0, 128)] = wind[r, pl.ds(c, 1), :]

    pl.semaphore_wait(barrier, n_lon - 1 + 6)

    winds = wind_copies()
    first = halo_copies(0)
    for copy in winds + first:
        copy.start()

    row_i = lax.broadcasted_iota(jnp.int32, (GROUP_ROWS, GROUP_ROWS), 0)
    col_i = lax.broadcasted_iota(jnp.int32, (GROUP_ROWS, GROUP_ROWS), 1)

    def slot_of(cell):
        blk = cell // (2 * WIDE)
        at = cell % (2 * WIDE)
        return (at // piece) * msg + blk * piece + at % piece

    shuffle = jnp.where(row_i == slot_of(col_i), 1.0, 0.0).astype(BF16)
    unshuffle = jnp.where(slot_of(row_i) == col_i, 1.0, 0.0).astype(BF16)

    for copy in winds + first:
        copy.wait_recv()
    for side in range(2):
        for at in range(2):
            wind[pl.ds(2, ROWS), side_slots[side][at], :] = wside_in[side, at]
    for at, (r, c) in enumerate(corner_slots):
        wind[r, pl.ds(c, 1), :] = corner_in[0, at, pl.ds(1, 1), pl.ds(0, 128)]
    place_halo(0)

    first_row = me_lat * ROWS
    last_face = n_lat * ROWS - 1
    low_half = lax.broadcasted_iota(jnp.int32, (EXT_C, 128), 1) < LEVELS

    def both(row):
        turned = pltpu.roll(row, LEVELS, axis=1)
        return jnp.where(low_half, row, turned), jnp.where(low_half, turned, row)

    def face_north(r, here, above):
        j = first_row + r - 2
        keep = jnp.where((j >= 0) & (j < last_face), 0.5, 0.0)
        return (here + above) * keep

    def make_coef(r, carry):
        _, n_low = both(wind[r - 1])
        e_here, n_here = both(wind[r])
        _, n_high = both(wind[r + 1])
        e_face = 0.5 * (e_here + roll(e_here, -1))
        w_face = roll(e_face, 1)
        n_face = face_north(r, n_here, n_high)
        s_face = face_north(r - 1, n_low, n_here)
        coef[0, r] = (
            1.0
            - jnp.maximum(e_face, 0.0)
            + jnp.minimum(w_face, 0.0)
            - jnp.maximum(n_face, 0.0)
            + jnp.minimum(s_face, 0.0)
        )
        coef[1, r] = -jnp.minimum(e_face, 0.0)
        coef[2, r] = jnp.maximum(w_face, 0.0)
        coef[3, r] = -jnp.minimum(n_face, 0.0)
        coef[4, r] = jnp.maximum(s_face, 0.0)
        return carry

    lax.fori_loop(1, EXT_R - 1, make_coef, 0)

    def advected(grid, r, lo, hi):
        w = hi - lo
        lanes = pl.ds(lo, w)
        first_lanes = pl.ds(0, w)
        q = grid[r, :, lanes]
        return (
            coef[0, r, :, first_lanes] * q
            + coef[1, r, :, first_lanes] * roll(q, -1)
            + coef[2, r, :, first_lanes] * roll(q, 1)
            + coef[3, r, :, first_lanes] * grid[r + 1, :, lanes]
            + coef[4, r, :, first_lanes] * grid[r - 1, :, lanes]
        )

    def owner_lanes(blk):
        return jnp.broadcast_to(owner[0, blk].astype(F32), (WIDE, 64)).astype(BF16)

    def exchange(step, phase, send, recv, group_step):
        def one(turn, carry):
            there = peer(group_step, far_first(turn, near))

            @pl.when(there != me)
            def _():
                remote(
                    send.at[step, there],
                    recv.at[step, me],
                    ex_send.at[step, phase],
                    ex_recv.at[step, phase, my_group],
                    (me_lat, there),
                ).start()

            @pl.when(there == me)
            def _():
                pltpu.make_async_copy(
                    send.at[step, me], recv.at[step, me], ex_recv.at[step, phase, my_group]
                ).start()

            return carry

        lax.fori_loop(0, near, one, 0)

    def arrived(step, phase, recv, group):
        part = recv.at[step, pl.ds(group * near, near)]
        pltpu.make_async_copy(part, part, ex_recv.at[step, phase, group]).wait()

    def group_at(group_step):
        return lax.rem(my_group + group_step, GROUPS)

    for step in range(STEPS):
        if step:
            stage_halo(step)
            copies = halo_copies(step)
            for copy in copies:
                copy.start()
            for copy in copies:
                copy.wait_recv()
            place_halo(step)

        def sweep_one(r, carry):
            for lo, hi in TILES:
                z[r, :, pl.ds(lo, hi - lo)] = advected(x.at[step], r, lo, hi)
            return carry

        lax.fori_loop(1, EXT_R - 1, sweep_one, 0)

        def sweep_two(r, carry):
            j = r - 2
            slot = (j % 8 // 2) * 8 + (j // 8) * 2 + j % 2
            for lo, hi in TILES:
                new = advected(z, r, lo, hi)[:WIDE]
                if step + 1 < STEPS:
                    x[step + 1, r, pl.ds(0, WIDE), pl.ds(lo, hi - lo)] = new
                else:
                    result[j, :, pl.ds(lo, hi - lo)] = new
                cur_bf[slot, :, pl.ds(lo, hi - lo)] = new.astype(BF16)
            if step == 0:
                cur_bf[slot, :, pl.ds(FEAT, 64)] = owner_lanes(j // 8)
            return carry

        lax.fori_loop(2, ROWS + 2, sweep_two, 0)

        def spread(turn, carry):
            group_step = far_first(turn, GROUPS)
            group = group_at(group_step)
            cells = cur_bf[pl.ds(group * 8, 8)].reshape(GROUP_ROWS, 384)
            moved = jnp.dot(shuffle, cells, preferred_element_type=F32).astype(BF16)
            send_one[step, pl.ds(group * near, near)] = moved.reshape(near, msg, 384)
            exchange(step, 0, send_one, recv_one, group_step)
            return carry

        lax.fori_loop(0, GROUPS, spread, 0)
        for group in range(GROUPS):
            arrived(step, 0, recv_one, group)

        if step == 0:
            lane = lax.broadcasted_iota(jnp.int32, (CELLS, 128), 1)
            tail = recv_one[0, :, :, pl.ds(256, 128)].reshape(CELLS, 128).astype(F32)
            scheme = (lane - 64).astype(F32)
            hit = jnp.where((lane >= 64) & (tail == scheme), 1.0, 0.0)
            q_i = lax.broadcasted_iota(jnp.int32, (CELLS, CELLS), 0)
            p_i = lax.broadcasted_iota(jnp.int32, (CELLS, CELLS), 1)
            before = (p_i // piece < q_i // piece) & (p_i % piece == 0)
            ahead = jnp.dot(
                jnp.where(before, 1.0, 0.0).astype(BF16),
                hit.astype(BF16),
                preferred_element_type=F32,
            )
            place = jnp.sum(hit * (scheme * msg + ahead * piece), axis=1, keepdims=True)
            part = lax.broadcasted_iota(jnp.int32, (CELLS, 1), 0) % piece
            place = place + part.astype(F32)
            picked = jnp.where(p_i.astype(F32) == place, 1.0, 0.0)
            perm_t[...] = picked.astype(BF16)
            perm[...] = picked.T.astype(BF16)

        def deliver(turn, carry):
            group_step = far_first(turn, GROUPS)
            group = group_at(group_step)
            rows = perm[pl.ds(group * GROUP_ROWS, GROUP_ROWS), :]
            held = recv_one[step, :, :, pl.ds(0, FEAT)].reshape(CELLS, FEAT)
            moved = jnp.dot(rows, held, preferred_element_type=F32).astype(BF16)
            send_two[step, pl.ds(group * near, near)] = moved.reshape(near, msg, FEAT)
            exchange(step, 1, send_two, recv_two, group_step)
            return carry

        lax.fori_loop(0, GROUPS, deliver, 0)

        if step == 0:
            for load in loads[3:]:
                load.wait()

        def physics(at, carry):
            group_step = far_first(at, GROUPS)
            group = group_at(group_step)
            arrived(step, 1, recv_two, group)
            column = recv_two[step, pl.ds(group * near, near)].reshape(GROUP_ROWS, FEAT)
            hidden = jnp.dot(column, v_in[0], preferred_element_type=F32)
            hidden = silu(hidden).astype(BF16)
            hidden = jnp.dot(hidden, v_two[0], preferred_element_type=F32)
            hidden = silu(hidden).astype(BF16)
            hidden = jnp.dot(hidden, v_three[0], preferred_element_type=F32)
            hidden = silu(hidden).astype(BF16)
            tendency = lax.dot_general(
                hidden, v_out[0], (((1,), (1,)), ((), ())), preferred_element_type=F32
            ).astype(BF16)
            send_three[step, pl.ds(group * near, near)] = tendency.reshape(near, msg, FEAT)
            exchange(step, 2, send_three, recv_three, group_step)
            return carry

        lax.fori_loop(0, GROUPS, physics, 0)
        for group in range(GROUPS):
            arrived(step, 2, recv_three, group)

        def homeward(turn, carry):
            group_step = far_first(turn, GROUPS)
            group = group_at(group_step)
            rows = perm_t[pl.ds(group * GROUP_ROWS, GROUP_ROWS), :]
            held = recv_three[step].reshape(CELLS, FEAT)
            moved = jnp.dot(rows, held, preferred_element_type=F32).astype(BF16)
            send_four[step, pl.ds(group * near, near)] = moved.reshape(near, msg, FEAT)
            exchange(step, 3, send_four, recv_four, group_step)
            return carry

        lax.fori_loop(0, GROUPS, homeward, 0)

        def add_home(at, carry):
            group = group_at(far_first(at, GROUPS))
            arrived(step, 3, recv_four, group)
            pieces = recv_four[step, pl.ds(group * near, near)].reshape(GROUP_ROWS, FEAT)
            home = jnp.dot(unshuffle, pieces, preferred_element_type=F32)
            for blk in range(BLKS):
                for odd in range(2):
                    j = 8 * blk + 2 * group + odd
                    lo = (2 * blk + odd) * WIDE
                    cell = (2 * group + odd) * WIDE + lax.broadcasted_iota(
                        jnp.int32, (WIDE, FEAT), 0
                    )
                    added = jnp.where(cell < counts[0, blk], home[lo : lo + WIDE], 0.0)
                    if step + 1 < STEPS:
                        x[step + 1, j + 2, pl.ds(0, WIDE), :] += added
                    else:
                        result[j] += added
            return carry

        lax.fori_loop(0, GROUPS, add_home, 0)

    finish = pltpu.make_async_copy(result, out, out_sem.at[0])
    finish.start()
    for copy in winds:
        copy.wait_send()
    for step in range(STEPS):
        for copy in halo_copies(step):
            copy.wait_send()
        for phase, send in enumerate((send_one, send_two, send_three, send_four)):
            sent = send.at[step, pl.ds(0, n_lon - 1)]
            pltpu.make_async_copy(sent, sent, ex_send.at[step, phase]).wait()
    finish.wait()


def solution(mesh):
    n_lat, n_lon = mesh.shape["lat"], mesh.shape["lon"]
    msg = BLKS * COLS // n_lon
    any_spec = pl.BlockSpec(memory_space=pl.ANY)
    smem = pl.BlockSpec(memory_space=pltpu.SMEM)
    dma = pltpu.SemaphoreType.DMA
    vmem = pltpu.VMEM
    scratch = [
        vmem((STEPS, EXT_R, EXT_C, FEAT), F32),
        vmem((EXT_R, EXT_C, FEAT), F32),
        vmem((EXT_R, EXT_C, 2 * LEVELS), F32),
        vmem((ROWS, WIDE, LEVELS), F32),
        vmem((ROWS, WIDE, LEVELS), F32),
        vmem((5, EXT_R, EXT_C, 128), F32),
        vmem((STEPS, 2, 2, ROWS, FEAT), F32),
        vmem((STEPS, 2, 2, ROWS, FEAT), F32),
        vmem((2, 2, ROWS, 128), F32),
        vmem((2, 2, ROWS, 128), F32),
        vmem((STEPS, 4, 8, FEAT), F32),
        vmem((STEPS, 4, 8, FEAT), F32),
        vmem((ROWS, WIDE, 384), BF16),
        vmem((STEPS, n_lon, msg, 384), BF16),
        vmem((STEPS, n_lon, msg, 384), BF16),
    ]
    scratch += [vmem((STEPS, n_lon, msg, FEAT), BF16)] * 6
    scratch += [
        vmem((CELLS, CELLS), BF16),
        vmem((CELLS, CELLS), BF16),
        vmem((ROWS, WIDE, FEAT), F32),
        vmem((1, FEAT, HID), BF16),
        vmem((1, HID, HID), BF16),
        vmem((1, HID, HID), BF16),
        vmem((1, FEAT, HID), BF16),
        dma((7,)),
        dma((STEPS, 8)),
        dma((STEPS, 8)),
        dma((4,)),
        dma((4,)),
        dma((STEPS, 4)),
        dma((STEPS, 4, GROUPS)),
        dma((1,)),
    ]

    call = pl.pallas_call(
        functools.partial(kernel, n_lat, n_lon),
        out_shape=jax.ShapeDtypeStruct((ROWS, WIDE, FEAT), F32),
        in_specs=[any_spec] * 3 + [smem] * 2 + [any_spec] * 4,
        out_specs=any_spec,
        scratch_shapes=scratch,
        compiler_params=pltpu.CompilerParams(
            collective_id=0, has_side_effects=True, vmem_limit_bytes=60 * 1024 * 1024
        ),
        name="coupled_steps",
    )

    def local(fields, wind_east, wind_north, owner, counts, w_in, w_two, w_three, w_out):
        w_out = jnp.swapaxes(w_out, 1, 2)
        return call(fields, wind_east, wind_north, owner, counts, w_in, w_two, w_three, w_out)

    return jax.shard_map(
        local,
        mesh=mesh,
        in_specs=(
            P("lat", "lon", None),
            P("lat", "lon", None),
            P("lat", "lon", None),
            P("lat", "lon"),
            P("lat", "lon"),
            P("lon", None, None),
            P("lon", None, None),
            P("lon", None, None),
            P("lon", None, None),
        ),
        out_specs=P("lat", "lon", None),
        check_vma=False,
    )
```

```python
import functools

import jax
import jax.numpy as jnp
from jax import lax
from jax.experimental import pallas as pl
from jax.experimental.pallas import tpu as pltpu
from jax.sharding import PartitionSpec as P

F32 = jnp.float32
BF16 = jnp.bfloat16
MESH = pl.DeviceIdType.MESH

STEPS = 2
COLS = 128
ROWS = 32
WIDE = 16
FEAT = 320
LEVELS = 64
HID = 512
BLKS = 4
GROUPS = 4
EXT_R = ROWS + 4
EXT_C = 24
CELLS = ROWS * WIDE
HALF = CELLS // 2
MAIN = 256
TILES = ((0, 128), (128, 256), (256, 320))
TAIL = FEAT - MAIN


def silu(x):
    half = 0.5 * x
    return half + half * jnp.tanh(half)


def roll(x, shift):
    return pltpu.roll(x, shift % x.shape[0], axis=0)


def kernel(
    n_lat,
    n_lon,
    fields,
    wind_east,
    wind_north,
    owner,
    counts,
    w_in,
    w_two,
    w_three,
    w_out,
    out,
    x,
    z,
    wind,
    raw_east,
    raw_north,
    coef,
    side_out,
    side_in,
    wside_out,
    wside_in,
    corner_out,
    corner_in,
    cur_bf,
    send_one,
    recv_one,
    send_two,
    recv_two,
    send_three,
    recv_three,
    send_four,
    recv_four,
    owner_out,
    owner_in,
    perm,
    perm_t,
    tail_perm,
    tail_perm_t,
    result,
    v_in,
    v_two,
    v_three,
    v_out,
    tail_first,
    tail_last,
    load_sem,
    halo_send,
    halo_recv,
    wind_send,
    wind_recv,
    own_send,
    own_recv,
    ex_send,
    ex_recv,
    out_sem,
):
    near = n_lon // GROUPS
    half = near // 2
    piece = COLS // n_lon
    msg = BLKS * piece
    pairs = msg // 2
    me_lat = lax.axis_index("lat")
    me = lax.axis_index("lon")
    my_y = me // near
    my_z = me % near
    north = lax.rem(me_lat + 1, n_lat)
    south = lax.rem(me_lat + n_lat - 1, n_lat)
    east = lax.rem(me + 1, n_lon)
    west = lax.rem(me + n_lon - 1, n_lon)
    corners = ((south, west), (south, east), (north, west), (north, east))

    def class_of(y, z):
        return (y + z + me_lat) % 2

    def slot_of(y, z):
        return y * near + class_of(y, z) * half + z // 2

    my_class = class_of(my_y, my_z)
    my_slot = slot_of(my_y, my_z)

    def hops(step, count):
        return min(step, count - step)

    row_order = sorted(range(GROUPS), key=lambda step: -hops(step, GROUPS))
    all_steps = sorted(range(near), key=lambda step: -hops(step, near))
    even_steps = [step for step in all_steps if step % 2 == 0]
    odd_steps = [step for step in all_steps if step % 2]

    loads = [
        pltpu.make_async_copy(wind_east, raw_east, load_sem.at[0]),
        pltpu.make_async_copy(wind_north, raw_north, load_sem.at[1]),
        pltpu.make_async_copy(
            fields, x.at[0, pl.ds(2, ROWS), pl.ds(0, WIDE), :], load_sem.at[2]
        ),
        pltpu.make_async_copy(w_in, v_in, load_sem.at[3]),
        pltpu.make_async_copy(w_two, v_two, load_sem.at[4]),
        pltpu.make_async_copy(w_three, v_three, load_sem.at[5]),
        pltpu.make_async_copy(w_out, v_out, load_sem.at[6]),
    ]
    for load in loads:
        load.start()

    barrier = pltpu.get_barrier_semaphore()

    def greet(step, carry):
        pl.semaphore_signal(
            barrier,
            inc=1,
            device_id=(me_lat, lax.rem(me + step, n_lon)),
            device_id_type=MESH,
        )
        return carry

    lax.fori_loop(1, n_lon, greet, 0)
    for there in ((south, me), (north, me)) + corners:
        pl.semaphore_signal(barrier, inc=1, device_id=there, device_id_type=MESH)

    def clear(r, carry):
        x[0, r, pl.ds(WIDE, 8), :] = jnp.zeros((8, FEAT), F32)
        x[1, r, pl.ds(WIDE, 8), :] = jnp.zeros((8, FEAT), F32)
        wind[r, pl.ds(WIDE, 8), :] = jnp.zeros((8, 2 * LEVELS), F32)
        return carry

    lax.fori_loop(0, EXT_R, clear, 0)

    loads[0].wait()
    loads[1].wait()

    def join(r, carry):
        wind[r + 2, pl.ds(0, WIDE), :] = jnp.concatenate([raw_east[r], raw_north[r]], axis=-1)
        return carry

    lax.fori_loop(0, ROWS, join, 0)
    loads[2].wait()

    def remote(src, dst, send, recv, where):
        return pltpu.make_async_remote_copy(
            src_ref=src,
            dst_ref=dst,
            send_sem=send,
            recv_sem=recv,
            device_id=where,
            device_id_type=MESH,
        )

    def halo_copies(step):
        grid = x.at[step]
        inner = pl.ds(0, WIDE)
        copies = [
            remote(
                grid.at[pl.ds(2, 2), inner, :],
                grid.at[pl.ds(ROWS + 2, 2), inner, :],
                halo_send.at[step, 0],
                halo_recv.at[step, 0],
                (south, me),
            ),
            remote(
                grid.at[pl.ds(ROWS, 2), inner, :],
                grid.at[pl.ds(0, 2), inner, :],
                halo_send.at[step, 1],
                halo_recv.at[step, 1],
                (north, me),
            ),
        ]
        for side, there in enumerate((west, east)):
            copies.append(
                remote(
                    side_out.at[step, side],
                    side_in.at[step, side],
                    halo_send.at[step, 2 + side],
                    halo_recv.at[step, 2 + side],
                    (me_lat, there),
                )
            )
        for at, there in enumerate(corners):
            copies.append(
                remote(
                    corner_out.at[step, at],
                    corner_in.at[step, at],
                    halo_send.at[step, 4 + at],
                    halo_recv.at[step, 4 + at],
                    there,
                )
            )
        return copies

    def wind_copies():
        inner = pl.ds(0, WIDE)
        copies = [
            remote(
                wind.at[pl.ds(2, 2), inner, :],
                wind.at[pl.ds(ROWS + 2, 2), inner, :],
                wind_send.at[0],
                wind_recv.at[0],
                (south, me),
            ),
            remote(
                wind.at[pl.ds(ROWS, 2), inner, :],
                wind.at[pl.ds(0, 2), inner, :],
                wind_send.at[1],
                wind_recv.at[1],
                (north, me),
            ),
        ]
        for side, there in enumerate((west, east)):
            copies.append(
                remote(
                    wside_out.at[side],
                    wside_in.at[side],
                    wind_send.at[2 + side],
                    wind_recv.at[2 + side],
                    (me_lat, there),
                )
            )
        return copies

    corner_cells = ((2, 0), (2, WIDE - 1), (ROWS + 1, 0), (ROWS + 1, WIDE - 1))
    corner_slots = ((ROWS + 2, 16), (ROWS + 2, 23), (1, 16), (1, 23))
    side_cells = ((0, 1), (WIDE - 2, WIDE - 1))
    side_slots = ((16, 17), (22, 23))

    def stage_halo(step):
        for side in range(2):
            for at in range(2):
                side_out[step, side, at] = x[step, pl.ds(2, ROWS), side_cells[side][at], :]
        for at, (r, c) in enumerate(corner_cells):
            corner_out[step, at, pl.ds(0, 1), :] = x[step, r, pl.ds(c, 1), :]

    def place_halo(step):
        for side in range(2):
            for at in range(2):
                x[step, pl.ds(2, ROWS), side_slots[side][at], :] = side_in[step, side, at]
        for at, (r, c) in enumerate(corner_slots):
            x[step, r, pl.ds(c, 1), :] = corner_in[step, at, pl.ds(0, 1), :]

    corner_out[...] = jnp.zeros_like(corner_out)
    stage_halo(0)
    for side in range(2):
        for at in range(2):
            wside_out[side, at] = wind[pl.ds(2, ROWS), side_cells[side][at], :]
    for at, (r, c) in enumerate(corner_cells):
        corner_out[0, at, pl.ds(1, 1), pl.ds(0, 128)] = wind[r, pl.ds(c, 1), :]

    owner_row = lax.broadcasted_iota(jnp.int32, (pairs, 128), 0) % BLKS
    owner_tile = jnp.zeros((pairs, 128), F32)
    for blk in range(BLKS):
        place = slot_of(owner[0, blk] // near, owner[0, blk] % near)
        owner_tile = jnp.where(owner_row == blk, place.astype(F32), owner_tile)
    owner_out[...] = owner_tile

    pl.semaphore_wait(barrier, n_lon - 1 + 6)

    winds = wind_copies()
    first = halo_copies(0)
    for copy in winds + first:
        copy.start()

    def tell_owner(step, carry):
        there = lax.rem(me + step, n_lon)
        remote(owner_out, owner_in.at[my_slot], own_send.at[0], own_recv.at[0], (me_lat, there)).start()
        return carry

    lax.fori_loop(1, n_lon, tell_owner, 0)
    pltpu.make_async_copy(owner_out, owner_in.at[my_slot], own_recv.at[0]).start()

    def iota(rows, cols):
        return (
            lax.broadcasted_iota(jnp.int32, (rows, cols), 0),
            lax.broadcasted_iota(jnp.int32, (rows, cols), 1),
        )

    def one_hot(where):
        return jnp.where(where, 1.0, 0.0).astype(BF16)

    def main_row(cell):
        blk, at = cell // (HALF // BLKS), cell % (HALF // BLKS)
        return at // piece * msg + at % piece * BLKS + blk

    def pair_row(cell):
        blk, at = cell // (HALF // BLKS), cell % (HALF // BLKS)
        return at // piece * pairs + at % (piece // 2) * BLKS + blk

    def upper(cell):
        return cell % piece >= piece // 2

    to_i, from_i = iota(HALF, HALF)
    shuffle = one_hot(to_i == main_row(from_i))
    unshuffle = one_hot(main_row(to_i) == from_i)
    to_i, from_i = iota(HALF // 2, HALF)
    pair_low = one_hot((to_i == pair_row(from_i)) & ~upper(from_i))
    pair_high = one_hot((to_i == pair_row(from_i)) & upper(from_i))
    to_i, from_i = iota(HALF, HALF // 2)
    unpair = one_hot(pair_row(to_i) == from_i)
    is_upper = upper(to_i)
    in_low = from_i < TAIL

    for copy in winds + first:
        copy.wait_recv()
    for side in range(2):
        for at in range(2):
            wind[pl.ds(2, ROWS), side_slots[side][at], :] = wside_in[side, at]
    for at, (r, c) in enumerate(corner_slots):
        wind[r, pl.ds(c, 1), :] = corner_in[0, at, pl.ds(1, 1), pl.ds(0, 128)]
    place_halo(0)

    first_row = me_lat * ROWS
    last_face = n_lat * ROWS - 1
    low_half = lax.broadcasted_iota(jnp.int32, (EXT_C, 128), 1) < LEVELS

    def both(row):
        turned = pltpu.roll(row, LEVELS, axis=1)
        return jnp.where(low_half, row, turned), jnp.where(low_half, turned, row)

    def face_north(r, here, above):
        j = first_row + r - 2
        keep = jnp.where((j >= 0) & (j < last_face), 0.5, 0.0)
        return (here + above) * keep

    def make_coef(r, carry):
        _, n_low = both(wind[r - 1])
        e_here, n_here = both(wind[r])
        _, n_high = both(wind[r + 1])
        e_face = 0.5 * (e_here + roll(e_here, -1))
        w_face = roll(e_face, 1)
        n_face = face_north(r, n_here, n_high)
        s_face = face_north(r - 1, n_low, n_here)
        coef[0, r] = (
            1.0
            - jnp.maximum(e_face, 0.0)
            + jnp.minimum(w_face, 0.0)
            - jnp.maximum(n_face, 0.0)
            + jnp.minimum(s_face, 0.0)
        )
        coef[1, r] = -jnp.minimum(e_face, 0.0)
        coef[2, r] = jnp.maximum(w_face, 0.0)
        coef[3, r] = -jnp.minimum(n_face, 0.0)
        coef[4, r] = jnp.maximum(s_face, 0.0)
        return carry

    lax.fori_loop(1, EXT_R - 1, make_coef, 0)

    def advected(grid, r, lo, hi):
        w = hi - lo
        lanes = pl.ds(lo, w)
        first_lanes = pl.ds(0, w)
        q = grid[r, :, lanes]
        return (
            coef[0, r, :, first_lanes] * q
            + coef[1, r, :, first_lanes] * roll(q, -1)
            + coef[2, r, :, first_lanes] * roll(q, 1)
            + coef[3, r, :, first_lanes] * grid[r + 1, :, lanes]
            + coef[4, r, :, first_lanes] * grid[r - 1, :, lanes]
        )

    def send_to(step, phase, send, recv, key, y, z, may_be_me):
        there = slot_of(y, z)
        arrive = ex_recv.at[step, phase, key]

        def start():
            remote(
                send.at[step, there],
                recv.at[step, my_slot],
                ex_send.at[step, phase],
                arrive,
                (me_lat, y * near + z),
            ).start()

        if not may_be_me:
            start()
            return
        pl.when(there != my_slot)(start)

        @pl.when(there == my_slot)
        def _():
            pltpu.make_async_copy(send.at[step, there], recv.at[step, my_slot], arrive).start()

    def row_at(turn):
        step = row_order[-1]
        for at, value in enumerate(row_order[:-1]):
            step = jnp.where(turn == at, value, step)
        return lax.rem(my_y + step, GROUPS)

    def send_class(step, phase, send, recv, cls):
        def one_row(turn, carry):
            y = row_at(turn)
            odd = (y + my_y + cls + my_class) % 2
            for even_step, odd_step in zip(even_steps, odd_steps):
                z = lax.rem(my_z + jnp.where(odd == 1, odd_step, even_step), near)
                send_to(step, phase, send, recv, 0, y, z, even_step == 0)
            return carry

        lax.fori_loop(0, GROUPS, one_row, 0)

    def send_row(step, phase, send, recv, y):
        for near_step in all_steps:
            z = lax.rem(my_z + near_step, near)
            send_to(step, phase, send, recv, my_class, y, z, near_step == 0)

    def arrived(step, phase, recv, count, key):
        part = recv.at[step, pl.ds(0, count)]
        pltpu.make_async_copy(part, part, ex_recv.at[step, phase, key]).wait()

    def main_of(buf, step, first, count):
        part = buf[step, pl.ds(first, count)]
        low = part[:, :msg].reshape(count * msg, 128)
        high = part[:, msg : 2 * msg].reshape(count * msg, 128)
        pair = part[:, 2 * msg :].reshape(count * pairs, 128)
        return low, high, pair

    def class_of_buf(buf, step, cls):
        parts = [main_of(buf, step, y * near + cls * half, half) for y in range(GROUPS)]
        low, high, pair = (jnp.concatenate(some, axis=0) for some in zip(*parts))
        return jnp.concatenate([low, high], axis=1), pair

    def put(buf, step, first, count, main, pair):
        main, pair = main.astype(BF16), pair.astype(BF16)
        where = pl.ds(first, count)
        buf[step, where, pl.ds(0, msg), :] = main[:, :128].reshape(count, msg, 128)
        buf[step, where, pl.ds(msg, msg), :] = main[:, 128:].reshape(count, msg, 128)
        buf[step, where, pl.ds(2 * msg, pairs), :] = pair.reshape(count, pairs, 128)

    def put_class(buf, step, cls, main, pair):
        for y in range(GROUPS):
            rows = slice(y * half * msg, (y + 1) * half * msg)
            pair_rows = slice(y * half * pairs, (y + 1) * half * pairs)
            put(buf, step, y * near + cls * half, half, main[rows], pair[pair_rows])

    def dot(a, b):
        return jnp.dot(a, b, preferred_element_type=F32)

    def dot_t(a, b):
        return lax.dot_general(a, b, (((1,), (1,)), ((), ())), preferred_element_type=F32)

    def reorder(step, phase, held, send, recv, order, tail_order):
        low, high, pair = main_of(held, step, 0, n_lon)
        main = jnp.concatenate([low, high], axis=1)

        def one_row(turn, carry):
            y = row_at(turn)
            moved = dot(order[pl.ds(y * near * msg, near * msg), :], main)
            moved_pair = dot(tail_order[pl.ds(y * near * pairs, near * pairs), :], pair)
            put(send, step, y * near, near, moved, moved_pair)
            send_row(step, phase, send, recv, y)
            return carry

        lax.fori_loop(0, GROUPS, one_row, 0)

    for step in range(STEPS):
        if step:
            stage_halo(step)
            copies = halo_copies(step)
            for copy in copies:
                copy.start()
            for copy in copies:
                copy.wait_recv()
            place_halo(step)

        def sweep_one(r, carry):
            for lo, hi in TILES:
                z[r, :, pl.ds(lo, hi - lo)] = advected(x.at[step], r, lo, hi)
            return carry

        lax.fori_loop(1, EXT_R - 1, sweep_one, 0)

        def sweep_two(r, carry):
            j = r - 2
            slot = (j % 8 // 4) * 16 + (j // 8) * 4 + j % 4
            for lo, hi in TILES:
                new = advected(z, r, lo, hi)[:WIDE]
                if step + 1 < STEPS:
                    x[step + 1, r, pl.ds(0, WIDE), pl.ds(lo, hi - lo)] = new
                else:
                    result[j, :, pl.ds(lo, hi - lo)] = new
                if hi == FEAT:
                    new = jnp.concatenate([new, new], axis=1)
                cur_bf[slot, :, pl.ds(lo, 128)] = new.astype(BF16)
            return carry

        lax.fori_loop(2, ROWS + 2, sweep_two, 0)

        for cls in range(2):
            cells = cur_bf[pl.ds(cls * 16, 16)].reshape(HALF, 384)
            tails = cells[:, MAIN:]
            moved = dot(shuffle, cells[:, :MAIN])
            moved_pair = jnp.where(in_low[: HALF // 2], dot(pair_low, tails), dot(pair_high, tails))
            put_class(send_one, step, cls, moved, moved_pair)
            send_class(step, 0, send_one, recv_one, cls)

        if step == 0:
            pltpu.make_async_copy(owner_in, owner_in, own_recv.at[0]).wait()
            count = n_lon * pairs
            scheme = owner_in[...].reshape(count, 128)
            lane = lax.broadcasted_iota(jnp.int32, (count, 128), 1).astype(F32)
            hit = jnp.where(scheme == lane, 1.0, 0.0)
            to_i, from_i = iota(count, count)
            order_to = to_i // pairs * BLKS + to_i % BLKS
            order_from = from_i // pairs * BLKS + from_i % BLKS
            before = (order_from < order_to) & (from_i % pairs < BLKS)
            ahead = dot(one_hot(before), hit.astype(BF16))
            rank = jnp.sum(hit * ahead, axis=1, keepdims=True)
            row = lax.broadcasted_iota(jnp.int32, (count, 1), 0) % pairs
            inside = rank + (row // BLKS * BLKS).astype(F32)
            tail_place = scheme[:, :1] * pairs + inside
            picked = jnp.where(from_i.astype(F32) == tail_place, 1.0, 0.0)
            tail_perm_t[...] = picked.astype(BF16)
            tail_perm[...] = picked.T.astype(BF16)
            place = (scheme[:, :1] * msg + inside).reshape(n_lon, pairs, 1)
            place = jnp.concatenate([place, place + pairs], axis=1).reshape(n_lon * msg, 1)
            _, from_i = iota(n_lon * msg, n_lon * msg)
            picked = jnp.where(from_i.astype(F32) == place, 1.0, 0.0)
            perm_t[...] = picked.astype(BF16)
            perm[...] = picked.T.astype(BF16)

            for load in loads[3:]:
                load.wait()
            tail_first[...] = jnp.zeros_like(tail_first)
            tail_last[...] = jnp.zeros_like(tail_last)
            for at in range(2):
                where = (pl.ds(at * TAIL, TAIL), pl.ds(at * HID, HID))
                tail_first[where] = v_in[0, pl.ds(MAIN, TAIL), :]
                tail_last[where] = v_out[0, pl.ds(MAIN, TAIL), :]

        arrived(step, 0, recv_one, n_lon, 0)
        reorder(step, 1, recv_one, send_two, recv_two, perm, tail_perm)

        def physics(cls, carry):
            arrived(step, 1, recv_two, n_lon // 2, cls)
            main, pair = class_of_buf(recv_two, step, cls)
            hidden = dot(main, v_in[0, pl.ds(0, MAIN), :])
            extra = dot(pair, tail_first[...])
            extra = extra.reshape(n_lon // 2, pairs, 2 * HID)
            extra = jnp.concatenate([extra[:, :, :HID], extra[:, :, HID:]], axis=1)
            hidden = silu(hidden + extra.reshape(HALF, HID)).astype(BF16)
            hidden = silu(dot(hidden, v_two[0])).astype(BF16)
            hidden = silu(dot(hidden, v_three[0]))
            tendency = dot_t(hidden.astype(BF16), v_out[0, pl.ds(0, MAIN), :])
            hidden = hidden.reshape(n_lon // 2, msg, HID)
            both_cells = jnp.concatenate([hidden[:, :pairs], hidden[:, pairs:]], axis=2)
            both_cells = both_cells.reshape(HALF // 2, 2 * HID).astype(BF16)
            put_class(send_three, step, cls, tendency, dot_t(both_cells, tail_last[...]))
            send_class(step, 2, send_three, recv_three, cls)
            return carry

        lax.fori_loop(0, 2, physics, 0)

        arrived(step, 2, recv_three, n_lon, 0)
        reorder(step, 3, recv_three, send_four, recv_four, perm_t, tail_perm_t)

        def add_home(cls, carry):
            arrived(step, 3, recv_four, n_lon // 2, cls)
            main, pair = class_of_buf(recv_four, step, cls)
            home = dot(unshuffle, main)
            tail = dot(unpair, pair)
            tail = jnp.where(is_upper, pltpu.roll(tail, TAIL, axis=1), tail)
            for blk in range(BLKS):
                for r in range(4):
                    j = 8 * blk + 4 * cls + r
                    lo = (4 * blk + r) * WIDE
                    first_cell = (4 * cls + r) * WIDE
                    for at, hi in ((0, MAIN), (MAIN, FEAT)):
                        part = home if at == 0 else tail[:, :TAIL]
                        part = part[lo : lo + WIDE]
                        cell = first_cell + lax.broadcasted_iota(jnp.int32, part.shape, 0)
                        added = jnp.where(cell < counts[0, blk], part, 0.0)
                        lanes = pl.ds(at, hi - at)
                        if step + 1 < STEPS:
                            x[step + 1, j + 2, pl.ds(0, WIDE), lanes] += added
                        else:
                            result[j, :, lanes] += added
            return carry

        lax.fori_loop(0, 2, add_home, 0)

    finish = pltpu.make_async_copy(result, out, out_sem.at[0])
    finish.start()
    for copy in winds:
        copy.wait_send()
    for step in range(STEPS):
        for copy in halo_copies(step):
            copy.wait_send()
        for phase, send in enumerate((send_one, send_two, send_three, send_four)):
            sent = send.at[step, pl.ds(0, n_lon - 1)]
            pltpu.make_async_copy(sent, sent, ex_send.at[step, phase]).wait()
    sent = owner_in.at[pl.ds(0, n_lon - 1)]
    pltpu.make_async_copy(sent, sent, own_send.at[0]).wait()
    finish.wait()


def solution(mesh):
    n_lat, n_lon = mesh.shape["lat"], mesh.shape["lon"]
    msg = BLKS * COLS // n_lon
    rows = msg * FEAT // 128
    any_spec = pl.BlockSpec(memory_space=pl.ANY)
    smem = pl.BlockSpec(memory_space=pltpu.SMEM)
    dma = pltpu.SemaphoreType.DMA
    vmem = pltpu.VMEM
    scratch = [
        vmem((STEPS, EXT_R, EXT_C, FEAT), F32),
        vmem((EXT_R, EXT_C, FEAT), F32),
        vmem((EXT_R, EXT_C, 2 * LEVELS), F32),
        vmem((ROWS, WIDE, LEVELS), F32),
        vmem((ROWS, WIDE, LEVELS), F32),
        vmem((5, EXT_R, EXT_C, 128), F32),
        vmem((STEPS, 2, 2, ROWS, FEAT), F32),
        vmem((STEPS, 2, 2, ROWS, FEAT), F32),
        vmem((2, 2, ROWS, 128), F32),
        vmem((2, 2, ROWS, 128), F32),
        vmem((STEPS, 4, 8, FEAT), F32),
        vmem((STEPS, 4, 8, FEAT), F32),
        vmem((ROWS, WIDE, 384), BF16),
    ]
    scratch += [vmem((STEPS, n_lon, rows, 128), BF16)] * 8
    scratch += [
        vmem((msg // 2, 128), F32),
        vmem((n_lon, msg // 2, 128), F32),
        vmem((CELLS, CELLS), BF16),
        vmem((CELLS, CELLS), BF16),
        vmem((HALF, HALF), BF16),
        vmem((HALF, HALF), BF16),
        vmem((ROWS, WIDE, FEAT), F32),
        vmem((1, FEAT, HID), BF16),
        vmem((1, HID, HID), BF16),
        vmem((1, HID, HID), BF16),
        vmem((1, FEAT, HID), BF16),
        vmem((2 * TAIL, 2 * HID), BF16),
        vmem((2 * TAIL, 2 * HID), BF16),
        dma((7,)),
        dma((STEPS, 8)),
        dma((STEPS, 8)),
        dma((4,)),
        dma((4,)),
        dma((1,)),
        dma((1,)),
        dma((STEPS, 4)),
        dma((STEPS, 4, 2)),
        dma((1,)),
    ]

    call = pl.pallas_call(
        functools.partial(kernel, n_lat, n_lon),
        out_shape=jax.ShapeDtypeStruct((ROWS, WIDE, FEAT), F32),
        in_specs=[any_spec] * 3 + [smem] * 2 + [any_spec] * 4,
        out_specs=any_spec,
        scratch_shapes=scratch,
        compiler_params=pltpu.CompilerParams(
            collective_id=0, has_side_effects=True, vmem_limit_bytes=60 * 1024 * 1024
        ),
        name="coupled_steps",
    )

    def local(fields, wind_east, wind_north, owner, counts, w_in, w_two, w_three, w_out):
        w_out = jnp.swapaxes(w_out, 1, 2)
        return call(fields, wind_east, wind_north, owner, counts, w_in, w_two, w_three, w_out)

    return jax.shard_map(
        local,
        mesh=mesh,
        in_specs=(
            P("lat", "lon", None),
            P("lat", "lon", None),
            P("lat", "lon", None),
            P("lat", "lon"),
            P("lat", "lon"),
            P("lon", None, None),
            P("lon", None, None),
            P("lon", None, None),
            P("lon", None, None),
        ),
        out_specs=P("lat", "lon", None),
        check_vma=False,
    )
```

```python
import functools

import jax
import jax.numpy as jnp
from jax import lax
from jax.experimental import pallas as pl
from jax.experimental.pallas import tpu as pltpu
from jax.sharding import PartitionSpec as P

F32 = jnp.float32
BF16 = jnp.bfloat16
MESH = pl.DeviceIdType.MESH

STEPS = 2
COLS = 128
ROWS = 32
WIDE = 16
FEAT = 320
LEVELS = 64
HID = 512
BLKS = 4
GROUPS = 4
EXT_R = ROWS + 4
EXT_C = 24
CELLS = ROWS * WIDE
HALF = CELLS // 2
MAIN = 256
TILES = ((0, 128), (128, 256), (256, 320))
TAIL = FEAT - MAIN
TWO = FEAT
THREE = TWO + HID
LAST = THREE + HID
LAYERS = LAST + FEAT


def silu(x):
    half = 0.5 * x
    return half + half * jnp.tanh(half)


def roll(x, shift):
    return pltpu.roll(x, shift % x.shape[0], axis=0)


def kernel(
    n_lat,
    n_lon,
    fields,
    wind_east,
    wind_north,
    owner,
    counts,
    w_in,
    w_two,
    w_three,
    w_out,
    out,
    x,
    z,
    wind,
    raw_east,
    raw_north,
    coef,
    side_out,
    side_in,
    wside_out,
    wside_in,
    corner_out,
    corner_in,
    cur_bf,
    send_one,
    recv_one,
    send_two,
    recv_two,
    send_three,
    recv_three,
    send_four,
    recv_four,
    owner_out,
    owner_in,
    perm,
    perm_t,
    tail_perm,
    tail_perm_t,
    result,
    weights,
    tail_first,
    tail_last,
    load_sem,
    halo_send,
    halo_recv,
    wind_send,
    wind_recv,
    own_send,
    own_recv,
    share_send,
    share_recv,
    ex_send,
    ex_recv,
    out_sem,
):
    near = n_lon // GROUPS
    half = near // 2
    piece = COLS // n_lon
    msg = BLKS * piece
    pairs = msg // 2
    me_lat = lax.axis_index("lat")
    me = lax.axis_index("lon")
    my_y = me // near
    my_z = me % near
    north = lax.rem(me_lat + 1, n_lat)
    south = lax.rem(me_lat + n_lat - 1, n_lat)
    east = lax.rem(me + 1, n_lon)
    west = lax.rem(me + n_lon - 1, n_lon)
    corners = ((south, west), (south, east), (north, west), (north, east))

    def class_of(y, z):
        return (y + z + me_lat) % 2

    def slot_of(y, z):
        return y * near + class_of(y, z) * half + z // 2

    my_class = class_of(my_y, my_z)
    my_slot = slot_of(my_y, my_z)

    wide = near // 2
    quarter = wide // 2

    def pair_slot(y, z):
        return y * wide + z % wide

    def scheme_slot(y, z):
        return pair_slot(y, z) * 2 + z // wide

    def window_slot(y, z):
        return y * wide + class_of(y, z) * quarter + z % wide // 2

    def hops(step, count):
        return min(step, count - step)

    row_order = sorted(range(GROUPS), key=lambda step: -hops(step, GROUPS))
    all_steps = sorted(range(near), key=lambda step: -hops(step, near))
    even_steps = [step for step in all_steps if step % 2 == 0]
    odd_steps = [step for step in all_steps if step % 2]

    def far_first(steps):
        return sorted(steps, key=lambda step: (-abs(step), -step))

    to_holder = [far_first(range(low, low + wide)) for low in (1 - quarter, -quarter)]
    from_holder = [
        [[step for step in far_first(range(low, low + wide)) if step % 2 == odd] for odd in range(2)]
        for low in (-quarter, 1 - quarter)
    ]

    loads = [
        pltpu.make_async_copy(wind_east, raw_east, load_sem.at[0]),
        pltpu.make_async_copy(wind_north, raw_north, load_sem.at[1]),
        pltpu.make_async_copy(
            fields, x.at[0, pl.ds(2, ROWS), pl.ds(0, WIDE), :], load_sem.at[2]
        ),
        pltpu.make_async_copy(w_in.at[0], weights.at[0, pl.ds(0, FEAT)], load_sem.at[3]),
        pltpu.make_async_copy(w_two.at[0], weights.at[0, pl.ds(TWO, HID)], load_sem.at[4]),
        pltpu.make_async_copy(w_three.at[0], weights.at[0, pl.ds(THREE, HID)], load_sem.at[5]),
        pltpu.make_async_copy(w_out.at[0], weights.at[0, pl.ds(LAST, FEAT)], load_sem.at[6]),
    ]
    for load in loads:
        load.start()

    barrier = pltpu.get_barrier_semaphore()

    def greet(step, carry):
        pl.semaphore_signal(
            barrier,
            inc=1,
            device_id=(me_lat, lax.rem(me + step, n_lon)),
            device_id_type=MESH,
        )
        return carry

    lax.fori_loop(1, n_lon, greet, 0)

    def greet_lat(step, carry):
        pl.semaphore_signal(
            barrier,
            inc=1,
            device_id=(lax.rem(me_lat + step, n_lat), me),
            device_id_type=MESH,
        )
        return carry

    lax.fori_loop(1, n_lat, greet_lat, 0)
    for there in corners:
        pl.semaphore_signal(barrier, inc=1, device_id=there, device_id_type=MESH)

    def clear(r, carry):
        x[0, r, pl.ds(WIDE, 8), :] = jnp.zeros((8, FEAT), F32)
        x[1, r, pl.ds(WIDE, 8), :] = jnp.zeros((8, FEAT), F32)
        wind[r, pl.ds(WIDE, 8), :] = jnp.zeros((8, 2 * LEVELS), F32)
        return carry

    lax.fori_loop(0, EXT_R, clear, 0)

    loads[0].wait()
    loads[1].wait()

    def join(r, carry):
        wind[r + 2, pl.ds(0, WIDE), :] = jnp.concatenate([raw_east[r], raw_north[r]], axis=-1)
        return carry

    lax.fori_loop(0, ROWS, join, 0)
    loads[2].wait()

    def remote(src, dst, send, recv, where):
        return pltpu.make_async_remote_copy(
            src_ref=src,
            dst_ref=dst,
            send_sem=send,
            recv_sem=recv,
            device_id=where,
            device_id_type=MESH,
        )

    def halo_copies(step):
        grid = x.at[step]
        inner = pl.ds(0, WIDE)
        copies = [
            remote(
                grid.at[pl.ds(2, 2), inner, :],
                grid.at[pl.ds(ROWS + 2, 2), inner, :],
                halo_send.at[step, 0],
                halo_recv.at[step, 0],
                (south, me),
            ),
            remote(
                grid.at[pl.ds(ROWS, 2), inner, :],
                grid.at[pl.ds(0, 2), inner, :],
                halo_send.at[step, 1],
                halo_recv.at[step, 1],
                (north, me),
            ),
        ]
        for side, there in enumerate((west, east)):
            copies.append(
                remote(
                    side_out.at[step, side],
                    side_in.at[step, side],
                    halo_send.at[step, 2 + side],
                    halo_recv.at[step, 2 + side],
                    (me_lat, there),
                )
            )
        for at, there in enumerate(corners):
            copies.append(
                remote(
                    corner_out.at[step, at],
                    corner_in.at[step, at],
                    halo_send.at[step, 4 + at],
                    halo_recv.at[step, 4 + at],
                    there,
                )
            )
        return copies

    def wind_copies():
        inner = pl.ds(0, WIDE)
        copies = [
            remote(
                wind.at[pl.ds(2, 2), inner, :],
                wind.at[pl.ds(ROWS + 2, 2), inner, :],
                wind_send.at[0],
                wind_recv.at[0],
                (south, me),
            ),
            remote(
                wind.at[pl.ds(ROWS, 2), inner, :],
                wind.at[pl.ds(0, 2), inner, :],
                wind_send.at[1],
                wind_recv.at[1],
                (north, me),
            ),
        ]
        for side, there in enumerate((west, east)):
            copies.append(
                remote(
                    wside_out.at[side],
                    wside_in.at[side],
                    wind_send.at[2 + side],
                    wind_recv.at[2 + side],
                    (me_lat, there),
                )
            )
        return copies

    corner_cells = ((2, 0), (2, WIDE - 1), (ROWS + 1, 0), (ROWS + 1, WIDE - 1))
    corner_slots = ((ROWS + 2, 16), (ROWS + 2, 23), (1, 16), (1, 23))
    side_cells = ((0, 1), (WIDE - 2, WIDE - 1))
    side_slots = ((16, 17), (22, 23))

    def stage_halo(step):
        for side in range(2):
            for at in range(2):
                side_out[step, side, at] = x[step, pl.ds(2, ROWS), side_cells[side][at], :]
        for at, (r, c) in enumerate(corner_cells):
            corner_out[step, at, pl.ds(0, 1), :] = x[step, r, pl.ds(c, 1), :]

    def place_halo(step):
        for side in range(2):
            for at in range(2):
                x[step, pl.ds(2, ROWS), side_slots[side][at], :] = side_in[step, side, at]
        for at, (r, c) in enumerate(corner_slots):
            x[step, r, pl.ds(c, 1), :] = corner_in[step, at, pl.ds(0, 1), :]

    corner_out[...] = jnp.zeros_like(corner_out)
    stage_halo(0)
    for side in range(2):
        for at in range(2):
            wside_out[side, at] = wind[pl.ds(2, ROWS), side_cells[side][at], :]
    for at, (r, c) in enumerate(corner_cells):
        corner_out[0, at, pl.ds(1, 1), pl.ds(0, 128)] = wind[r, pl.ds(c, 1), :]

    owner_row = lax.broadcasted_iota(jnp.int32, (pairs, 128), 0) % BLKS
    owner_tile = jnp.zeros((pairs, 128), F32)
    for blk in range(BLKS):
        place = scheme_slot(owner[0, blk] // near, owner[0, blk] % near)
        owner_tile = jnp.where(owner_row == blk, place.astype(F32), owner_tile)
    owner_out[...] = owner_tile

    pl.semaphore_wait(barrier, n_lon - 1 + n_lat - 1 + 4)

    winds = wind_copies()
    first = halo_copies(0)
    for copy in winds + first:
        copy.start()

    def tell_owner(step, carry):
        there = lax.rem(me + step, n_lon)
        remote(owner_out, owner_in.at[my_slot], own_send.at[0], own_recv.at[0], (me_lat, there)).start()
        return carry

    lax.fori_loop(1, n_lon, tell_owner, 0)
    pltpu.make_async_copy(owner_out, owner_in.at[my_slot], own_recv.at[0]).start()

    for load in loads[3:]:
        load.wait()
    other = my_y * near + lax.rem(my_z + wide, near)
    share = LAYERS // n_lat

    def share_of(which, lat):
        return weights.at[which, pl.ds(pl.multiple_of(lat * share, 16), share)]

    give = remote(
        share_of(0, me_lat), share_of(1, me_lat), share_send.at[0], share_recv.at[0], (me_lat, other)
    )
    give.start()

    def iota(rows, cols):
        return (
            lax.broadcasted_iota(jnp.int32, (rows, cols), 0),
            lax.broadcasted_iota(jnp.int32, (rows, cols), 1),
        )

    def one_hot(where):
        return jnp.where(where, 1.0, 0.0).astype(BF16)

    def main_row(cell):
        blk, at = cell // (HALF // BLKS), cell % (HALF // BLKS)
        return at // piece * msg + at % piece * BLKS + blk

    def pair_row(cell):
        blk, at = cell // (HALF // BLKS), cell % (HALF // BLKS)
        return at // piece * pairs + at % (piece // 2) * BLKS + blk

    def upper(cell):
        return cell % piece >= piece // 2

    to_i, from_i = iota(HALF, HALF)
    shuffle = one_hot(to_i == main_row(from_i))
    unshuffle = one_hot(main_row(to_i) == from_i)
    to_i, from_i = iota(HALF // 2, HALF)
    pair_low = one_hot((to_i == pair_row(from_i)) & ~upper(from_i))
    pair_high = one_hot((to_i == pair_row(from_i)) & upper(from_i))
    to_i, from_i = iota(HALF, HALF // 2)
    unpair = one_hot(pair_row(to_i) == from_i)
    is_upper = upper(to_i)
    in_low = from_i < TAIL

    for copy in winds + first:
        copy.wait_recv()
    for side in range(2):
        for at in range(2):
            wind[pl.ds(2, ROWS), side_slots[side][at], :] = wside_in[side, at]
    for at, (r, c) in enumerate(corner_slots):
        wind[r, pl.ds(c, 1), :] = corner_in[0, at, pl.ds(1, 1), pl.ds(0, 128)]
    place_halo(0)

    first_row = me_lat * ROWS
    last_face = n_lat * ROWS - 1
    low_half = lax.broadcasted_iota(jnp.int32, (EXT_C, 128), 1) < LEVELS

    def both(row):
        turned = pltpu.roll(row, LEVELS, axis=1)
        return jnp.where(low_half, row, turned), jnp.where(low_half, turned, row)

    def face_north(r, here, above):
        j = first_row + r - 2
        keep = jnp.where((j >= 0) & (j < last_face), 0.5, 0.0)
        return (here + above) * keep

    def make_coef(r, carry):
        _, n_low = both(wind[r - 1])
        e_here, n_here = both(wind[r])
        _, n_high = both(wind[r + 1])
        e_face = 0.5 * (e_here + roll(e_here, -1))
        w_face = roll(e_face, 1)
        n_face = face_north(r, n_here, n_high)
        s_face = face_north(r - 1, n_low, n_here)
        coef[0, r] = (
            1.0
            - jnp.maximum(e_face, 0.0)
            + jnp.minimum(w_face, 0.0)
            - jnp.maximum(n_face, 0.0)
            + jnp.minimum(s_face, 0.0)
        )
        coef[1, r] = -jnp.minimum(e_face, 0.0)
        coef[2, r] = jnp.maximum(w_face, 0.0)
        coef[3, r] = -jnp.minimum(n_face, 0.0)
        coef[4, r] = jnp.maximum(s_face, 0.0)
        return carry

    lax.fori_loop(1, EXT_R - 1, make_coef, 0)

    def advected(grid, r, lo, hi):
        w = hi - lo
        lanes = pl.ds(lo, w)
        first_lanes = pl.ds(0, w)
        q = grid[r, :, lanes]
        return (
            coef[0, r, :, first_lanes] * q
            + coef[1, r, :, first_lanes] * roll(q, -1)
            + coef[2, r, :, first_lanes] * roll(q, 1)
            + coef[3, r, :, first_lanes] * grid[r + 1, :, lanes]
            + coef[4, r, :, first_lanes] * grid[r - 1, :, lanes]
        )

    def send_to(step, phase, send, recv, key, y, z, may_be_me):
        from_slot, to_slot = (
            (slot_of(y, z), my_slot),
            (pair_slot(y, z), window_slot(my_y, my_z)),
            (window_slot(y, z), pair_slot(my_y, my_z)),
            (slot_of(y, z), my_slot),
        )[phase]
        there = y * near + z
        arrive = ex_recv.at[step, phase, key]
        src, dst = send.at[step, from_slot], recv.at[step, to_slot]

        def start():
            remote(src, dst, ex_send.at[step, phase], arrive, (me_lat, there)).start()

        if not may_be_me:
            start()
            return
        pl.when(there != me)(start)

        @pl.when(there == me)
        def _():
            pltpu.make_async_copy(src, dst, arrive).start()

    def row_at(turn):
        step = row_order[-1]
        for at, value in enumerate(row_order[:-1]):
            step = jnp.where(turn == at, value, step)
        return lax.rem(my_y + step, GROUPS)

    def send_class(step, phase, send, recv, cls):
        def one_row(turn, carry):
            y = row_at(turn)
            odd = (y + my_y + cls + my_class) % 2
            for even_step, odd_step in zip(even_steps, odd_steps):
                z = lax.rem(my_z + jnp.where(odd == 1, odd_step, even_step), near)
                send_to(step, phase, send, recv, 0, y, z, even_step == 0)
            return carry

        lax.fori_loop(0, GROUPS, one_row, 0)

    def send_row(step, phase, send, recv, y):
        if phase == 3:
            for near_step in all_steps:
                z = lax.rem(my_z + near_step, near)
                send_to(step, phase, send, recv, my_class, y, z, near_step == 0)
            return
        for even_step, odd_step in zip(*to_holder):
            z_step = jnp.where(my_y % 2 == 0, even_step, odd_step)
            z = lax.rem(my_z + z_step + near, near)
            send_to(step, phase, send, recv, my_class, y, z, 0 in (even_step, odd_step))

    def send_back(step, phase, send, recv, cls):
        def one_row(turn, carry):
            y = row_at(turn)
            odd = (y + my_y + cls + my_class) % 2
            (even_even, even_odd), (odd_even, odd_odd) = from_holder
            for steps in zip(even_even, even_odd, odd_even, odd_odd):
                in_even = jnp.where(odd == 1, steps[1], steps[0])
                in_odd = jnp.where(odd == 1, steps[3], steps[2])
                z = lax.rem(my_z + jnp.where(y % 2 == 0, in_even, in_odd) + near, near)
                send_to(step, phase, send, recv, 0, y, z, 0 in steps)
            return carry

        lax.fori_loop(0, GROUPS, one_row, 0)

    def arrived(step, phase, recv, count, key):
        part = recv.at[step, pl.ds(0, count)]
        pltpu.make_async_copy(part, part, ex_recv.at[step, phase, key]).wait()

    def main_of(buf, step, first, count, size, lo, rows):
        where = pl.ds(first, count)
        low = buf[step, where, pl.ds(lo, rows), :].reshape(count * rows, 128)
        high = buf[step, where, pl.ds(size + lo, rows), :].reshape(count * rows, 128)
        pair = buf[step, where, pl.ds(2 * size + lo // 2, rows // 2), :]
        return low, high, pair.reshape(count * rows // 2, 128)

    def joined(parts):
        low, high, pair = (jnp.concatenate(some, axis=0) for some in zip(*parts))
        return jnp.concatenate([low, high], axis=1), pair

    def put(buf, step, first, count, size, lo, rows, main, pair):
        main, pair = main.astype(BF16), pair.astype(BF16)
        where = pl.ds(first, count)
        buf[step, where, pl.ds(lo, rows), :] = main[:, :128].reshape(count, rows, 128)
        buf[step, where, pl.ds(size + lo, rows), :] = main[:, 128:].reshape(count, rows, 128)
        buf[step, where, pl.ds(2 * size + lo // 2, rows // 2), :] = pair.reshape(
            count, rows // 2, 128
        )

    def dot(a, b):
        return jnp.dot(a, b, preferred_element_type=F32)

    def dot_t(a, b):
        return lax.dot_general(a, b, (((1,), (1,)), ((), ())), preferred_element_type=F32)

    def reorder(step, phase, held, held_count, held_size, send, recv, size, order, tail_order):
        main, pair = joined([main_of(held, step, 0, held_count, held_size, 0, held_size)])
        count = near * msg // size

        def one_row(turn, carry):
            y = row_at(turn)
            moved = dot(order[pl.ds(y * near * msg, near * msg), :], main)
            moved_pair = dot(tail_order[pl.ds(y * near * pairs, near * pairs), :], pair)
            put(send, step, y * count, count, size, 0, size, moved, moved_pair)
            send_row(step, phase, send, recv, y)
            return carry

        lax.fori_loop(0, GROUPS, one_row, 0)

    for step in range(STEPS):
        if step:
            stage_halo(step)
            copies = halo_copies(step)
            for copy in copies:
                copy.start()
            for copy in copies:
                copy.wait_recv()
            place_halo(step)

        def sweep_one(r, carry):
            for lo, hi in TILES:
                z[r, :, pl.ds(lo, hi - lo)] = advected(x.at[step], r, lo, hi)
            return carry

        lax.fori_loop(1, EXT_R - 1, sweep_one, 0)

        def sweep_two(r, carry):
            j = r - 2
            slot = (j % 8 // 4) * 16 + (j // 8) * 4 + j % 4
            for lo, hi in TILES:
                new = advected(z, r, lo, hi)[:WIDE]
                if step + 1 < STEPS:
                    x[step + 1, r, pl.ds(0, WIDE), pl.ds(lo, hi - lo)] = new
                else:
                    result[j, :, pl.ds(lo, hi - lo)] = new
                if hi == FEAT:
                    new = jnp.concatenate([new, new], axis=1)
                cur_bf[slot, :, pl.ds(lo, 128)] = new.astype(BF16)
            return carry

        lax.fori_loop(2, ROWS + 2, sweep_two, 0)

        for cls in range(2):
            cells = cur_bf[pl.ds(cls * 16, 16)].reshape(HALF, 384)
            tails = cells[:, MAIN:]
            moved = dot(shuffle, cells[:, :MAIN])
            moved_pair = jnp.where(in_low[: HALF // 2], dot(pair_low, tails), dot(pair_high, tails))
            for y in range(GROUPS):
                rows = slice(y * half * msg, (y + 1) * half * msg)
                pair_rows = slice(y * half * pairs, (y + 1) * half * pairs)
                first = y * near + cls * half
                put(send_one, step, first, half, msg, 0, msg, moved[rows], moved_pair[pair_rows])
            send_class(step, 0, send_one, recv_one, cls)

        if step == 0:
            give.wait_recv()

            def hand_on(at, carry):
                lat = lax.rem(me_lat + at, n_lat)
                mine = share_of(1, me_lat)
                remote(mine, mine, share_send.at[1], share_recv.at[1], (lat, me)).start()
                return carry

            lax.fori_loop(1, n_lat, hand_on, 0)

            pltpu.make_async_copy(owner_in, owner_in, own_recv.at[0]).wait()
            count = n_lon * pairs
            scheme = owner_in[...].reshape(count, 128)
            lane = lax.broadcasted_iota(jnp.int32, (count, 128), 1).astype(F32)
            hit = jnp.where(scheme == lane, 1.0, 0.0)
            to_i, from_i = iota(count, count)
            order_to = to_i // pairs * BLKS + to_i % BLKS
            order_from = from_i // pairs * BLKS + from_i % BLKS
            before = (order_from < order_to) & (from_i % pairs < BLKS)
            ahead = dot(one_hot(before), hit.astype(BF16))
            rank = jnp.sum(hit * ahead, axis=1, keepdims=True)
            row = lax.broadcasted_iota(jnp.int32, (count, 1), 0) % pairs
            inside = rank + (row // BLKS * BLKS).astype(F32)
            tail_place = scheme[:, :1] * pairs + inside
            picked = jnp.where(from_i.astype(F32) == tail_place, 1.0, 0.0)
            tail_perm_t[...] = picked.astype(BF16)
            tail_perm[...] = picked.T.astype(BF16)
            place = (scheme[:, :1] * msg + inside).reshape(n_lon, pairs, 1)
            place = jnp.concatenate([place, place + pairs], axis=1).reshape(n_lon * msg, 1)
            _, from_i = iota(n_lon * msg, n_lon * msg)
            picked = jnp.where(from_i.astype(F32) == place, 1.0, 0.0)
            perm_t[...] = picked.astype(BF16)
            perm[...] = picked.T.astype(BF16)

        arrived(step, 0, recv_one, n_lon, 0)
        reorder(
            step, 1, recv_one, n_lon, msg, send_two, recv_two, 2 * msg, perm, tail_perm
        )

        if step == 0:
            handed = weights.at[1, pl.ds(0, LAYERS - share)]
            pltpu.make_async_copy(handed, handed, share_recv.at[1]).wait()
            tail_first[...] = jnp.zeros_like(tail_first)
            tail_last[...] = jnp.zeros_like(tail_last)
            for which in range(2):
                for at in range(2):
                    rows, lanes = pl.ds(at * TAIL, TAIL), pl.ds(at * HID, HID)
                    tail_first[which, rows, lanes] = weights[which, pl.ds(MAIN, TAIL), :]
                    tail_last[which, rows, lanes] = weights[which, pl.ds(LAST + MAIN, TAIL), :]

        def physics(cls, carry):
            arrived(step, 1, recv_two, n_lon // 4, cls)
            messages = n_lon // 4
            for scheme in range(2):
                which = (scheme + my_z // wide) % 2
                places = [y * wide + cls * quarter for y in range(GROUPS)]
                part = (quarter, 2 * msg, scheme * msg, msg)
                main, pair = joined([main_of(recv_two, step, first, *part) for first in places])
                hidden = dot(main, weights[which, pl.ds(0, MAIN), :])
                extra = dot(pair, tail_first[which])
                extra = extra.reshape(messages, pairs, 2 * HID)
                extra = jnp.concatenate([extra[:, :, :HID], extra[:, :, HID:]], axis=1)
                hidden = silu(hidden + extra.reshape(messages * msg, HID)).astype(BF16)
                hidden = silu(dot(hidden, weights[which, pl.ds(TWO, HID), :])).astype(BF16)
                hidden = silu(dot(hidden, weights[which, pl.ds(THREE, HID), :]))
                tendency = dot_t(hidden.astype(BF16), weights[which, pl.ds(LAST, MAIN), :])
                hidden = hidden.reshape(messages, msg, HID)
                both_cells = jnp.concatenate([hidden[:, :pairs], hidden[:, pairs:]], axis=2)
                both_cells = both_cells.reshape(messages * pairs, 2 * HID).astype(BF16)
                tail = dot_t(both_cells, tail_last[which])
                for y, first in enumerate(places):
                    rows = slice(y * quarter * msg, (y + 1) * quarter * msg)
                    pair_rows = slice(y * quarter * pairs, (y + 1) * quarter * pairs)
                    put(send_three, step, first, *part, tendency[rows], tail[pair_rows])
            send_back(step, 2, send_three, recv_three, cls)
            return carry

        lax.fori_loop(0, 2, physics, 0)

        arrived(step, 2, recv_three, n_lon // 2, 0)
        reorder(
            step, 3, recv_three, n_lon // 2, 2 * msg, send_four, recv_four, msg, perm_t, tail_perm_t
        )

        def add_home(cls, carry):
            arrived(step, 3, recv_four, n_lon // 2, cls)
            main, pair = joined(
                [
                    main_of(recv_four, step, y * near + cls * half, half, msg, 0, msg)
                    for y in range(GROUPS)
                ]
            )
            home = dot(unshuffle, main)
            tail = dot(unpair, pair)
            tail = jnp.where(is_upper, pltpu.roll(tail, TAIL, axis=1), tail)
            for blk in range(BLKS):
                for r in range(4):
                    j = 8 * blk + 4 * cls + r
                    lo = (4 * blk + r) * WIDE
                    first_cell = (4 * cls + r) * WIDE
                    for at, hi in ((0, MAIN), (MAIN, FEAT)):
                        part = home if at == 0 else tail[:, :TAIL]
                        part = part[lo : lo + WIDE]
                        cell = first_cell + lax.broadcasted_iota(jnp.int32, part.shape, 0)
                        added = jnp.where(cell < counts[0, blk], part, 0.0)
                        lanes = pl.ds(at, hi - at)
                        if step + 1 < STEPS:
                            x[step + 1, j + 2, pl.ds(0, WIDE), lanes] += added
                        else:
                            result[j, :, lanes] += added
            return carry

        lax.fori_loop(0, 2, add_home, 0)

    finish = pltpu.make_async_copy(result, out, out_sem.at[0])
    finish.start()
    for copy in winds:
        copy.wait_send()
    for step in range(STEPS):
        for copy in halo_copies(step):
            copy.wait_send()
        for phase, send in enumerate((send_one, send_two, send_three, send_four)):
            sent = send.at[step, pl.ds(0, send.shape[1] - 1)]
            pltpu.make_async_copy(sent, sent, ex_send.at[step, phase]).wait()
    sent = owner_in.at[pl.ds(0, n_lon - 1)]
    pltpu.make_async_copy(sent, sent, own_send.at[0]).wait()
    give.wait_send()
    sent = weights.at[1, pl.ds(0, LAYERS - share)]
    pltpu.make_async_copy(sent, sent, share_send.at[1]).wait()
    finish.wait()


def solution(mesh):
    n_lat, n_lon = mesh.shape["lat"], mesh.shape["lon"]
    msg = BLKS * COLS // n_lon
    rows = msg * FEAT // 128
    any_spec = pl.BlockSpec(memory_space=pl.ANY)
    smem = pl.BlockSpec(memory_space=pltpu.SMEM)
    dma = pltpu.SemaphoreType.DMA
    vmem = pltpu.VMEM
    scratch = [
        vmem((STEPS, EXT_R, EXT_C, FEAT), F32),
        vmem((EXT_R, EXT_C, FEAT), F32),
        vmem((EXT_R, EXT_C, 2 * LEVELS), F32),
        vmem((ROWS, WIDE, LEVELS), F32),
        vmem((ROWS, WIDE, LEVELS), F32),
        vmem((5, EXT_R, EXT_C, 128), F32),
        vmem((STEPS, 2, 2, ROWS, FEAT), F32),
        vmem((STEPS, 2, 2, ROWS, FEAT), F32),
        vmem((2, 2, ROWS, 128), F32),
        vmem((2, 2, ROWS, 128), F32),
        vmem((STEPS, 4, 8, FEAT), F32),
        vmem((STEPS, 4, 8, FEAT), F32),
        vmem((ROWS, WIDE, 384), BF16),
    ]
    whole = vmem((STEPS, n_lon, rows, 128), BF16)
    paired = vmem((STEPS, n_lon // 2, 2 * rows, 128), BF16)
    scratch += [whole, whole, paired, paired, paired, paired, whole, whole]
    scratch += [
        vmem((msg // 2, 128), F32),
        vmem((n_lon, msg // 2, 128), F32),
        vmem((CELLS, CELLS), BF16),
        vmem((CELLS, CELLS), BF16),
        vmem((HALF, HALF), BF16),
        vmem((HALF, HALF), BF16),
        vmem((ROWS, WIDE, FEAT), F32),
        vmem((2, LAYERS, HID), BF16),
        vmem((2, 2 * TAIL, 2 * HID), BF16),
        vmem((2, 2 * TAIL, 2 * HID), BF16),
        dma((7,)),
        dma((STEPS, 8)),
        dma((STEPS, 8)),
        dma((4,)),
        dma((4,)),
        dma((1,)),
        dma((1,)),
        dma((2,)),
        dma((2,)),
        dma((STEPS, 4)),
        dma((STEPS, 4, 2)),
        dma((1,)),
    ]

    call = pl.pallas_call(
        functools.partial(kernel, n_lat, n_lon),
        out_shape=jax.ShapeDtypeStruct((ROWS, WIDE, FEAT), F32),
        in_specs=[any_spec] * 3 + [smem] * 2 + [any_spec] * 4,
        out_specs=any_spec,
        scratch_shapes=scratch,
        compiler_params=pltpu.CompilerParams(
            collective_id=0, has_side_effects=True, vmem_limit_bytes=60 * 1024 * 1024
        ),
        name="coupled_steps",
    )

    def local(fields, wind_east, wind_north, owner, counts, w_in, w_two, w_three, w_out):
        w_out = jnp.swapaxes(w_out, 1, 2)
        return call(fields, wind_east, wind_north, owner, counts, w_in, w_two, w_three, w_out)

    return jax.shard_map(
        local,
        mesh=mesh,
        in_specs=(
            P("lat", "lon", None),
            P("lat", "lon", None),
            P("lat", "lon", None),
            P("lat", "lon"),
            P("lat", "lon"),
            P("lon", None, None),
            P("lon", None, None),
            P("lon", None, None),
            P("lon", None, None),
        ),
        out_specs=P("lat", "lon", None),
        check_vma=False,
    )
```

```python
import functools

import jax
import jax.numpy as jnp
from jax import lax
from jax.experimental import pallas as pl
from jax.experimental.pallas import tpu as pltpu
from jax.sharding import PartitionSpec as P

F32 = jnp.float32
BF16 = jnp.bfloat16
MESH = pl.DeviceIdType.MESH

STEPS = 2
COLS = 128
ROWS = 32
WIDE = 16
FEAT = 320
LEVELS = 64
HID = 512
BLKS = 4
GROUPS = 4
EXT_R = ROWS + 4
EXT_C = 24
CELLS = ROWS * WIDE
HALF = CELLS // 2
MAIN = 256
TILES = ((0, 128), (128, 256), (256, 320))
TAIL = FEAT - MAIN


def silu(x):
    half = 0.5 * x
    return half + half * jnp.tanh(half)


def roll(x, shift):
    return pltpu.roll(x, shift % x.shape[0], axis=0)


def kernel(
    n_lat,
    n_lon,
    fields,
    wind_east,
    wind_north,
    owner,
    counts,
    w_in,
    w_two,
    w_three,
    w_out,
    out,
    x,
    z,
    wind,
    raw_east,
    raw_north,
    coef,
    side_out,
    side_in,
    wside_out,
    wside_in,
    corner_out,
    corner_in,
    cur_bf,
    send_one,
    recv_one,
    send_two,
    recv_two,
    send_three,
    recv_three,
    send_four,
    recv_four,
    owner_out,
    owner_in,
    perm,
    perm_t,
    tail_perm,
    tail_perm_t,
    result,
    v_in,
    v_two,
    v_three,
    v_out,
    tail_first,
    tail_last,
    load_sem,
    halo_send,
    halo_recv,
    wind_send,
    wind_recv,
    own_send,
    own_recv,
    ex_send,
    ex_recv,
    out_sem,
):
    near = n_lon // GROUPS
    half = near // 2
    piece = COLS // n_lon
    msg = BLKS * piece
    pairs = msg // 2
    me_lat = lax.axis_index("lat")
    me = lax.axis_index("lon")
    my_y = me // near
    my_z = me % near
    north = lax.rem(me_lat + 1, n_lat)
    south = lax.rem(me_lat + n_lat - 1, n_lat)
    east = lax.rem(me + 1, n_lon)
    west = lax.rem(me + n_lon - 1, n_lon)
    corners = ((south, west), (south, east), (north, west), (north, east))

    def class_of(y, z):
        return (y + z + me_lat) % 2

    def slot_of(y, z):
        return y * near + class_of(y, z) * half + z // 2

    my_class = class_of(my_y, my_z)
    my_slot = slot_of(my_y, my_z)

    def hops(step, count):
        return min(step, count - step)

    row_order = sorted(range(GROUPS), key=lambda step: -hops(step, GROUPS))
    all_steps = sorted(range(near), key=lambda step: -hops(step, near))
    even_steps = [step for step in all_steps if step % 2 == 0]
    odd_steps = [step for step in all_steps if step % 2]

    loads = [
        pltpu.make_async_copy(wind_east, raw_east, load_sem.at[0]),
        pltpu.make_async_copy(wind_north, raw_north, load_sem.at[1]),
        pltpu.make_async_copy(
            fields, x.at[0, pl.ds(2, ROWS), pl.ds(0, WIDE), :], load_sem.at[2]
        ),
        pltpu.make_async_copy(w_in, v_in, load_sem.at[3]),
        pltpu.make_async_copy(w_two, v_two, load_sem.at[4]),
        pltpu.make_async_copy(w_three, v_three, load_sem.at[5]),
        pltpu.make_async_copy(w_out, v_out, load_sem.at[6]),
    ]
    for load in loads:
        load.start()

    barrier = pltpu.get_barrier_semaphore()

    def greet(step, carry):
        pl.semaphore_signal(
            barrier,
            inc=1,
            device_id=(me_lat, lax.rem(me + step, n_lon)),
            device_id_type=MESH,
        )
        return carry

    lax.fori_loop(1, n_lon, greet, 0)
    for there in ((south, me), (north, me)) + corners:
        pl.semaphore_signal(barrier, inc=1, device_id=there, device_id_type=MESH)

    def clear(r, carry):
        x[0, r, pl.ds(WIDE, 8), :] = jnp.zeros((8, FEAT), F32)
        x[1, r, pl.ds(WIDE, 8), :] = jnp.zeros((8, FEAT), F32)
        wind[r, pl.ds(WIDE, 8), :] = jnp.zeros((8, 2 * LEVELS), F32)
        return carry

    lax.fori_loop(0, EXT_R, clear, 0)

    loads[0].wait()
    loads[1].wait()

    def join(r, carry):
        wind[r + 2, pl.ds(0, WIDE), :] = jnp.concatenate([raw_east[r], raw_north[r]], axis=-1)
        return carry

    lax.fori_loop(0, ROWS, join, 0)
    loads[2].wait()

    def remote(src, dst, send, recv, where):
        return pltpu.make_async_remote_copy(
            src_ref=src,
            dst_ref=dst,
            send_sem=send,
            recv_sem=recv,
            device_id=where,
            device_id_type=MESH,
        )

    def halo_copies(step):
        grid = x.at[step]
        inner = pl.ds(0, WIDE)
        copies = [
            remote(
                grid.at[pl.ds(2, 2), inner, :],
                grid.at[pl.ds(ROWS + 2, 2), inner, :],
                halo_send.at[step, 0],
                halo_recv.at[step, 0],
                (south, me),
            ),
            remote(
                grid.at[pl.ds(ROWS, 2), inner, :],
                grid.at[pl.ds(0, 2), inner, :],
                halo_send.at[step, 1],
                halo_recv.at[step, 1],
                (north, me),
            ),
        ]
        for side, there in enumerate((west, east)):
            copies.append(
                remote(
                    side_out.at[step, side],
                    side_in.at[step, side],
                    halo_send.at[step, 2 + side],
                    halo_recv.at[step, 2 + side],
                    (me_lat, there),
                )
            )
        for at, there in enumerate(corners):
            copies.append(
                remote(
                    corner_out.at[step, at],
                    corner_in.at[step, at],
                    halo_send.at[step, 4 + at],
                    halo_recv.at[step, 4 + at],
                    there,
                )
            )
        return copies

    def wind_copies():
        inner = pl.ds(0, WIDE)
        copies = [
            remote(
                wind.at[pl.ds(2, 2), inner, :],
                wind.at[pl.ds(ROWS + 2, 2), inner, :],
                wind_send.at[0],
                wind_recv.at[0],
                (south, me),
            ),
            remote(
                wind.at[pl.ds(ROWS, 2), inner, :],
                wind.at[pl.ds(0, 2), inner, :],
                wind_send.at[1],
                wind_recv.at[1],
                (north, me),
            ),
        ]
        for side, there in enumerate((west, east)):
            copies.append(
                remote(
                    wside_out.at[side],
                    wside_in.at[side],
                    wind_send.at[2 + side],
                    wind_recv.at[2 + side],
                    (me_lat, there),
                )
            )
        return copies

    corner_cells = ((2, 0), (2, WIDE - 1), (ROWS + 1, 0), (ROWS + 1, WIDE - 1))
    corner_slots = ((ROWS + 2, 16), (ROWS + 2, 23), (1, 16), (1, 23))
    side_cells = ((0, 1), (WIDE - 2, WIDE - 1))
    side_slots = ((16, 17), (22, 23))

    def iota(rows, cols):
        return (
            lax.broadcasted_iota(jnp.int32, (rows, cols), 0),
            lax.broadcasted_iota(jnp.int32, (rows, cols), 1),
        )

    def one_hot(where):
        return jnp.where(where, 1.0, 0.0).astype(BF16)

    def dot(a, b):
        return jnp.dot(a, b, preferred_element_type=F32)

    to_i, from_i = iota(4 * ROWS, CELLS)
    side, second = to_i // (2 * ROWS), to_i // ROWS % 2
    pick_sides = one_hot(from_i == to_i % ROWS * WIDE + side * (WIDE - 2) + second)
    to_i, from_i = iota(8 * ROWS, 4 * ROWS)
    side, second = from_i // (2 * ROWS), from_i // ROWS % 2
    place_sides = one_hot(
        (to_i // 8 == from_i % ROWS) & (to_i % 8 == side * (EXT_C - WIDE - 2) + second)
    )

    def stage_halo(step):
        cells = x[step, pl.ds(2, ROWS), pl.ds(0, WIDE), :].astype(BF16).reshape(CELLS, FEAT)
        picked = dot(pick_sides, cells).astype(BF16)
        side_out[step] = picked.reshape(2, 2 * ROWS, FEAT)
        for at, (r, c) in enumerate(corner_cells):
            corner_out[step, at, pl.ds(0, 1), :] = x[step, r, pl.ds(c, 1), :]

    def place_halo(step):
        sides = dot(place_sides, side_in[step].reshape(4 * ROWS, FEAT))
        x[step, pl.ds(2, ROWS), pl.ds(WIDE, 8), :] = sides.reshape(ROWS, 8, FEAT)
        for at, (r, c) in enumerate(corner_slots):
            x[step, r, pl.ds(c, 1), :] = corner_in[step, at, pl.ds(0, 1), :]

    corner_out[...] = jnp.zeros_like(corner_out)
    stage_halo(0)
    for side in range(2):
        for at in range(2):
            wside_out[side, at] = wind[pl.ds(2, ROWS), side_cells[side][at], :]
    for at, (r, c) in enumerate(corner_cells):
        corner_out[0, at, pl.ds(1, 1), pl.ds(0, 128)] = wind[r, pl.ds(c, 1), :]

    owner_row = lax.broadcasted_iota(jnp.int32, (pairs, 128), 0) % BLKS
    owner_tile = jnp.zeros((pairs, 128), F32)
    for blk in range(BLKS):
        place = slot_of(owner[0, blk] // near, owner[0, blk] % near)
        owner_tile = jnp.where(owner_row == blk, place.astype(F32), owner_tile)
    owner_out[...] = owner_tile

    pl.semaphore_wait(barrier, n_lon - 1 + 6)

    winds = wind_copies()
    first = halo_copies(0)
    for copy in winds + first:
        copy.start()

    def tell_owner(step, carry):
        there = lax.rem(me + step, n_lon)
        remote(owner_out, owner_in.at[my_slot], own_send.at[0], own_recv.at[0], (me_lat, there)).start()
        return carry

    lax.fori_loop(1, n_lon, tell_owner, 0)
    pltpu.make_async_copy(owner_out, owner_in.at[my_slot], own_recv.at[0]).start()

    def main_row(cell):
        blk, at = cell // (HALF // BLKS), cell % (HALF // BLKS)
        return at // piece * msg + at % piece * BLKS + blk

    def pair_row(cell):
        blk, at = cell // (HALF // BLKS), cell % (HALF // BLKS)
        return at // piece * pairs + at % (piece // 2) * BLKS + blk

    def upper(cell):
        return cell % piece >= piece // 2

    to_i, from_i = iota(HALF, HALF)
    shuffle = one_hot(to_i == main_row(from_i))
    unshuffle = one_hot(main_row(to_i) == from_i)
    to_i, from_i = iota(HALF // 2, HALF)
    pair_low = one_hot((to_i == pair_row(from_i)) & ~upper(from_i))
    pair_high = one_hot((to_i == pair_row(from_i)) & upper(from_i))
    to_i, from_i = iota(HALF, HALF // 2)
    unpair = one_hot(pair_row(to_i) == from_i)
    is_upper = upper(to_i)
    in_low = from_i < TAIL

    for copy in winds + first:
        copy.wait_recv()
    for side in range(2):
        for at in range(2):
            wind[pl.ds(2, ROWS), side_slots[side][at], :] = wside_in[side, at]
    for at, (r, c) in enumerate(corner_slots):
        wind[r, pl.ds(c, 1), :] = corner_in[0, at, pl.ds(1, 1), pl.ds(0, 128)]
    place_halo(0)

    first_row = me_lat * ROWS
    last_face = n_lat * ROWS - 1
    low_half = lax.broadcasted_iota(jnp.int32, (EXT_C, 128), 1) < LEVELS

    def both(row):
        turned = pltpu.roll(row, LEVELS, axis=1)
        return jnp.where(low_half, row, turned), jnp.where(low_half, turned, row)

    def face_north(r, here, above):
        j = first_row + r - 2
        keep = jnp.where((j >= 0) & (j < last_face), 0.5, 0.0)
        return (here + above) * keep

    def make_coef(r, carry):
        e_here, n_here, s_face = carry
        e_high, n_high = both(wind[r + 1])
        e_face = 0.5 * (e_here + roll(e_here, -1))
        w_face = roll(e_face, 1)
        n_face = face_north(r, n_here, n_high)
        e_neg, w_pos = jnp.minimum(e_face, 0.0), jnp.maximum(w_face, 0.0)
        n_neg, s_pos = jnp.minimum(n_face, 0.0), jnp.maximum(s_face, 0.0)
        coef[0, r] = 1.0 - (e_face - e_neg) + (w_face - w_pos) - (n_face - n_neg) + (s_face - s_pos)
        coef[1, r] = -e_neg
        coef[2, r] = w_pos
        coef[3, r] = -n_neg
        coef[4, r] = s_pos
        return e_high, n_high, n_face

    _, n_first = both(wind[0])
    e_second, n_second = both(wind[1])
    below = face_north(0, n_first, n_second)
    lax.fori_loop(1, EXT_R - 1, make_coef, (e_second, n_second, below), unroll=2)

    def advected(grid, r, cols):
        at = pl.ds(0, cols)
        here, east_of, west_of, north_of, south_of = (coef[k, r, at, :] for k in range(5))
        out_tiles = []
        for lo, hi in TILES:
            lanes = pl.ds(lo, hi - lo)
            keep = slice(0, hi - lo)
            q = grid[r, :, lanes]
            out_tiles.append(
                here[:, keep] * q[:cols]
                + east_of[:, keep] * roll(q, -1)[:cols]
                + west_of[:, keep] * roll(q, 1)[:cols]
                + north_of[:, keep] * grid[r + 1, at, lanes]
                + south_of[:, keep] * grid[r - 1, at, lanes]
            )
        return out_tiles

    def send_to(step, phase, send, recv, key, y, z, may_be_me):
        there = slot_of(y, z)
        arrive = ex_recv.at[step, phase, key]

        def start():
            remote(
                send.at[step, there],
                recv.at[step, my_slot],
                ex_send.at[step, phase],
                arrive,
                (me_lat, y * near + z),
            ).start()

        if not may_be_me:
            start()
            return
        pl.when(there != my_slot)(start)

        @pl.when(there == my_slot)
        def _():
            pltpu.make_async_copy(send.at[step, there], recv.at[step, my_slot], arrive).start()

    def row_at(turn):
        step = row_order[-1]
        for at, value in enumerate(row_order[:-1]):
            step = jnp.where(turn == at, value, step)
        return lax.rem(my_y + step, GROUPS)

    def send_class(step, phase, send, recv, cls):
        def one_row(turn, carry):
            y = row_at(turn)
            odd = (y + my_y + cls + my_class) % 2
            for even_step, odd_step in zip(even_steps, odd_steps):
                z = lax.rem(my_z + jnp.where(odd == 1, odd_step, even_step), near)
                send_to(step, phase, send, recv, 0, y, z, even_step == 0)
            return carry

        lax.fori_loop(0, GROUPS, one_row, 0)

    def send_row(step, phase, send, recv, y):
        for near_step in all_steps:
            z = lax.rem(my_z + near_step, near)
            send_to(step, phase, send, recv, my_class, y, z, near_step == 0)

    def arrived(step, phase, recv, count, key):
        part = recv.at[step, pl.ds(0, count)]
        pltpu.make_async_copy(part, part, ex_recv.at[step, phase, key]).wait()

    def main_of(buf, step, first, count):
        part = buf[step, pl.ds(first, count)]
        low = part[:, :msg].reshape(count * msg, 128)
        high = part[:, msg : 2 * msg].reshape(count * msg, 128)
        pair = part[:, 2 * msg :].reshape(count * pairs, 128)
        return low, high, pair

    def class_of_buf(buf, step, cls):
        parts = [main_of(buf, step, y * near + cls * half, half) for y in range(GROUPS)]
        low, high, pair = (jnp.concatenate(some, axis=0) for some in zip(*parts))
        return jnp.concatenate([low, high], axis=1), pair

    def put(buf, step, first, count, main, pair):
        main, pair = main.astype(BF16), pair.astype(BF16)
        where = pl.ds(first, count)
        buf[step, where, pl.ds(0, msg), :] = main[:, :128].reshape(count, msg, 128)
        buf[step, where, pl.ds(msg, msg), :] = main[:, 128:].reshape(count, msg, 128)
        buf[step, where, pl.ds(2 * msg, pairs), :] = pair.reshape(count, pairs, 128)

    def put_class(buf, step, cls, main, pair):
        for y in range(GROUPS):
            rows = slice(y * half * msg, (y + 1) * half * msg)
            pair_rows = slice(y * half * pairs, (y + 1) * half * pairs)
            put(buf, step, y * near + cls * half, half, main[rows], pair[pair_rows])

    def dot_t(a, b):
        return lax.dot_general(a, b, (((1,), (1,)), ((), ())), preferred_element_type=F32)

    def reorder(step, phase, held, send, recv, order, tail_order):
        low, high, pair = main_of(held, step, 0, n_lon)
        main = jnp.concatenate([low, high], axis=1)

        def one_row(turn, carry):
            y = row_at(turn)
            moved = dot(order[pl.ds(y * near * msg, near * msg), :], main)
            moved_pair = dot(tail_order[pl.ds(y * near * pairs, near * pairs), :], pair)
            put(send, step, y * near, near, moved, moved_pair)
            send_row(step, phase, send, recv, y)
            return carry

        lax.fori_loop(0, GROUPS, one_row, 0)

    for step in range(STEPS):
        if step:
            stage_halo(step)
            copies = halo_copies(step)
            for copy in copies:
                copy.start()
            for copy in copies:
                copy.wait_recv()
            place_halo(step)

        def sweep_one(r, carry):
            for (lo, hi), new in zip(TILES, advected(x.at[step], r, EXT_C)):
                z[r, :, pl.ds(lo, hi - lo)] = new
            return carry

        lax.fori_loop(1, EXT_R - 1, sweep_one, 0, unroll=2)

        def sweep_two(r, carry):
            j = r - 2
            slot = (j % 8 // 4) * 16 + (j // 8) * 4 + j % 4
            for (lo, hi), new in zip(TILES, advected(z, r, WIDE)):
                if step + 1 < STEPS:
                    x[step + 1, r, pl.ds(0, WIDE), pl.ds(lo, hi - lo)] = new
                else:
                    result[j, :, pl.ds(lo, hi - lo)] = new
                if hi == FEAT:
                    new = jnp.concatenate([new, new], axis=1)
                cur_bf[slot, :, pl.ds(lo, 128)] = new.astype(BF16)
            return carry

        lax.fori_loop(2, ROWS + 2, sweep_two, 0, unroll=2)

        for cls in range(2):
            cells = cur_bf[pl.ds(cls * 16, 16)].reshape(HALF, 384)
            tails = cells[:, MAIN:]
            moved = dot(shuffle, cells[:, :MAIN])
            moved_pair = jnp.where(in_low[: HALF // 2], dot(pair_low, tails), dot(pair_high, tails))
            put_class(send_one, step, cls, moved, moved_pair)
            send_class(step, 0, send_one, recv_one, cls)

        if step == 0:
            pltpu.make_async_copy(owner_in, owner_in, own_recv.at[0]).wait()
            count = n_lon * pairs
            scheme = owner_in[...].reshape(count, 128)
            lane = lax.broadcasted_iota(jnp.int32, (count, 128), 1).astype(F32)
            hit = jnp.where(scheme == lane, 1.0, 0.0)
            to_i, from_i = iota(count, count)
            order_to = to_i // pairs * BLKS + to_i % BLKS
            order_from = from_i // pairs * BLKS + from_i % BLKS
            before = (order_from < order_to) & (from_i % pairs < BLKS)
            ahead = dot(one_hot(before), hit.astype(BF16))
            rank = jnp.sum(hit * ahead, axis=1, keepdims=True)
            row = lax.broadcasted_iota(jnp.int32, (count, 1), 0) % pairs
            inside = rank + (row // BLKS * BLKS).astype(F32)
            tail_place = scheme[:, :1] * pairs + inside
            picked = jnp.where(from_i.astype(F32) == tail_place, 1.0, 0.0)
            tail_perm_t[...] = picked.astype(BF16)
            tail_perm[...] = picked.T.astype(BF16)
            place = (scheme[:, :1] * msg + inside).reshape(n_lon, pairs, 1)
            place = jnp.concatenate([place, place + pairs], axis=1).reshape(n_lon * msg, 1)
            _, from_i = iota(n_lon * msg, n_lon * msg)
            picked = jnp.where(from_i.astype(F32) == place, 1.0, 0.0)
            perm_t[...] = picked.astype(BF16)
            perm[...] = picked.T.astype(BF16)

            for load in loads[3:]:
                load.wait()
            tail_first[...] = jnp.zeros_like(tail_first)
            tail_last[...] = jnp.zeros_like(tail_last)
            for at in range(2):
                where = (pl.ds(at * TAIL, TAIL), pl.ds(at * HID, HID))
                tail_first[where] = v_in[0, pl.ds(MAIN, TAIL), :]
                tail_last[where] = v_out[0, pl.ds(MAIN, TAIL), :]

        arrived(step, 0, recv_one, n_lon, 0)
        reorder(step, 1, recv_one, send_two, recv_two, perm, tail_perm)

        def physics(cls, carry):
            arrived(step, 1, recv_two, n_lon // 2, cls)
            main, pair = class_of_buf(recv_two, step, cls)
            hidden = dot(main, v_in[0, pl.ds(0, MAIN), :])
            extra = dot(pair, tail_first[...])
            extra = extra.reshape(n_lon // 2, pairs, 2 * HID)
            extra = jnp.concatenate([extra[:, :, :HID], extra[:, :, HID:]], axis=1)
            hidden = silu(hidden + extra.reshape(HALF, HID)).astype(BF16)
            hidden = silu(dot(hidden, v_two[0])).astype(BF16)
            hidden = silu(dot(hidden, v_three[0]))
            tendency = dot_t(hidden.astype(BF16), v_out[0, pl.ds(0, MAIN), :])
            hidden = hidden.reshape(n_lon // 2, msg, HID)
            both_cells = jnp.concatenate([hidden[:, :pairs], hidden[:, pairs:]], axis=2)
            both_cells = both_cells.reshape(HALF // 2, 2 * HID).astype(BF16)
            put_class(send_three, step, cls, tendency, dot_t(both_cells, tail_last[...]))
            send_class(step, 2, send_three, recv_three, cls)
            return carry

        lax.fori_loop(0, 2, physics, 0)

        arrived(step, 2, recv_three, n_lon, 0)
        reorder(step, 3, recv_three, send_four, recv_four, perm_t, tail_perm_t)

        def add_home(cls, carry):
            arrived(step, 3, recv_four, n_lon // 2, cls)
            main, pair = class_of_buf(recv_four, step, cls)
            home = dot(unshuffle, main)
            tail = dot(unpair, pair)
            tail = jnp.where(is_upper, pltpu.roll(tail, TAIL, axis=1), tail)
            for blk in range(BLKS):
                for r in range(4):
                    j = 8 * blk + 4 * cls + r
                    lo = (4 * blk + r) * WIDE
                    first_cell = (4 * cls + r) * WIDE
                    for at, hi in ((0, MAIN), (MAIN, FEAT)):
                        part = home if at == 0 else tail[:, :TAIL]
                        part = part[lo : lo + WIDE]
                        cell = first_cell + lax.broadcasted_iota(jnp.int32, part.shape, 0)
                        added = jnp.where(cell < counts[0, blk], part, 0.0)
                        lanes = pl.ds(at, hi - at)
                        if step + 1 < STEPS:
                            x[step + 1, j + 2, pl.ds(0, WIDE), lanes] += added
                        else:
                            result[j, :, lanes] += added
            return carry

        lax.fori_loop(0, 2, add_home, 0)

    finish = pltpu.make_async_copy(result, out, out_sem.at[0])
    finish.start()
    for copy in winds:
        copy.wait_send()
    for step in range(STEPS):
        for copy in halo_copies(step):
            copy.wait_send()
        for phase, send in enumerate((send_one, send_two, send_three, send_four)):
            sent = send.at[step, pl.ds(0, n_lon - 1)]
            pltpu.make_async_copy(sent, sent, ex_send.at[step, phase]).wait()
    sent = owner_in.at[pl.ds(0, n_lon - 1)]
    pltpu.make_async_copy(sent, sent, own_send.at[0]).wait()
    finish.wait()


def solution(mesh):
    n_lat, n_lon = mesh.shape["lat"], mesh.shape["lon"]
    msg = BLKS * COLS // n_lon
    rows = msg * FEAT // 128
    any_spec = pl.BlockSpec(memory_space=pl.ANY)
    smem = pl.BlockSpec(memory_space=pltpu.SMEM)
    dma = pltpu.SemaphoreType.DMA
    vmem = pltpu.VMEM
    scratch = [
        vmem((STEPS, EXT_R, EXT_C, FEAT), F32),
        vmem((EXT_R, EXT_C, FEAT), F32),
        vmem((EXT_R, EXT_C, 2 * LEVELS), F32),
        vmem((ROWS, WIDE, LEVELS), F32),
        vmem((ROWS, WIDE, LEVELS), F32),
        vmem((5, EXT_R, EXT_C, 128), F32),
        vmem((STEPS, 2, 2 * ROWS, FEAT), BF16),
        vmem((STEPS, 2, 2 * ROWS, FEAT), BF16),
        vmem((2, 2, ROWS, 128), F32),
        vmem((2, 2, ROWS, 128), F32),
        vmem((STEPS, 4, 8, FEAT), F32),
        vmem((STEPS, 4, 8, FEAT), F32),
        vmem((ROWS, WIDE, 384), BF16),
    ]
    scratch += [vmem((STEPS, n_lon, rows, 128), BF16)] * 8
    scratch += [
        vmem((msg // 2, 128), F32),
        vmem((n_lon, msg // 2, 128), F32),
        vmem((CELLS, CELLS), BF16),
        vmem((CELLS, CELLS), BF16),
        vmem((HALF, HALF), BF16),
        vmem((HALF, HALF), BF16),
        vmem((ROWS, WIDE, FEAT), F32),
        vmem((1, FEAT, HID), BF16),
        vmem((1, HID, HID), BF16),
        vmem((1, HID, HID), BF16),
        vmem((1, FEAT, HID), BF16),
        vmem((2 * TAIL, 2 * HID), BF16),
        vmem((2 * TAIL, 2 * HID), BF16),
        dma((7,)),
        dma((STEPS, 8)),
        dma((STEPS, 8)),
        dma((4,)),
        dma((4,)),
        dma((1,)),
        dma((1,)),
        dma((STEPS, 4)),
        dma((STEPS, 4, 2)),
        dma((1,)),
    ]

    call = pl.pallas_call(
        functools.partial(kernel, n_lat, n_lon),
        out_shape=jax.ShapeDtypeStruct((ROWS, WIDE, FEAT), F32),
        in_specs=[any_spec] * 3 + [smem] * 2 + [any_spec] * 4,
        out_specs=any_spec,
        scratch_shapes=scratch,
        compiler_params=pltpu.CompilerParams(
            collective_id=0, has_side_effects=True, vmem_limit_bytes=60 * 1024 * 1024
        ),
        name="coupled_steps",
    )

    def local(fields, wind_east, wind_north, owner, counts, w_in, w_two, w_three, w_out):
        w_out = jnp.swapaxes(w_out, 1, 2)
        return call(fields, wind_east, wind_north, owner, counts, w_in, w_two, w_three, w_out)

    return jax.shard_map(
        local,
        mesh=mesh,
        in_specs=(
            P("lat", "lon", None),
            P("lat", "lon", None),
            P("lat", "lon", None),
            P("lat", "lon"),
            P("lat", "lon"),
            P("lon", None, None),
            P("lon", None, None),
            P("lon", None, None),
            P("lon", None, None),
        ),
        out_specs=P("lat", "lon", None),
        check_vma=False,
    )
```

```python
import functools

import jax
import jax.numpy as jnp
from jax import lax
from jax.experimental import pallas as pl
from jax.experimental.pallas import tpu as pltpu
from jax.sharding import PartitionSpec as P

F32 = jnp.float32
BF16 = jnp.bfloat16
MESH = pl.DeviceIdType.MESH

STEPS = 2
COLS = 128
ROWS = 32
WIDE = 16
FEAT = 320
LEVELS = 64
HID = 512
BLKS = 4
GROUPS = 4
EXT_R = ROWS + 4
EXT_C = 24
CELLS = ROWS * WIDE
HALF = CELLS // 2
MAIN = 256
TILES = ((0, 128), (128, 256), (256, 320))
TAIL = FEAT - MAIN


def silu(x):
    half = 0.5 * x
    return half + half * jnp.tanh(half)


def roll(x, shift):
    return pltpu.roll(x, shift % x.shape[0], axis=0)


def kernel(
    n_lat,
    n_lon,
    fields,
    wind_east,
    wind_north,
    owner,
    counts,
    w_in,
    w_two,
    w_three,
    w_out,
    out,
    x,
    z,
    wind,
    raw_east,
    raw_north,
    coef,
    side_out,
    side_in,
    wside_out,
    wside_in,
    corner_out,
    corner_in,
    cur_bf,
    send_one,
    recv_one,
    send_two,
    recv_two,
    send_three,
    recv_three,
    send_four,
    recv_four,
    owner_out,
    owner_in,
    perm,
    perm_t,
    tail_perm,
    tail_perm_t,
    result,
    v_in,
    v_two,
    v_three,
    v_out,
    tail_first,
    tail_last,
    load_sem,
    halo_send,
    halo_recv,
    wind_send,
    wind_recv,
    own_send,
    own_recv,
    ex_send,
    ex_recv,
    out_sem,
):
    near = n_lon // GROUPS
    half = near // 2
    piece = COLS // n_lon
    msg = BLKS * piece
    pairs = msg // 2
    me_lat = lax.axis_index("lat")
    me = lax.axis_index("lon")
    my_y = me // near
    my_z = me % near
    north = lax.rem(me_lat + 1, n_lat)
    south = lax.rem(me_lat + n_lat - 1, n_lat)
    east = lax.rem(me + 1, n_lon)
    west = lax.rem(me + n_lon - 1, n_lon)
    corners = ((south, west), (south, east), (north, west), (north, east))

    def class_of(y, z):
        return (y + z + me_lat) % 2

    def slot_of(y, z):
        return y * near + class_of(y, z) * half + z // 2

    my_class = class_of(my_y, my_z)
    my_slot = slot_of(my_y, my_z)

    def hops(step, count):
        return min(step, count - step)

    row_order = sorted(range(GROUPS), key=lambda step: -hops(step, GROUPS))
    all_steps = sorted(range(near), key=lambda step: -hops(step, near))
    even_steps = [step for step in all_steps if step % 2 == 0]
    odd_steps = [step for step in all_steps if step % 2]

    loads = [
        pltpu.make_async_copy(wind_east, raw_east, load_sem.at[0]),
        pltpu.make_async_copy(wind_north, raw_north, load_sem.at[1]),
        pltpu.make_async_copy(
            fields, x.at[0, pl.ds(2, ROWS), pl.ds(0, WIDE), :], load_sem.at[2]
        ),
        pltpu.make_async_copy(w_in, v_in, load_sem.at[3]),
        pltpu.make_async_copy(w_two, v_two, load_sem.at[4]),
        pltpu.make_async_copy(w_three, v_three, load_sem.at[5]),
        pltpu.make_async_copy(w_out, v_out, load_sem.at[6]),
    ]
    for load in loads:
        load.start()

    barrier = pltpu.get_barrier_semaphore()

    def greet(step, carry):
        pl.semaphore_signal(
            barrier,
            inc=1,
            device_id=(me_lat, lax.rem(me + step, n_lon)),
            device_id_type=MESH,
        )
        return carry

    lax.fori_loop(1, n_lon, greet, 0)
    for there in ((south, me), (north, me)) + corners:
        pl.semaphore_signal(barrier, inc=1, device_id=there, device_id_type=MESH)

    def clear(r, carry):
        x[0, r, pl.ds(WIDE, 8), :] = jnp.zeros((8, FEAT), F32)
        x[1, r, pl.ds(WIDE, 8), :] = jnp.zeros((8, FEAT), F32)
        wind[r, pl.ds(WIDE, 8), :] = jnp.zeros((8, 2 * LEVELS), F32)
        return carry

    lax.fori_loop(0, EXT_R, clear, 0)

    loads[0].wait()
    loads[1].wait()

    def join(r, carry):
        wind[r + 2, pl.ds(0, WIDE), :] = jnp.concatenate([raw_east[r], raw_north[r]], axis=-1)
        return carry

    lax.fori_loop(0, ROWS, join, 0)
    loads[2].wait()

    def remote(src, dst, send, recv, where):
        return pltpu.make_async_remote_copy(
            src_ref=src,
            dst_ref=dst,
            send_sem=send,
            recv_sem=recv,
            device_id=where,
            device_id_type=MESH,
        )

    def halo_copies(step):
        grid = x.at[step]
        inner = pl.ds(0, WIDE)
        copies = [
            remote(
                grid.at[pl.ds(2, 2), inner, :],
                grid.at[pl.ds(ROWS + 2, 2), inner, :],
                halo_send.at[step, 0],
                halo_recv.at[step, 0],
                (south, me),
            ),
            remote(
                grid.at[pl.ds(ROWS, 2), inner, :],
                grid.at[pl.ds(0, 2), inner, :],
                halo_send.at[step, 1],
                halo_recv.at[step, 1],
                (north, me),
            ),
        ]
        for side, there in enumerate((west, east)):
            copies.append(
                remote(
                    side_out.at[step, side],
                    side_in.at[step, side],
                    halo_send.at[step, 2 + side],
                    halo_recv.at[step, 2 + side],
                    (me_lat, there),
                )
            )
        for at, there in enumerate(corners):
            copies.append(
                remote(
                    corner_out.at[step, at],
                    corner_in.at[step, at],
                    halo_send.at[step, 4 + at],
                    halo_recv.at[step, 4 + at],
                    there,
                )
            )
        return copies

    def wind_copies():
        inner = pl.ds(0, WIDE)
        copies = [
            remote(
                wind.at[pl.ds(2, 2), inner, :],
                wind.at[pl.ds(ROWS + 2, 2), inner, :],
                wind_send.at[0],
                wind_recv.at[0],
                (south, me),
            ),
            remote(
                wind.at[pl.ds(ROWS, 2), inner, :],
                wind.at[pl.ds(0, 2), inner, :],
                wind_send.at[1],
                wind_recv.at[1],
                (north, me),
            ),
        ]
        for side, there in enumerate((west, east)):
            copies.append(
                remote(
                    wside_out.at[side],
                    wside_in.at[side],
                    wind_send.at[2 + side],
                    wind_recv.at[2 + side],
                    (me_lat, there),
                )
            )
        return copies

    corner_cells = ((2, 0), (2, WIDE - 1), (ROWS + 1, 0), (ROWS + 1, WIDE - 1))
    corner_slots = ((ROWS + 2, 16), (ROWS + 2, 23), (1, 16), (1, 23))
    side_cells = ((0, 1), (WIDE - 2, WIDE - 1))
    side_slots = ((16, 17), (22, 23))

    def iota(rows, cols):
        return (
            lax.broadcasted_iota(jnp.int32, (rows, cols), 0),
            lax.broadcasted_iota(jnp.int32, (rows, cols), 1),
        )

    def one_hot(where):
        return jnp.where(where, 1.0, 0.0).astype(BF16)

    def dot(a, b):
        return jnp.dot(a, b, preferred_element_type=F32)

    to_i, from_i = iota(4 * ROWS, CELLS)
    side, second = to_i // (2 * ROWS), to_i // ROWS % 2
    pick_sides = one_hot(from_i == to_i % ROWS * WIDE + side * (WIDE - 2) + second)
    to_i, from_i = iota(8 * ROWS, 4 * ROWS)
    side, second = from_i // (2 * ROWS), from_i // ROWS % 2
    place_sides = one_hot(
        (to_i // 8 == from_i % ROWS) & (to_i % 8 == side * (EXT_C - WIDE - 2) + second)
    )

    def stage_halo(step):
        cells = x[step, pl.ds(2, ROWS), pl.ds(0, WIDE), :].astype(BF16).reshape(CELLS, FEAT)
        picked = dot(pick_sides, cells).astype(BF16)
        side_out[step] = picked.reshape(2, 2 * ROWS, FEAT)
        for at, (r, c) in enumerate(corner_cells):
            corner_out[step, at, pl.ds(0, 1), :] = x[step, r, pl.ds(c, 1), :]

    def place_halo(step):
        sides = dot(place_sides, side_in[step].reshape(4 * ROWS, FEAT))
        x[step, pl.ds(2, ROWS), pl.ds(WIDE, 8), :] = sides.reshape(ROWS, 8, FEAT)
        for at, (r, c) in enumerate(corner_slots):
            x[step, r, pl.ds(c, 1), :] = corner_in[step, at, pl.ds(0, 1), :]

    corner_out[...] = jnp.zeros_like(corner_out)
    stage_halo(0)
    for side in range(2):
        for at in range(2):
            wside_out[side, at] = wind[pl.ds(2, ROWS), side_cells[side][at], :]
    for at, (r, c) in enumerate(corner_cells):
        corner_out[0, at, pl.ds(1, 1), pl.ds(0, 128)] = wind[r, pl.ds(c, 1), :]

    owner_row = lax.broadcasted_iota(jnp.int32, (pairs, 128), 0) % BLKS
    owner_tile = jnp.zeros((pairs, 128), F32)
    for blk in range(BLKS):
        place = slot_of(owner[0, blk] // near, owner[0, blk] % near)
        owner_tile = jnp.where(owner_row == blk, place.astype(F32), owner_tile)
    owner_out[...] = owner_tile

    pl.semaphore_wait(barrier, n_lon - 1 + 6)

    winds = wind_copies()
    first = halo_copies(0)
    for copy in winds + first:
        copy.start()

    def tell_owner(step, carry):
        there = lax.rem(me + step, n_lon)
        remote(owner_out, owner_in.at[my_slot], own_send.at[0], own_recv.at[0], (me_lat, there)).start()
        return carry

    lax.fori_loop(1, n_lon, tell_owner, 0)
    pltpu.make_async_copy(owner_out, owner_in.at[my_slot], own_recv.at[0]).start()

    def main_row(cell):
        blk, at = cell // (HALF // BLKS), cell % (HALF // BLKS)
        return at // piece * msg + at % piece * BLKS + blk

    def pair_row(cell):
        blk, at = cell // (HALF // BLKS), cell % (HALF // BLKS)
        return at // piece * pairs + at % (piece // 2) * BLKS + blk

    def upper(cell):
        return cell % piece >= piece // 2

    to_i, from_i = iota(HALF, HALF)
    shuffle = one_hot(to_i == main_row(from_i))
    unshuffle = one_hot(main_row(to_i) == from_i)
    to_i, from_i = iota(HALF // 2, HALF)
    pair_low = one_hot((to_i == pair_row(from_i)) & ~upper(from_i))
    pair_high = one_hot((to_i == pair_row(from_i)) & upper(from_i))
    to_i, from_i = iota(HALF, HALF // 2)
    unpair = one_hot(pair_row(to_i) == from_i)
    is_upper = upper(to_i)
    in_low = from_i < TAIL

    for copy in winds + first:
        copy.wait_recv()
    for side in range(2):
        for at in range(2):
            wind[pl.ds(2, ROWS), side_slots[side][at], :] = wside_in[side, at]
    for at, (r, c) in enumerate(corner_slots):
        wind[r, pl.ds(c, 1), :] = corner_in[0, at, pl.ds(1, 1), pl.ds(0, 128)]
    place_halo(0)

    first_row = me_lat * ROWS
    last_face = n_lat * ROWS - 1
    low_half = lax.broadcasted_iota(jnp.int32, (EXT_C, 128), 1) < LEVELS

    def both(row):
        turned = pltpu.roll(row, LEVELS, axis=1)
        return jnp.where(low_half, row, turned), jnp.where(low_half, turned, row)

    def face_north(r, here, above):
        j = first_row + r - 2
        keep = jnp.where((j >= 0) & (j < last_face), 0.5, 0.0)
        return (here + above) * keep

    def make_coef(r, carry):
        e_here, n_here, s_face = carry
        e_high, n_high = both(wind[r + 1])
        e_face = 0.5 * (e_here + roll(e_here, -1))
        w_face = roll(e_face, 1)
        n_face = face_north(r, n_here, n_high)
        e_neg, w_pos = jnp.minimum(e_face, 0.0), jnp.maximum(w_face, 0.0)
        n_neg, s_pos = jnp.minimum(n_face, 0.0), jnp.maximum(s_face, 0.0)
        coef[0, r] = 1.0 - (e_face - e_neg) + (w_face - w_pos) - (n_face - n_neg) + (s_face - s_pos)
        coef[1, r] = -e_neg
        coef[2, r] = w_pos
        coef[3, r] = -n_neg
        coef[4, r] = s_pos
        return e_high, n_high, n_face

    _, n_first = both(wind[0])
    e_second, n_second = both(wind[1])
    below = face_north(0, n_first, n_second)
    lax.fori_loop(1, EXT_R - 1, make_coef, (e_second, n_second, below), unroll=2)

    def advected(grid, r, cols):
        at = pl.ds(0, cols)
        here, east_of, west_of, north_of, south_of = (coef[k, r, at, :] for k in range(5))
        out_tiles = []
        for lo, hi in TILES:
            lanes = pl.ds(lo, hi - lo)
            keep = slice(0, hi - lo)
            q = grid[r, :, lanes]
            out_tiles.append(
                here[:, keep] * q[:cols]
                + east_of[:, keep] * roll(q, -1)[:cols]
                + west_of[:, keep] * roll(q, 1)[:cols]
                + north_of[:, keep] * grid[r + 1, at, lanes]
                + south_of[:, keep] * grid[r - 1, at, lanes]
            )
        return out_tiles

    def send_to(step, phase, send, recv, key, y, z, may_be_me):
        there = slot_of(y, z)
        arrive = ex_recv.at[step, phase, key]

        def start():
            remote(
                send.at[step, there],
                recv.at[step, my_slot],
                ex_send.at[step, phase],
                arrive,
                (me_lat, y * near + z),
            ).start()

        if not may_be_me:
            start()
            return
        pl.when(there != my_slot)(start)

        @pl.when(there == my_slot)
        def _():
            pltpu.make_async_copy(send.at[step, there], recv.at[step, my_slot], arrive).start()

    def row_at(turn):
        step = row_order[-1]
        for at, value in enumerate(row_order[:-1]):
            step = jnp.where(turn == at, value, step)
        return lax.rem(my_y + step, GROUPS)

    def send_class(step, phase, send, recv, cls):
        def one_row(turn, carry):
            y = row_at(turn)
            odd = (y + my_y + cls + my_class) % 2
            for even_step, odd_step in zip(even_steps, odd_steps):
                z = lax.rem(my_z + jnp.where(odd == 1, odd_step, even_step), near)
                send_to(step, phase, send, recv, 0, y, z, even_step == 0)
            return carry

        lax.fori_loop(0, GROUPS, one_row, 0)

    def send_row(step, phase, send, recv, y):
        for near_step in all_steps:
            z = lax.rem(my_z + near_step, near)
            send_to(step, phase, send, recv, my_class, y, z, near_step == 0)

    def arrived(step, phase, recv, count, key):
        part = recv.at[step, pl.ds(0, count)]
        pltpu.make_async_copy(part, part, ex_recv.at[step, phase, key]).wait()

    def main_of(buf, step, first, count):
        part = buf[step, pl.ds(first, count)]
        low = part[:, :msg].reshape(count * msg, 128)
        high = part[:, msg : 2 * msg].reshape(count * msg, 128)
        pair = part[:, 2 * msg :].reshape(count * pairs, 128)
        return low, high, pair

    def class_of_buf(buf, step, cls):
        parts = [main_of(buf, step, y * near + cls * half, half) for y in range(GROUPS)]
        low, high, pair = (jnp.concatenate(some, axis=0) for some in zip(*parts))
        return jnp.concatenate([low, high], axis=1), pair

    def put(buf, step, first, count, main, pair):
        main, pair = main.astype(BF16), pair.astype(BF16)
        where = pl.ds(first, count)
        buf[step, where, pl.ds(0, msg), :] = main[:, :128].reshape(count, msg, 128)
        buf[step, where, pl.ds(msg, msg), :] = main[:, 128:].reshape(count, msg, 128)
        buf[step, where, pl.ds(2 * msg, pairs), :] = pair.reshape(count, pairs, 128)

    def put_class(buf, step, cls, main, pair):
        for y in range(GROUPS):
            rows = slice(y * half * msg, (y + 1) * half * msg)
            pair_rows = slice(y * half * pairs, (y + 1) * half * pairs)
            put(buf, step, y * near + cls * half, half, main[rows], pair[pair_rows])

    def dot_t(a, b):
        return lax.dot_general(a, b, (((1,), (1,)), ((), ())), preferred_element_type=F32)

    def reorder(step, phase, held, send, recv, order, tail_order):
        low, high, pair = main_of(held, step, 0, n_lon)
        main = jnp.concatenate([low, high], axis=1)

        def one_row(turn, carry):
            y = row_at(turn)
            moved = dot(order[pl.ds(y * near * msg, near * msg), :], main)
            moved_pair = dot(tail_order[pl.ds(y * near * pairs, near * pairs), :], pair)
            put(send, step, y * near, near, moved, moved_pair)
            send_row(step, phase, send, recv, y)
            return carry

        lax.fori_loop(0, GROUPS, one_row, 0)

    for step in range(STEPS):
        if step:
            copies = halo_copies(step)
            for copy in copies[:2]:
                copy.start()
            stage_halo(step)
            for copy in copies[2:]:
                copy.start()
            for copy in copies:
                copy.wait_recv()
            place_halo(step)

        def sweep_one(r, carry):
            for (lo, hi), new in zip(TILES, advected(x.at[step], r, EXT_C)):
                z[r, :, pl.ds(lo, hi - lo)] = new
            return carry

        lax.fori_loop(1, EXT_R - 1, sweep_one, 0, unroll=2)

        def sweep_two(r, carry):
            j = r - 2
            slot = (j % 8 // 4) * 16 + (j // 8) * 4 + j % 4
            for (lo, hi), new in zip(TILES, advected(z, r, WIDE)):
                if step + 1 < STEPS:
                    x[step + 1, r, pl.ds(0, WIDE), pl.ds(lo, hi - lo)] = new
                else:
                    result[j, :, pl.ds(lo, hi - lo)] = new
                if hi == FEAT:
                    new = jnp.concatenate([new, new], axis=1)
                cur_bf[slot, :, pl.ds(lo, 128)] = new.astype(BF16)
            return carry

        lax.fori_loop(2, ROWS + 2, sweep_two, 0, unroll=4)

        for cls in range(2):
            cells = cur_bf[pl.ds(cls * 16, 16)].reshape(HALF, 384)
            tails = cells[:, MAIN:]
            moved = dot(shuffle, cells[:, :MAIN])
            moved_pair = jnp.where(in_low[: HALF // 2], dot(pair_low, tails), dot(pair_high, tails))
            put_class(send_one, step, cls, moved, moved_pair)
            send_class(step, 0, send_one, recv_one, cls)

        if step == 0:
            pltpu.make_async_copy(owner_in, owner_in, own_recv.at[0]).wait()
            count = n_lon * pairs
            scheme = owner_in[...].reshape(count, 128)
            lane = lax.broadcasted_iota(jnp.int32, (count, 128), 1).astype(F32)
            hit = jnp.where(scheme == lane, 1.0, 0.0)
            to_i, from_i = iota(count, count)
            order_to = to_i // pairs * BLKS + to_i % BLKS
            order_from = from_i // pairs * BLKS + from_i % BLKS
            before = (order_from < order_to) & (from_i % pairs < BLKS)
            ahead = dot(one_hot(before), hit.astype(BF16))
            rank = jnp.sum(hit * ahead, axis=1, keepdims=True)
            row = lax.broadcasted_iota(jnp.int32, (count, 1), 0) % pairs
            inside = rank + (row // BLKS * BLKS).astype(F32)
            tail_place = scheme[:, :1] * pairs + inside
            place = (scheme[:, :1] * msg + inside).reshape(n_lon, pairs, 1)
            place = jnp.concatenate([place, place + pairs], axis=1).reshape(n_lon * msg, 1)

            def ordered(column, size):
                row = jnp.broadcast_to(column, (size, 128)).T[:1]
                to_i, _ = iota(size, size)
                return one_hot(to_i.astype(F32) == row)

            tail_perm[...] = ordered(tail_place, count)
            perm[...] = ordered(place, n_lon * msg)

        arrived(step, 0, recv_one, n_lon, 0)
        reorder(step, 1, recv_one, send_two, recv_two, perm, tail_perm)

        if step == 0:
            _, from_i = iota(n_lon * pairs, n_lon * pairs)
            tail_perm_t[...] = one_hot(from_i.astype(F32) == tail_place)
            _, from_i = iota(n_lon * msg, n_lon * msg)
            perm_t[...] = one_hot(from_i.astype(F32) == place)
            for load in loads[3:]:
                load.wait()
            tail_first[...] = jnp.zeros_like(tail_first)
            tail_last[...] = jnp.zeros_like(tail_last)
            for at in range(2):
                where = (pl.ds(at * TAIL, TAIL), pl.ds(at * HID, HID))
                tail_first[where] = v_in[0, pl.ds(MAIN, TAIL), :]
                tail_last[where] = v_out[0, pl.ds(MAIN, TAIL), :]

        def physics(cls, carry):
            arrived(step, 1, recv_two, n_lon // 2, cls)
            main, pair = class_of_buf(recv_two, step, cls)
            hidden = dot(main, v_in[0, pl.ds(0, MAIN), :])
            extra = dot(pair, tail_first[...])
            extra = extra.reshape(n_lon // 2, pairs, 2 * HID)
            extra = jnp.concatenate([extra[:, :, :HID], extra[:, :, HID:]], axis=1)
            hidden = silu(hidden + extra.reshape(HALF, HID)).astype(BF16)
            hidden = silu(dot(hidden, v_two[0])).astype(BF16)
            hidden = silu(dot(hidden, v_three[0]))
            tendency = dot_t(hidden.astype(BF16), v_out[0, pl.ds(0, MAIN), :])
            hidden = hidden.reshape(n_lon // 2, msg, HID)
            both_cells = jnp.concatenate([hidden[:, :pairs], hidden[:, pairs:]], axis=2)
            both_cells = both_cells.reshape(HALF // 2, 2 * HID).astype(BF16)
            put_class(send_three, step, cls, tendency, dot_t(both_cells, tail_last[...]))
            send_class(step, 2, send_three, recv_three, cls)
            return carry

        lax.fori_loop(0, 2, physics, 0)

        arrived(step, 2, recv_three, n_lon, 0)
        reorder(step, 3, recv_three, send_four, recv_four, perm_t, tail_perm_t)

        def add_home(cls, carry):
            arrived(step, 3, recv_four, n_lon // 2, cls)
            main, pair = class_of_buf(recv_four, step, cls)
            home = dot(unshuffle, main)
            tail = dot(unpair, pair)
            tail = jnp.where(is_upper, pltpu.roll(tail, TAIL, axis=1), tail)
            for blk in range(BLKS):
                for r in range(4):
                    j = 8 * blk + 4 * cls + r
                    lo = (4 * blk + r) * WIDE
                    first_cell = (4 * cls + r) * WIDE
                    for at, hi in ((0, MAIN), (MAIN, FEAT)):
                        part = home if at == 0 else tail[:, :TAIL]
                        part = part[lo : lo + WIDE]
                        cell = first_cell + lax.broadcasted_iota(jnp.int32, part.shape, 0)
                        added = jnp.where(cell < counts[0, blk], part, 0.0)
                        lanes = pl.ds(at, hi - at)
                        if step + 1 < STEPS:
                            x[step + 1, j + 2, pl.ds(0, WIDE), lanes] += added
                        else:
                            result[j, :, lanes] += added
                if step + 1 == STEPS:
                    some = pl.ds(8 * blk + 4 * cls, 4)
                    pltpu.make_async_copy(result.at[some], out.at[some], out_sem.at[0]).start()
            return carry

        lax.fori_loop(0, 2, add_home, 0)

    for copy in winds:
        copy.wait_send()
    for step in range(STEPS):
        for copy in halo_copies(step):
            copy.wait_send()
        for phase, send in enumerate((send_one, send_two, send_three, send_four)):
            sent = send.at[step, pl.ds(0, n_lon - 1)]
            pltpu.make_async_copy(sent, sent, ex_send.at[step, phase]).wait()
    sent = owner_in.at[pl.ds(0, n_lon - 1)]
    pltpu.make_async_copy(sent, sent, own_send.at[0]).wait()
    pltpu.make_async_copy(result, out, out_sem.at[0]).wait()


def solution(mesh):
    n_lat, n_lon = mesh.shape["lat"], mesh.shape["lon"]
    msg = BLKS * COLS // n_lon
    rows = msg * FEAT // 128
    any_spec = pl.BlockSpec(memory_space=pl.ANY)
    smem = pl.BlockSpec(memory_space=pltpu.SMEM)
    dma = pltpu.SemaphoreType.DMA
    vmem = pltpu.VMEM
    scratch = [
        vmem((STEPS, EXT_R, EXT_C, FEAT), F32),
        vmem((EXT_R, EXT_C, FEAT), F32),
        vmem((EXT_R, EXT_C, 2 * LEVELS), F32),
        vmem((ROWS, WIDE, LEVELS), F32),
        vmem((ROWS, WIDE, LEVELS), F32),
        vmem((5, EXT_R, EXT_C, 128), F32),
        vmem((STEPS, 2, 2 * ROWS, FEAT), BF16),
        vmem((STEPS, 2, 2 * ROWS, FEAT), BF16),
        vmem((2, 2, ROWS, 128), F32),
        vmem((2, 2, ROWS, 128), F32),
        vmem((STEPS, 4, 8, FEAT), F32),
        vmem((STEPS, 4, 8, FEAT), F32),
        vmem((ROWS, WIDE, 384), BF16),
    ]
    scratch += [vmem((STEPS, n_lon, rows, 128), BF16)] * 8
    scratch += [
        vmem((msg // 2, 128), F32),
        vmem((n_lon, msg // 2, 128), F32),
        vmem((CELLS, CELLS), BF16),
        vmem((CELLS, CELLS), BF16),
        vmem((HALF, HALF), BF16),
        vmem((HALF, HALF), BF16),
        vmem((ROWS, WIDE, FEAT), F32),
        vmem((1, FEAT, HID), BF16),
        vmem((1, HID, HID), BF16),
        vmem((1, HID, HID), BF16),
        vmem((1, FEAT, HID), BF16),
        vmem((2 * TAIL, 2 * HID), BF16),
        vmem((2 * TAIL, 2 * HID), BF16),
        dma((7,)),
        dma((STEPS, 8)),
        dma((STEPS, 8)),
        dma((4,)),
        dma((4,)),
        dma((1,)),
        dma((1,)),
        dma((STEPS, 4)),
        dma((STEPS, 4, 2)),
        dma((1,)),
    ]

    call = pl.pallas_call(
        functools.partial(kernel, n_lat, n_lon),
        out_shape=jax.ShapeDtypeStruct((ROWS, WIDE, FEAT), F32),
        in_specs=[any_spec] * 3 + [smem] * 2 + [any_spec] * 4,
        out_specs=any_spec,
        scratch_shapes=scratch,
        compiler_params=pltpu.CompilerParams(
            collective_id=0, has_side_effects=True, vmem_limit_bytes=60 * 1024 * 1024
        ),
        name="coupled_steps",
    )

    def local(fields, wind_east, wind_north, owner, counts, w_in, w_two, w_three, w_out):
        w_out = jnp.swapaxes(w_out, 1, 2)
        return call(fields, wind_east, wind_north, owner, counts, w_in, w_two, w_three, w_out)

    return jax.shard_map(
        local,
        mesh=mesh,
        in_specs=(
            P("lat", "lon", None),
            P("lat", "lon", None),
            P("lat", "lon", None),
            P("lat", "lon"),
            P("lat", "lon"),
            P("lon", None, None),
            P("lon", None, None),
            P("lon", None, None),
            P("lon", None, None),
        ),
        out_specs=P("lat", "lon", None),
        check_vma=False,
    )
```

```python
import functools

import jax
import jax.numpy as jnp
from jax import lax
from jax.experimental import pallas as pl
from jax.experimental.pallas import tpu as pltpu
from jax.sharding import PartitionSpec as P

F32 = jnp.float32
BF16 = jnp.bfloat16
MESH = pl.DeviceIdType.MESH

STEPS = 2
COLS = 128
ROWS = 32
WIDE = 16
FEAT = 320
LEVELS = 64
HID = 512
BLKS = 4
GROUPS = 4
EXT_R = ROWS + 4
EXT_C = 24
CELLS = ROWS * WIDE
CLASSES = 2
PART = CELLS // CLASSES
BAND = 8 // CLASSES
MAIN = 256
TILES = ((0, 128), (128, 256), (256, 320))
TAIL = FEAT - MAIN


def silu(x):
    half = 0.5 * x
    return half + half * jnp.tanh(half)


def roll(x, shift):
    return pltpu.roll(x, shift % x.shape[0], axis=0)


def kernel(
    n_lat,
    n_lon,
    fields,
    wind_east,
    wind_north,
    owner,
    counts,
    w_in,
    w_two,
    w_three,
    w_out,
    out,
    x,
    z,
    wind,
    raw_east,
    raw_north,
    coef,
    side_out,
    side_in,
    wside_out,
    wside_in,
    corner_out,
    corner_in,
    cur_bf,
    send_one,
    recv_one,
    send_two,
    recv_two,
    send_three,
    recv_three,
    send_four,
    recv_four,
    owner_out,
    owner_in,
    perm,
    perm_t,
    tail_perm,
    tail_perm_t,
    result,
    v_in,
    v_two,
    v_three,
    v_out,
    tail_first,
    tail_last,
    load_sem,
    halo_send,
    halo_recv,
    wind_send,
    wind_recv,
    own_send,
    own_recv,
    ex_send,
    ex_recv,
    out_sem,
):
    near = n_lon // GROUPS
    half = near // CLASSES
    piece = COLS // n_lon
    msg = BLKS * piece
    pairs = msg // 2
    me_lat = lax.axis_index("lat")
    me = lax.axis_index("lon")
    my_y = me // near
    my_z = me % near
    north = lax.rem(me_lat + 1, n_lat)
    south = lax.rem(me_lat + n_lat - 1, n_lat)
    east = lax.rem(me + 1, n_lon)
    west = lax.rem(me + n_lon - 1, n_lon)
    corners = ((south, west), (south, east), (north, west), (north, east))

    def class_of(y, z):
        return (y + z + me_lat) % CLASSES

    def slot_of(y, z):
        return y * near + class_of(y, z) * half + z // CLASSES

    my_class = class_of(my_y, my_z)
    my_slot = slot_of(my_y, my_z)

    def hops(step, count):
        return min(step, count - step)

    row_order = sorted(range(GROUPS), key=lambda step: -hops(step, GROUPS))
    all_steps = sorted(range(near), key=lambda step: -hops(step, near))
    class_steps = [[step for step in all_steps if step % CLASSES == c] for c in range(CLASSES)]

    loads = [
        pltpu.make_async_copy(wind_east, raw_east, load_sem.at[0]),
        pltpu.make_async_copy(wind_north, raw_north, load_sem.at[1]),
        pltpu.make_async_copy(
            fields, x.at[0, pl.ds(2, ROWS), pl.ds(0, WIDE), :], load_sem.at[2]
        ),
        pltpu.make_async_copy(w_in, v_in, load_sem.at[3]),
        pltpu.make_async_copy(w_two, v_two, load_sem.at[4]),
        pltpu.make_async_copy(w_three, v_three, load_sem.at[5]),
        pltpu.make_async_copy(w_out, v_out, load_sem.at[6]),
    ]
    for load in loads:
        load.start()

    barrier = pltpu.get_barrier_semaphore()

    def greet(step, carry):
        pl.semaphore_signal(
            barrier,
            inc=1,
            device_id=(me_lat, lax.rem(me + step, n_lon)),
            device_id_type=MESH,
        )
        return carry

    lax.fori_loop(1, n_lon, greet, 0)
    for there in ((south, me), (north, me)) + corners:
        pl.semaphore_signal(barrier, inc=1, device_id=there, device_id_type=MESH)

    def clear(r, carry):
        x[0, r, pl.ds(WIDE, 8), :] = jnp.zeros((8, FEAT), F32)
        x[1, r, pl.ds(WIDE, 8), :] = jnp.zeros((8, FEAT), F32)
        wind[r, pl.ds(WIDE, 8), :] = jnp.zeros((8, 2 * LEVELS), F32)
        return carry

    lax.fori_loop(0, EXT_R, clear, 0)

    loads[0].wait()
    loads[1].wait()

    def join(r, carry):
        wind[r + 2, pl.ds(0, WIDE), :] = jnp.concatenate([raw_east[r], raw_north[r]], axis=-1)
        return carry

    lax.fori_loop(0, ROWS, join, 0)
    loads[2].wait()

    def remote(src, dst, send, recv, where):
        return pltpu.make_async_remote_copy(
            src_ref=src,
            dst_ref=dst,
            send_sem=send,
            recv_sem=recv,
            device_id=where,
            device_id_type=MESH,
        )

    def halo_copies(step):
        grid = x.at[step]
        inner = pl.ds(0, WIDE)
        copies = [
            remote(
                grid.at[pl.ds(2, 2), inner, :],
                grid.at[pl.ds(ROWS + 2, 2), inner, :],
                halo_send.at[step, 0],
                halo_recv.at[step, 0],
                (south, me),
            ),
            remote(
                grid.at[pl.ds(ROWS, 2), inner, :],
                grid.at[pl.ds(0, 2), inner, :],
                halo_send.at[step, 1],
                halo_recv.at[step, 1],
                (north, me),
            ),
        ]
        for side, there in enumerate((west, east)):
            copies.append(
                remote(
                    side_out.at[step, side],
                    side_in.at[step, side],
                    halo_send.at[step, 2 + side],
                    halo_recv.at[step, 2 + side],
                    (me_lat, there),
                )
            )
        for at, there in enumerate(corners):
            copies.append(
                remote(
                    corner_out.at[step, at],
                    corner_in.at[step, at],
                    halo_send.at[step, 4 + at],
                    halo_recv.at[step, 4 + at],
                    there,
                )
            )
        return copies

    def wind_copies():
        inner = pl.ds(0, WIDE)
        copies = [
            remote(
                wind.at[pl.ds(2, 2), inner, :],
                wind.at[pl.ds(ROWS + 2, 2), inner, :],
                wind_send.at[0],
                wind_recv.at[0],
                (south, me),
            ),
            remote(
                wind.at[pl.ds(ROWS, 2), inner, :],
                wind.at[pl.ds(0, 2), inner, :],
                wind_send.at[1],
                wind_recv.at[1],
                (north, me),
            ),
        ]
        for side, there in enumerate((west, east)):
            copies.append(
                remote(
                    wside_out.at[side],
                    wside_in.at[side],
                    wind_send.at[2 + side],
                    wind_recv.at[2 + side],
                    (me_lat, there),
                )
            )
        return copies

    corner_cells = ((2, 0), (2, WIDE - 1), (ROWS + 1, 0), (ROWS + 1, WIDE - 1))
    corner_slots = ((ROWS + 2, 16), (ROWS + 2, 23), (1, 16), (1, 23))
    side_cells = ((0, 1), (WIDE - 2, WIDE - 1))
    side_slots = ((16, 17), (22, 23))

    def iota(rows, cols):
        return (
            lax.broadcasted_iota(jnp.int32, (rows, cols), 0),
            lax.broadcasted_iota(jnp.int32, (rows, cols), 1),
        )

    def one_hot(where):
        return jnp.where(where, 1.0, 0.0).astype(BF16)

    def dot(a, b):
        return jnp.dot(a, b, preferred_element_type=F32)

    to_i, from_i = iota(4 * ROWS, CELLS)
    side, second = to_i // (2 * ROWS), to_i // ROWS % 2
    pick_sides = one_hot(from_i == to_i % ROWS * WIDE + side * (WIDE - 2) + second)
    to_i, from_i = iota(8 * ROWS, 4 * ROWS)
    side, second = from_i // (2 * ROWS), from_i // ROWS % 2
    place_sides = one_hot(
        (to_i // 8 == from_i % ROWS) & (to_i % 8 == side * (EXT_C - WIDE - 2) + second)
    )

    def stage_halo(step):
        cells = x[step, pl.ds(2, ROWS), pl.ds(0, WIDE), :].astype(BF16).reshape(CELLS, FEAT)
        picked = dot(pick_sides, cells).astype(BF16)
        side_out[step] = picked.reshape(2, 2 * ROWS, FEAT)
        for at, (r, c) in enumerate(corner_cells):
            corner_out[step, at, pl.ds(0, 1), :] = x[step, r, pl.ds(c, 1), :]

    def place_halo(step):
        sides = dot(place_sides, side_in[step].reshape(4 * ROWS, FEAT))
        x[step, pl.ds(2, ROWS), pl.ds(WIDE, 8), :] = sides.reshape(ROWS, 8, FEAT)
        for at, (r, c) in enumerate(corner_slots):
            x[step, r, pl.ds(c, 1), :] = corner_in[step, at, pl.ds(0, 1), :]

    corner_out[...] = jnp.zeros_like(corner_out)
    stage_halo(0)
    for side in range(2):
        for at in range(2):
            wside_out[side, at] = wind[pl.ds(2, ROWS), side_cells[side][at], :]
    for at, (r, c) in enumerate(corner_cells):
        corner_out[0, at, pl.ds(1, 1), pl.ds(0, 128)] = wind[r, pl.ds(c, 1), :]

    owner_row = lax.broadcasted_iota(jnp.int32, (pairs, 128), 0) % BLKS
    owner_tile = jnp.zeros((pairs, 128), F32)
    for blk in range(BLKS):
        place = slot_of(owner[0, blk] // near, owner[0, blk] % near)
        owner_tile = jnp.where(owner_row == blk, place.astype(F32), owner_tile)
    owner_out[...] = owner_tile

    pl.semaphore_wait(barrier, n_lon - 1 + 6)

    winds = wind_copies()
    first = halo_copies(0)
    for copy in winds + first:
        copy.start()

    def tell_owner(step, carry):
        there = lax.rem(me + step, n_lon)
        remote(owner_out, owner_in.at[my_slot], own_send.at[0], own_recv.at[0], (me_lat, there)).start()
        return carry

    lax.fori_loop(1, n_lon, tell_owner, 0)
    pltpu.make_async_copy(owner_out, owner_in.at[my_slot], own_recv.at[0]).start()

    def main_row(cell):
        blk, at = cell // (PART // BLKS), cell % (PART // BLKS)
        return at // piece * msg + at % piece * BLKS + blk

    def pair_row(cell):
        blk, at = cell // (PART // BLKS), cell % (PART // BLKS)
        return at // piece * pairs + at % (piece // 2) * BLKS + blk

    def upper(cell):
        return cell % piece >= piece // 2

    to_i, from_i = iota(PART, PART)
    shuffle = one_hot(to_i == main_row(from_i))
    unshuffle = one_hot(main_row(to_i) == from_i)
    to_i, from_i = iota(PART // 2, PART)
    pair_low = one_hot((to_i == pair_row(from_i)) & ~upper(from_i))
    pair_high = one_hot((to_i == pair_row(from_i)) & upper(from_i))
    to_i, from_i = iota(PART, PART // 2)
    unpair = one_hot(pair_row(to_i) == from_i)
    to_i, from_i = iota(PART, 128)
    is_upper = upper(to_i)
    in_low = from_i < TAIL

    for copy in winds + first:
        copy.wait_recv()
    for side in range(2):
        for at in range(2):
            wind[pl.ds(2, ROWS), side_slots[side][at], :] = wside_in[side, at]
    for at, (r, c) in enumerate(corner_slots):
        wind[r, pl.ds(c, 1), :] = corner_in[0, at, pl.ds(1, 1), pl.ds(0, 128)]
    place_halo(0)

    first_row = me_lat * ROWS
    last_face = n_lat * ROWS - 1
    low_half = lax.broadcasted_iota(jnp.int32, (EXT_C, 128), 1) < LEVELS

    def both(row):
        turned = pltpu.roll(row, LEVELS, axis=1)
        return jnp.where(low_half, row, turned), jnp.where(low_half, turned, row)

    def face_north(r, here, above):
        j = first_row + r - 2
        keep = jnp.where((j >= 0) & (j < last_face), 0.5, 0.0)
        return (here + above) * keep

    def make_coef(r, carry):
        e_here, n_here, s_face = carry
        e_high, n_high = both(wind[r + 1])
        e_face = 0.5 * (e_here + roll(e_here, -1))
        w_face = roll(e_face, 1)
        n_face = face_north(r, n_here, n_high)
        e_neg, w_pos = jnp.minimum(e_face, 0.0), jnp.maximum(w_face, 0.0)
        n_neg, s_pos = jnp.minimum(n_face, 0.0), jnp.maximum(s_face, 0.0)
        coef[0, r] = 1.0 - (e_face - e_neg) + (w_face - w_pos) - (n_face - n_neg) + (s_face - s_pos)
        coef[1, r] = -e_neg
        coef[2, r] = w_pos
        coef[3, r] = -n_neg
        coef[4, r] = s_pos
        return e_high, n_high, n_face

    _, n_first = both(wind[0])
    e_second, n_second = both(wind[1])
    below = face_north(0, n_first, n_second)
    lax.fori_loop(1, EXT_R - 1, make_coef, (e_second, n_second, below), unroll=2)

    def advected(grid, r, cols):
        at = pl.ds(0, cols)
        here, east_of, west_of, north_of, south_of = (coef[k, r, at, :] for k in range(5))
        out_tiles = []
        for lo, hi in TILES:
            lanes = pl.ds(lo, hi - lo)
            keep = slice(0, hi - lo)
            q = grid[r, :, lanes]
            out_tiles.append(
                here[:, keep] * q[:cols]
                + east_of[:, keep] * roll(q, -1)[:cols]
                + west_of[:, keep] * roll(q, 1)[:cols]
                + north_of[:, keep] * grid[r + 1, at, lanes]
                + south_of[:, keep] * grid[r - 1, at, lanes]
            )
        return out_tiles

    def send_to(step, phase, send, recv, key, y, z, may_be_me):
        there = slot_of(y, z)
        arrive = ex_recv.at[step, phase, key]

        def start():
            remote(
                send.at[step, there],
                recv.at[step, my_slot],
                ex_send.at[step, phase],
                arrive,
                (me_lat, y * near + z),
            ).start()

        if not may_be_me:
            start()
            return
        pl.when(there != my_slot)(start)

        @pl.when(there == my_slot)
        def _():
            pltpu.make_async_copy(send.at[step, there], recv.at[step, my_slot], arrive).start()

    def row_at(turn):
        step = row_order[-1]
        for at, value in enumerate(row_order[:-1]):
            step = jnp.where(turn == at, value, step)
        return lax.rem(my_y + step, GROUPS)

    def send_class(step, phase, send, recv, cls):
        def one_row(turn, carry):
            y = row_at(turn)
            turn_of = (cls + my_y + 2 * CLASSES - my_class - y + GROUPS * CLASSES) % CLASSES
            for steps in zip(*class_steps):
                z_step = steps[0]
                for at, value in enumerate(steps[1:]):
                    z_step = jnp.where(turn_of == at + 1, value, z_step)
                z = lax.rem(my_z + z_step, near)
                send_to(step, phase, send, recv, 0, y, z, 0 in steps)
            return carry

        lax.fori_loop(0, GROUPS, one_row, 0)

    def send_row(step, phase, send, recv, y):
        for near_step in all_steps:
            z = lax.rem(my_z + near_step, near)
            send_to(step, phase, send, recv, my_class, y, z, near_step == 0)

    def arrived(step, phase, recv, count, key):
        part = recv.at[step, pl.ds(0, count)]
        pltpu.make_async_copy(part, part, ex_recv.at[step, phase, key]).wait()

    def main_of(buf, step, first, count):
        part = buf[step, pl.ds(first, count)]
        low = part[:, :msg].reshape(count * msg, 128)
        high = part[:, msg : 2 * msg].reshape(count * msg, 128)
        pair = part[:, 2 * msg :].reshape(count * pairs, 128)
        return low, high, pair

    def class_of_buf(buf, step, cls):
        parts = [main_of(buf, step, y * near + cls * half, half) for y in range(GROUPS)]
        low, high, pair = (jnp.concatenate(some, axis=0) for some in zip(*parts))
        return jnp.concatenate([low, high], axis=1), pair

    def put(buf, step, first, count, main, pair):
        main, pair = main.astype(BF16), pair.astype(BF16)
        where = pl.ds(first, count)
        buf[step, where, pl.ds(0, msg), :] = main[:, :128].reshape(count, msg, 128)
        buf[step, where, pl.ds(msg, msg), :] = main[:, 128:].reshape(count, msg, 128)
        buf[step, where, pl.ds(2 * msg, pairs), :] = pair.reshape(count, pairs, 128)

    def put_class(buf, step, cls, main, pair):
        for y in range(GROUPS):
            rows = slice(y * half * msg, (y + 1) * half * msg)
            pair_rows = slice(y * half * pairs, (y + 1) * half * pairs)
            put(buf, step, y * near + cls * half, half, main[rows], pair[pair_rows])

    def dot_t(a, b):
        return lax.dot_general(a, b, (((1,), (1,)), ((), ())), preferred_element_type=F32)

    def reorder(step, phase, held, send, recv, order, tail_order):
        low, high, pair = main_of(held, step, 0, n_lon)
        main = jnp.concatenate([low, high], axis=1)

        def one_row(turn, carry):
            y = row_at(turn)
            moved = dot(order[pl.ds(y * near * msg, near * msg), :], main)
            moved_pair = dot(tail_order[pl.ds(y * near * pairs, near * pairs), :], pair)
            put(send, step, y * near, near, moved, moved_pair)
            send_row(step, phase, send, recv, y)
            return carry

        lax.fori_loop(0, GROUPS, one_row, 0)

    for step in range(STEPS):
        if step:
            copies = halo_copies(step)
            for copy in copies[:2]:
                copy.start()
            stage_halo(step)
            for copy in copies[2:]:
                copy.start()
            for copy in copies:
                copy.wait_recv()
            place_halo(step)

        def sweep_one(r, carry):
            for (lo, hi), new in zip(TILES, advected(x.at[step], r, EXT_C)):
                z[r, :, pl.ds(lo, hi - lo)] = new
            return carry

        lax.fori_loop(1, EXT_R - 1, sweep_one, 0, unroll=2)

        def sweep_two(cls, t):
            j = t // BAND * 8 + cls * BAND + t % BAND
            for (lo, hi), new in zip(TILES, advected(z, j + 2, WIDE)):
                if step + 1 < STEPS:
                    x[step + 1, j + 2, pl.ds(0, WIDE), pl.ds(lo, hi - lo)] = new
                else:
                    result[j, :, pl.ds(lo, hi - lo)] = new
                if hi == FEAT:
                    new = jnp.concatenate([new, new], axis=1)
                cur_bf[cls * (ROWS // CLASSES) + t, :, pl.ds(lo, 128)] = new.astype(BF16)

        def spread(cls, carry):
            def sweep_some(t, carry):
                for at in range(4):
                    sweep_two(cls, 4 * t + at)
                return carry

            lax.fori_loop(0, ROWS // CLASSES // 4, sweep_some, 0)
            cells = cur_bf[pl.ds(cls * (ROWS // CLASSES), ROWS // CLASSES)].reshape(PART, 384)
            tails = cells[:, MAIN:]
            moved = dot(shuffle, cells[:, :MAIN])
            moved_pair = jnp.where(in_low[: PART // 2], dot(pair_low, tails), dot(pair_high, tails))
            put_class(send_one, step, cls, moved, moved_pair)
            send_class(step, 0, send_one, recv_one, cls)
            return carry

        lax.fori_loop(0, CLASSES, spread, 0)

        if step == 0:
            pltpu.make_async_copy(owner_in, owner_in, own_recv.at[0]).wait()
            count = n_lon * pairs
            scheme = owner_in[...].reshape(count, 128)
            lane = lax.broadcasted_iota(jnp.int32, (count, 128), 1).astype(F32)
            hit = jnp.where(scheme == lane, 1.0, 0.0)
            to_i, from_i = iota(count, count)
            order_to = to_i // pairs * BLKS + to_i % BLKS
            order_from = from_i // pairs * BLKS + from_i % BLKS
            before = (order_from < order_to) & (from_i % pairs < BLKS)
            ahead = dot(one_hot(before), hit.astype(BF16))
            rank = jnp.sum(hit * ahead, axis=1, keepdims=True)
            row = lax.broadcasted_iota(jnp.int32, (count, 1), 0) % pairs
            inside = rank + (row // BLKS * BLKS).astype(F32)
            tail_place = scheme[:, :1] * pairs + inside
            place = (scheme[:, :1] * msg + inside).reshape(n_lon, pairs, 1)
            place = jnp.concatenate([place, place + pairs], axis=1).reshape(n_lon * msg, 1)

            def ordered(column, size):
                row = jnp.broadcast_to(column, (size, 128)).T[:1]
                to_i, _ = iota(size, size)
                return one_hot(to_i.astype(F32) == row)

            tail_perm[...] = ordered(tail_place, count)
            perm[...] = ordered(place, n_lon * msg)

        arrived(step, 0, recv_one, n_lon, 0)
        reorder(step, 1, recv_one, send_two, recv_two, perm, tail_perm)

        if step == 0:
            _, from_i = iota(n_lon * pairs, n_lon * pairs)
            tail_perm_t[...] = one_hot(from_i.astype(F32) == tail_place)
            _, from_i = iota(n_lon * msg, n_lon * msg)
            perm_t[...] = one_hot(from_i.astype(F32) == place)
            for load in loads[3:]:
                load.wait()
            tail_first[...] = jnp.zeros_like(tail_first)
            tail_last[...] = jnp.zeros_like(tail_last)
            for at in range(2):
                where = (pl.ds(at * TAIL, TAIL), pl.ds(at * HID, HID))
                tail_first[where] = v_in[0, pl.ds(MAIN, TAIL), :]
                tail_last[where] = v_out[0, pl.ds(MAIN, TAIL), :]

        def physics(cls, carry):
            arrived(step, 1, recv_two, n_lon // CLASSES, cls)
            main, pair = class_of_buf(recv_two, step, cls)
            hidden = dot(main, v_in[0, pl.ds(0, MAIN), :])
            extra = dot(pair, tail_first[...])
            extra = extra.reshape(n_lon // CLASSES, pairs, 2 * HID)
            extra = jnp.concatenate([extra[:, :, :HID], extra[:, :, HID:]], axis=1)
            hidden = silu(hidden + extra.reshape(PART, HID)).astype(BF16)
            hidden = silu(dot(hidden, v_two[0])).astype(BF16)
            hidden = silu(dot(hidden, v_three[0]))
            tendency = dot_t(hidden.astype(BF16), v_out[0, pl.ds(0, MAIN), :])
            hidden = hidden.reshape(n_lon // CLASSES, msg, HID)
            both_cells = jnp.concatenate([hidden[:, :pairs], hidden[:, pairs:]], axis=2)
            both_cells = both_cells.reshape(PART // 2, 2 * HID).astype(BF16)
            put_class(send_three, step, cls, tendency, dot_t(both_cells, tail_last[...]))
            send_class(step, 2, send_three, recv_three, cls)
            return carry

        lax.fori_loop(0, CLASSES, physics, 0)

        arrived(step, 2, recv_three, n_lon, 0)
        reorder(step, 3, recv_three, send_four, recv_four, perm_t, tail_perm_t)

        def add_home(cls, carry):
            arrived(step, 3, recv_four, n_lon // CLASSES, cls)
            main, pair = class_of_buf(recv_four, step, cls)
            home = dot(unshuffle, main)
            tail = dot(unpair, pair)
            tail = jnp.where(is_upper, pltpu.roll(tail, TAIL, axis=1), tail)
            for blk in range(BLKS):
                for r in range(BAND):
                    j = 8 * blk + BAND * cls + r
                    lo = (BAND * blk + r) * WIDE
                    first_cell = (BAND * cls + r) * WIDE
                    for at, hi in ((0, MAIN), (MAIN, FEAT)):
                        part = home if at == 0 else tail[:, :TAIL]
                        part = part[lo : lo + WIDE]
                        cell = first_cell + lax.broadcasted_iota(jnp.int32, part.shape, 0)
                        added = jnp.where(cell < counts[0, blk], part, 0.0)
                        lanes = pl.ds(at, hi - at)
                        if step + 1 < STEPS:
                            x[step + 1, j + 2, pl.ds(0, WIDE), lanes] += added
                        else:
                            result[j, :, lanes] += added
                if step + 1 == STEPS:
                    some = pl.ds(8 * blk + BAND * cls, BAND)
                    pltpu.make_async_copy(result.at[some], out.at[some], out_sem.at[0]).start()
            return carry

        lax.fori_loop(0, CLASSES, add_home, 0)

    for copy in winds:
        copy.wait_send()
    for step in range(STEPS):
        for copy in halo_copies(step):
            copy.wait_send()
        for phase, send in enumerate((send_one, send_two, send_three, send_four)):
            sent = send.at[step, pl.ds(0, n_lon - 1)]
            pltpu.make_async_copy(sent, sent, ex_send.at[step, phase]).wait()
    sent = owner_in.at[pl.ds(0, n_lon - 1)]
    pltpu.make_async_copy(sent, sent, own_send.at[0]).wait()
    pltpu.make_async_copy(result, out, out_sem.at[0]).wait()


def solution(mesh):
    n_lat, n_lon = mesh.shape["lat"], mesh.shape["lon"]
    msg = BLKS * COLS // n_lon
    rows = msg * FEAT // 128
    any_spec = pl.BlockSpec(memory_space=pl.ANY)
    smem = pl.BlockSpec(memory_space=pltpu.SMEM)
    dma = pltpu.SemaphoreType.DMA
    vmem = pltpu.VMEM
    scratch = [
        vmem((STEPS, EXT_R, EXT_C, FEAT), F32),
        vmem((EXT_R, EXT_C, FEAT), F32),
        vmem((EXT_R, EXT_C, 2 * LEVELS), F32),
        vmem((ROWS, WIDE, LEVELS), F32),
        vmem((ROWS, WIDE, LEVELS), F32),
        vmem((5, EXT_R, EXT_C, 128), F32),
        vmem((STEPS, 2, 2 * ROWS, FEAT), BF16),
        vmem((STEPS, 2, 2 * ROWS, FEAT), BF16),
        vmem((2, 2, ROWS, 128), F32),
        vmem((2, 2, ROWS, 128), F32),
        vmem((STEPS, 4, 8, FEAT), F32),
        vmem((STEPS, 4, 8, FEAT), F32),
        vmem((ROWS, WIDE, 384), BF16),
    ]
    scratch += [vmem((STEPS, n_lon, rows, 128), BF16)] * 8
    scratch += [
        vmem((msg // 2, 128), F32),
        vmem((n_lon, msg // 2, 128), F32),
        vmem((CELLS, CELLS), BF16),
        vmem((CELLS, CELLS), BF16),
        vmem((CELLS // 2, CELLS // 2), BF16),
        vmem((CELLS // 2, CELLS // 2), BF16),
        vmem((ROWS, WIDE, FEAT), F32),
        vmem((1, FEAT, HID), BF16),
        vmem((1, HID, HID), BF16),
        vmem((1, HID, HID), BF16),
        vmem((1, FEAT, HID), BF16),
        vmem((2 * TAIL, 2 * HID), BF16),
        vmem((2 * TAIL, 2 * HID), BF16),
        dma((7,)),
        dma((STEPS, 8)),
        dma((STEPS, 8)),
        dma((4,)),
        dma((4,)),
        dma((1,)),
        dma((1,)),
        dma((STEPS, 4)),
        dma((STEPS, 4, CLASSES)),
        dma((1,)),
    ]

    call = pl.pallas_call(
        functools.partial(kernel, n_lat, n_lon),
        out_shape=jax.ShapeDtypeStruct((ROWS, WIDE, FEAT), F32),
        in_specs=[any_spec] * 3 + [smem] * 2 + [any_spec] * 4,
        out_specs=any_spec,
        scratch_shapes=scratch,
        compiler_params=pltpu.CompilerParams(
            collective_id=0, has_side_effects=True, vmem_limit_bytes=60 * 1024 * 1024
        ),
        name="coupled_steps",
    )

    def local(fields, wind_east, wind_north, owner, counts, w_in, w_two, w_three, w_out):
        w_out = jnp.swapaxes(w_out, 1, 2)
        return call(fields, wind_east, wind_north, owner, counts, w_in, w_two, w_three, w_out)

    return jax.shard_map(
        local,
        mesh=mesh,
        in_specs=(
            P("lat", "lon", None),
            P("lat", "lon", None),
            P("lat", "lon", None),
            P("lat", "lon"),
            P("lat", "lon"),
            P("lon", None, None),
            P("lon", None, None),
            P("lon", None, None),
            P("lon", None, None),
        ),
        out_specs=P("lat", "lon", None),
        check_vma=False,
    )
```

```python
import functools

import jax
import jax.numpy as jnp
from jax import lax
from jax.experimental import pallas as pl
from jax.experimental.pallas import tpu as pltpu
from jax.sharding import PartitionSpec as P

F32 = jnp.float32
BF16 = jnp.bfloat16
MESH = pl.DeviceIdType.MESH

STEPS = 2
COLS = 128
ROWS = 32
WIDE = 16
FEAT = 320
LEVELS = 64
HID = 512
BLKS = 4
GROUPS = 4
EXT_R = ROWS + 4
EXT_C = 24
CELLS = ROWS * WIDE
CLASSES = 2
PART = CELLS // CLASSES
BAND = 8 // CLASSES
MAIN = 256
TILES = ((0, 128), (128, 256), (256, 320))
TAIL = FEAT - MAIN


def silu(x):
    half = 0.5 * x
    return half + half * jnp.tanh(half)


def roll(x, shift):
    return pltpu.roll(x, shift % x.shape[0], axis=0)


def kernel(
    n_lat,
    n_lon,
    fields,
    wind_east,
    wind_north,
    owner,
    counts,
    w_in,
    w_two,
    w_three,
    w_out,
    out,
    x,
    z,
    wind,
    raw_east,
    raw_north,
    coef,
    side_out,
    side_in,
    wside_out,
    wside_in,
    corner_out,
    corner_in,
    cur_bf,
    send_one,
    recv_one,
    send_two,
    recv_two,
    send_three,
    recv_three,
    send_four,
    recv_four,
    owner_out,
    owner_in,
    perm,
    perm_t,
    tail_perm,
    tail_perm_t,
    result,
    v_in,
    v_two,
    v_three,
    v_out,
    tail_first,
    tail_last,
    load_sem,
    halo_send,
    halo_recv,
    wind_send,
    wind_recv,
    own_send,
    own_recv,
    ex_send,
    ex_recv,
    out_sem,
):
    near = n_lon // GROUPS
    half = near // CLASSES
    piece = COLS // n_lon
    msg = BLKS * piece
    pairs = msg // 2
    me_lat = lax.axis_index("lat")
    me = lax.axis_index("lon")
    my_y = me // near
    my_z = me % near
    north = lax.rem(me_lat + 1, n_lat)
    south = lax.rem(me_lat + n_lat - 1, n_lat)
    east = lax.rem(me + 1, n_lon)
    west = lax.rem(me + n_lon - 1, n_lon)
    corners = ((south, west), (south, east), (north, west), (north, east))

    def class_of(y, z):
        return (y + z + me_lat) % CLASSES

    def slot_of(y, z):
        return y * near + class_of(y, z) * half + z // CLASSES

    my_class = class_of(my_y, my_z)
    my_slot = slot_of(my_y, my_z)

    def hops(step, count):
        return min(step, count - step)

    row_order = sorted(range(GROUPS), key=lambda step: -hops(step, GROUPS))
    all_steps = sorted(range(near), key=lambda step: -hops(step, near))
    class_steps = [[step for step in all_steps if step % CLASSES == c] for c in range(CLASSES)]

    loads = [
        pltpu.make_async_copy(wind_east, raw_east, load_sem.at[0]),
        pltpu.make_async_copy(wind_north, raw_north, load_sem.at[1]),
        pltpu.make_async_copy(
            fields, x.at[0, pl.ds(2, ROWS), pl.ds(0, WIDE), :], load_sem.at[2]
        ),
        pltpu.make_async_copy(w_in, v_in, load_sem.at[3]),
        pltpu.make_async_copy(w_two, v_two, load_sem.at[4]),
        pltpu.make_async_copy(w_three, v_three, load_sem.at[5]),
        pltpu.make_async_copy(w_out, v_out, load_sem.at[6]),
    ]
    for load in loads[:3]:
        load.start()

    barrier = pltpu.get_barrier_semaphore()

    def greet(step, carry):
        pl.semaphore_signal(
            barrier,
            inc=1,
            device_id=(me_lat, lax.rem(me + step, n_lon)),
            device_id_type=MESH,
        )
        return carry

    lax.fori_loop(1, n_lon, greet, 0)
    for there in ((south, me), (north, me)) + corners:
        pl.semaphore_signal(barrier, inc=1, device_id=there, device_id_type=MESH)

    def clear(r, carry):
        x[0, r, pl.ds(WIDE, 8), :] = jnp.zeros((8, FEAT), F32)
        x[1, r, pl.ds(WIDE, 8), :] = jnp.zeros((8, FEAT), F32)
        wind[r, pl.ds(WIDE, 8), :] = jnp.zeros((8, 2 * LEVELS), F32)
        return carry

    lax.fori_loop(0, EXT_R, clear, 0)

    loads[0].wait()
    loads[1].wait()

    def join(r, carry):
        wind[r + 2, pl.ds(0, WIDE), :] = jnp.concatenate([raw_east[r], raw_north[r]], axis=-1)
        return carry

    lax.fori_loop(0, ROWS, join, 0)
    loads[2].wait()

    def remote(src, dst, send, recv, where):
        return pltpu.make_async_remote_copy(
            src_ref=src,
            dst_ref=dst,
            send_sem=send,
            recv_sem=recv,
            device_id=where,
            device_id_type=MESH,
        )

    def halo_copies(step):
        grid = x.at[step]
        inner = pl.ds(0, WIDE)
        copies = [
            remote(
                grid.at[pl.ds(2, 2), inner, :],
                grid.at[pl.ds(ROWS + 2, 2), inner, :],
                halo_send.at[step, 0],
                halo_recv.at[step, 0],
                (south, me),
            ),
            remote(
                grid.at[pl.ds(ROWS, 2), inner, :],
                grid.at[pl.ds(0, 2), inner, :],
                halo_send.at[step, 1],
                halo_recv.at[step, 1],
                (north, me),
            ),
        ]
        for side, there in enumerate((west, east)):
            copies.append(
                remote(
                    side_out.at[step, side],
                    side_in.at[step, side],
                    halo_send.at[step, 2 + side],
                    halo_recv.at[step, 2 + side],
                    (me_lat, there),
                )
            )
        for at, there in enumerate(corners):
            copies.append(
                remote(
                    corner_out.at[step, at],
                    corner_in.at[step, at],
                    halo_send.at[step, 4 + at],
                    halo_recv.at[step, 4 + at],
                    there,
                )
            )
        return copies

    def wind_copies():
        inner = pl.ds(0, WIDE)
        copies = [
            remote(
                wind.at[pl.ds(2, 2), inner, :],
                wind.at[pl.ds(ROWS + 2, 2), inner, :],
                wind_send.at[0],
                wind_recv.at[0],
                (south, me),
            ),
            remote(
                wind.at[pl.ds(ROWS, 2), inner, :],
                wind.at[pl.ds(0, 2), inner, :],
                wind_send.at[1],
                wind_recv.at[1],
                (north, me),
            ),
        ]
        for side, there in enumerate((west, east)):
            copies.append(
                remote(
                    wside_out.at[side],
                    wside_in.at[side],
                    wind_send.at[2 + side],
                    wind_recv.at[2 + side],
                    (me_lat, there),
                )
            )
        return copies

    corner_cells = ((2, 0), (2, WIDE - 1), (ROWS + 1, 0), (ROWS + 1, WIDE - 1))
    corner_slots = ((ROWS + 2, 16), (ROWS + 2, 23), (1, 16), (1, 23))
    side_cells = ((0, 1), (WIDE - 2, WIDE - 1))
    side_slots = ((16, 17), (22, 23))

    def iota(rows, cols):
        return (
            lax.broadcasted_iota(jnp.int32, (rows, cols), 0),
            lax.broadcasted_iota(jnp.int32, (rows, cols), 1),
        )

    def one_hot(where):
        return jnp.where(where, 1.0, 0.0).astype(BF16)

    def dot(a, b):
        return jnp.dot(a, b, preferred_element_type=F32)

    to_i, from_i = iota(4 * ROWS, CELLS)
    side, second = to_i // (2 * ROWS), to_i // ROWS % 2
    pick_sides = one_hot(from_i == to_i % ROWS * WIDE + side * (WIDE - 2) + second)
    to_i, from_i = iota(8 * ROWS, 4 * ROWS)
    side, second = from_i // (2 * ROWS), from_i // ROWS % 2
    place_sides = one_hot(
        (to_i // 8 == from_i % ROWS) & (to_i % 8 == side * (EXT_C - WIDE - 2) + second)
    )

    def stage_halo(step):
        cells = x[step, pl.ds(2, ROWS), pl.ds(0, WIDE), :].astype(BF16).reshape(CELLS, FEAT)
        picked = dot(pick_sides, cells).astype(BF16)
        side_out[step] = picked.reshape(2, 2 * ROWS, FEAT)
        for at, (r, c) in enumerate(corner_cells):
            corner_out[step, at, pl.ds(0, 1), :] = x[step, r, pl.ds(c, 1), :]

    def place_halo(step):
        sides = dot(place_sides, side_in[step].reshape(4 * ROWS, FEAT))
        x[step, pl.ds(2, ROWS), pl.ds(WIDE, 8), :] = sides.reshape(ROWS, 8, FEAT)
        for at, (r, c) in enumerate(corner_slots):
            x[step, r, pl.ds(c, 1), :] = corner_in[step, at, pl.ds(0, 1), :]

    corner_out[...] = jnp.zeros_like(corner_out)
    stage_halo(0)
    for side in range(2):
        for at in range(2):
            wside_out[side, at] = wind[pl.ds(2, ROWS), side_cells[side][at], :]
    for at, (r, c) in enumerate(corner_cells):
        corner_out[0, at, pl.ds(1, 1), pl.ds(0, 128)] = wind[r, pl.ds(c, 1), :]

    owner_row = lax.broadcasted_iota(jnp.int32, (pairs, 128), 0) % BLKS
    owner_tile = jnp.zeros((pairs, 128), F32)
    for blk in range(BLKS):
        place = slot_of(owner[0, blk] // near, owner[0, blk] % near)
        owner_tile = jnp.where(owner_row == blk, place.astype(F32), owner_tile)
    owner_out[...] = owner_tile

    pl.semaphore_wait(barrier, n_lon - 1 + 6)

    winds = wind_copies()
    first = halo_copies(0)
    for copy in winds + first:
        copy.start()
    for load in loads[3:]:
        load.start()

    def tell_owner(step, carry):
        there = lax.rem(me + step, n_lon)
        remote(owner_out, owner_in.at[my_slot], own_send.at[0], own_recv.at[0], (me_lat, there)).start()
        return carry

    lax.fori_loop(1, n_lon, tell_owner, 0)
    pltpu.make_async_copy(owner_out, owner_in.at[my_slot], own_recv.at[0]).start()

    def main_row(cell):
        blk, at = cell // (PART // BLKS), cell % (PART // BLKS)
        return at // piece * msg + at % piece * BLKS + blk

    def pair_row(cell):
        blk, at = cell // (PART // BLKS), cell % (PART // BLKS)
        return at // piece * pairs + at % (piece // 2) * BLKS + blk

    def upper(cell):
        return cell % piece >= piece // 2

    to_i, from_i = iota(PART, PART)
    shuffle = one_hot(to_i == main_row(from_i))
    unshuffle = one_hot(main_row(to_i) == from_i)
    to_i, from_i = iota(PART // 2, PART)
    pair_low = one_hot((to_i == pair_row(from_i)) & ~upper(from_i))
    pair_high = one_hot((to_i == pair_row(from_i)) & upper(from_i))
    to_i, from_i = iota(PART, PART // 2)
    unpair = one_hot(pair_row(to_i) == from_i)
    to_i, from_i = iota(PART, 128)
    is_upper = upper(to_i)
    in_low = from_i < TAIL

    for copy in winds + first:
        copy.wait_recv()
    for side in range(2):
        for at in range(2):
            wind[pl.ds(2, ROWS), side_slots[side][at], :] = wside_in[side, at]
    for at, (r, c) in enumerate(corner_slots):
        wind[r, pl.ds(c, 1), :] = corner_in[0, at, pl.ds(1, 1), pl.ds(0, 128)]
    place_halo(0)

    first_row = me_lat * ROWS
    last_face = n_lat * ROWS - 1
    low_half = lax.broadcasted_iota(jnp.int32, (EXT_C, 128), 1) < LEVELS

    def both(row):
        turned = pltpu.roll(row, LEVELS, axis=1)
        return jnp.where(low_half, row, turned), jnp.where(low_half, turned, row)

    def face_north(r, here, above):
        j = first_row + r - 2
        keep = jnp.where((j >= 0) & (j < last_face), 0.5, 0.0)
        return (here + above) * keep

    def make_coef(r, carry):
        e_here, n_here, s_face = carry
        e_high, n_high = both(wind[r + 1])
        e_face = 0.5 * (e_here + roll(e_here, -1))
        w_face = roll(e_face, 1)
        n_face = face_north(r, n_here, n_high)
        e_neg, w_pos = jnp.minimum(e_face, 0.0), jnp.maximum(w_face, 0.0)
        n_neg, s_pos = jnp.minimum(n_face, 0.0), jnp.maximum(s_face, 0.0)
        coef[0, r] = 1.0 - (e_face - e_neg) + (w_face - w_pos) - (n_face - n_neg) + (s_face - s_pos)
        coef[1, r] = -e_neg
        coef[2, r] = w_pos
        coef[3, r] = -n_neg
        coef[4, r] = s_pos
        return e_high, n_high, n_face

    _, n_first = both(wind[0])
    e_second, n_second = both(wind[1])
    below = face_north(0, n_first, n_second)
    lax.fori_loop(1, EXT_R - 1, make_coef, (e_second, n_second, below), unroll=2)

    def advected(grid, r, cols):
        at = pl.ds(0, cols)
        here, east_of, west_of, north_of, south_of = (coef[k, r, at, :] for k in range(5))
        out_tiles = []
        for lo, hi in TILES:
            lanes = pl.ds(lo, hi - lo)
            keep = slice(0, hi - lo)
            q = grid[r, :, lanes]
            out_tiles.append(
                here[:, keep] * q[:cols]
                + east_of[:, keep] * roll(q, -1)[:cols]
                + west_of[:, keep] * roll(q, 1)[:cols]
                + north_of[:, keep] * grid[r + 1, at, lanes]
                + south_of[:, keep] * grid[r - 1, at, lanes]
            )
        return out_tiles

    def send_to(step, phase, send, recv, key, y, z, may_be_me):
        there = slot_of(y, z)
        arrive = ex_recv.at[step, phase, key]

        def start():
            remote(
                send.at[step, there],
                recv.at[step, my_slot],
                ex_send.at[step, phase],
                arrive,
                (me_lat, y * near + z),
            ).start()

        if not may_be_me:
            start()
            return
        pl.when(there != my_slot)(start)

        @pl.when(there == my_slot)
        def _():
            pltpu.make_async_copy(send.at[step, there], recv.at[step, my_slot], arrive).start()

    def row_at(turn):
        step = row_order[-1]
        for at, value in enumerate(row_order[:-1]):
            step = jnp.where(turn == at, value, step)
        return lax.rem(my_y + step, GROUPS)

    def send_class(step, phase, send, recv, cls):
        def one_row(turn, carry):
            y = row_at(turn)
            turn_of = (cls + my_y + 2 * CLASSES - my_class - y + GROUPS * CLASSES) % CLASSES
            for steps in zip(*class_steps):
                z_step = steps[0]
                for at, value in enumerate(steps[1:]):
                    z_step = jnp.where(turn_of == at + 1, value, z_step)
                z = lax.rem(my_z + z_step, near)
                send_to(step, phase, send, recv, 0, y, z, 0 in steps)
            return carry

        lax.fori_loop(0, GROUPS, one_row, 0)

    def send_row(step, phase, send, recv, y):
        for near_step in all_steps:
            z = lax.rem(my_z + near_step, near)
            send_to(step, phase, send, recv, my_class, y, z, near_step == 0)

    def arrived(step, phase, recv, count, key):
        part = recv.at[step, pl.ds(0, count)]
        pltpu.make_async_copy(part, part, ex_recv.at[step, phase, key]).wait()

    def main_of(buf, step, first, count):
        part = buf[step, pl.ds(first, count)]
        low = part[:, :msg].reshape(count * msg, 128)
        high = part[:, msg : 2 * msg].reshape(count * msg, 128)
        pair = part[:, 2 * msg :].reshape(count * pairs, 128)
        return low, high, pair

    def class_of_buf(buf, step, cls):
        parts = [main_of(buf, step, y * near + cls * half, half) for y in range(GROUPS)]
        low, high, pair = (jnp.concatenate(some, axis=0) for some in zip(*parts))
        return jnp.concatenate([low, high], axis=1), pair

    def put(buf, step, first, count, main, pair):
        main, pair = main.astype(BF16), pair.astype(BF16)
        where = pl.ds(first, count)
        buf[step, where, pl.ds(0, msg), :] = main[:, :128].reshape(count, msg, 128)
        buf[step, where, pl.ds(msg, msg), :] = main[:, 128:].reshape(count, msg, 128)
        buf[step, where, pl.ds(2 * msg, pairs), :] = pair.reshape(count, pairs, 128)

    def put_class(buf, step, cls, main, pair):
        for y in range(GROUPS):
            rows = slice(y * half * msg, (y + 1) * half * msg)
            pair_rows = slice(y * half * pairs, (y + 1) * half * pairs)
            put(buf, step, y * near + cls * half, half, main[rows], pair[pair_rows])

    def dot_t(a, b):
        return lax.dot_general(a, b, (((1,), (1,)), ((), ())), preferred_element_type=F32)

    def reorder(step, phase, held, send, recv, order, tail_order):
        low, high, pair = main_of(held, step, 0, n_lon)
        main = jnp.concatenate([low, high], axis=1)

        def one_row(turn, carry):
            y = row_at(turn)
            moved = dot(order[pl.ds(y * near * msg, near * msg), :], main)
            moved_pair = dot(tail_order[pl.ds(y * near * pairs, near * pairs), :], pair)
            put(send, step, y * near, near, moved, moved_pair)
            send_row(step, phase, send, recv, y)
            return carry

        lax.fori_loop(0, GROUPS, one_row, 0)

    for step in range(STEPS):
        if step:
            copies = halo_copies(step)
            for copy in copies[:2]:
                copy.start()
            stage_halo(step)
            for copy in copies[2:]:
                copy.start()
            for copy in copies:
                copy.wait_recv()
            place_halo(step)

        def sweep_one(r, carry):
            for (lo, hi), new in zip(TILES, advected(x.at[step], r, EXT_C)):
                z[r, :, pl.ds(lo, hi - lo)] = new
            return carry

        lax.fori_loop(1, EXT_R - 1, sweep_one, 0, unroll=2)

        def sweep_two(cls, t):
            j = t // BAND * 8 + cls * BAND + t % BAND
            for (lo, hi), new in zip(TILES, advected(z, j + 2, WIDE)):
                if step + 1 < STEPS:
                    x[step + 1, j + 2, pl.ds(0, WIDE), pl.ds(lo, hi - lo)] = new
                else:
                    result[j, :, pl.ds(lo, hi - lo)] = new
                if hi == FEAT:
                    new = jnp.concatenate([new, new], axis=1)
                cur_bf[cls * (ROWS // CLASSES) + t, :, pl.ds(lo, 128)] = new.astype(BF16)

        def spread(cls, carry):
            def sweep_some(t, carry):
                for at in range(4):
                    sweep_two(cls, 4 * t + at)
                return carry

            lax.fori_loop(0, ROWS // CLASSES // 4, sweep_some, 0)
            cells = cur_bf[pl.ds(cls * (ROWS // CLASSES), ROWS // CLASSES)].reshape(PART, 384)
            tails = cells[:, MAIN:]
            moved = dot(shuffle, cells[:, :MAIN])
            moved_pair = jnp.where(in_low[: PART // 2], dot(pair_low, tails), dot(pair_high, tails))
            put_class(send_one, step, cls, moved, moved_pair)
            send_class(step, 0, send_one, recv_one, cls)
            return carry

        lax.fori_loop(0, CLASSES, spread, 0)

        if step == 0:
            pltpu.make_async_copy(owner_in, owner_in, own_recv.at[0]).wait()
            count = n_lon * pairs
            scheme = owner_in[...].reshape(count, 128)
            lane = lax.broadcasted_iota(jnp.int32, (count, 128), 1).astype(F32)
            hit = jnp.where(scheme == lane, 1.0, 0.0)
            to_i, from_i = iota(count, count)
            order_to = to_i // pairs * BLKS + to_i % BLKS
            order_from = from_i // pairs * BLKS + from_i % BLKS
            before = (order_from < order_to) & (from_i % pairs < BLKS)
            ahead = dot(one_hot(before), hit.astype(BF16))
            rank = jnp.sum(hit * ahead, axis=1, keepdims=True)
            row = lax.broadcasted_iota(jnp.int32, (count, 1), 0) % pairs
            inside = rank + (row // BLKS * BLKS).astype(F32)
            tail_place = scheme[:, :1] * pairs + inside
            place = (scheme[:, :1] * msg + inside).reshape(n_lon, pairs, 1)
            place = jnp.concatenate([place, place + pairs], axis=1).reshape(n_lon * msg, 1)

            def ordered(column, size):
                row = jnp.broadcast_to(column, (size, 128)).T[:1]
                to_i, _ = iota(size, size)
                return one_hot(to_i.astype(F32) == row)

            tail_perm[...] = ordered(tail_place, count)
            perm[...] = ordered(place, n_lon * msg)

        arrived(step, 0, recv_one, n_lon, 0)
        reorder(step, 1, recv_one, send_two, recv_two, perm, tail_perm)

        if step == 0:
            _, from_i = iota(n_lon * pairs, n_lon * pairs)
            tail_perm_t[...] = one_hot(from_i.astype(F32) == tail_place)
            _, from_i = iota(n_lon * msg, n_lon * msg)
            perm_t[...] = one_hot(from_i.astype(F32) == place)
            for load in loads[3:]:
                load.wait()
            tail_first[...] = jnp.zeros_like(tail_first)
            tail_last[...] = jnp.zeros_like(tail_last)
            for at in range(2):
                where = (pl.ds(at * TAIL, TAIL), pl.ds(at * HID, HID))
                tail_first[where] = v_in[0, pl.ds(MAIN, TAIL), :]
                tail_last[where] = v_out[0, pl.ds(MAIN, TAIL), :]

        def physics(cls, carry):
            arrived(step, 1, recv_two, n_lon // CLASSES, cls)
            main, pair = class_of_buf(recv_two, step, cls)
            hidden = dot(main, v_in[0, pl.ds(0, MAIN), :])
            extra = dot(pair, tail_first[...])
            extra = extra.reshape(n_lon // CLASSES, pairs, 2 * HID)
            extra = jnp.concatenate([extra[:, :, :HID], extra[:, :, HID:]], axis=1)
            hidden = silu(hidden + extra.reshape(PART, HID)).astype(BF16)
            hidden = silu(dot(hidden, v_two[0])).astype(BF16)
            hidden = silu(dot(hidden, v_three[0]))
            tendency = dot_t(hidden.astype(BF16), v_out[0, pl.ds(0, MAIN), :])
            hidden = hidden.reshape(n_lon // CLASSES, msg, HID)
            both_cells = jnp.concatenate([hidden[:, :pairs], hidden[:, pairs:]], axis=2)
            both_cells = both_cells.reshape(PART // 2, 2 * HID).astype(BF16)
            put_class(send_three, step, cls, tendency, dot_t(both_cells, tail_last[...]))
            send_class(step, 2, send_three, recv_three, cls)
            return carry

        lax.fori_loop(0, CLASSES, physics, 0)

        arrived(step, 2, recv_three, n_lon, 0)
        reorder(step, 3, recv_three, send_four, recv_four, perm_t, tail_perm_t)

        def add_home(cls, carry):
            arrived(step, 3, recv_four, n_lon // CLASSES, cls)
            main, pair = class_of_buf(recv_four, step, cls)
            home = dot(unshuffle, main)
            tail = dot(unpair, pair)
            tail = jnp.where(is_upper, pltpu.roll(tail, TAIL, axis=1), tail)
            for blk in range(BLKS):
                for r in range(BAND):
                    j = 8 * blk + BAND * cls + r
                    lo = (BAND * blk + r) * WIDE
                    first_cell = (BAND * cls + r) * WIDE
                    for at, hi in ((0, MAIN), (MAIN, FEAT)):
                        part = home if at == 0 else tail[:, :TAIL]
                        part = part[lo : lo + WIDE]
                        cell = first_cell + lax.broadcasted_iota(jnp.int32, part.shape, 0)
                        added = jnp.where(cell < counts[0, blk], part, 0.0)
                        lanes = pl.ds(at, hi - at)
                        if step + 1 < STEPS:
                            x[step + 1, j + 2, pl.ds(0, WIDE), lanes] += added
                        else:
                            result[j, :, lanes] += added
                if step + 1 == STEPS:
                    some = pl.ds(8 * blk + BAND * cls, BAND)
                    pltpu.make_async_copy(result.at[some], out.at[some], out_sem.at[0]).start()
            return carry

        lax.fori_loop(0, CLASSES, add_home, 0)

    for copy in winds:
        copy.wait_send()
    for step in range(STEPS):
        for copy in halo_copies(step):
            copy.wait_send()
        for phase, send in enumerate((send_one, send_two, send_three, send_four)):
            sent = send.at[step, pl.ds(0, n_lon - 1)]
            pltpu.make_async_copy(sent, sent, ex_send.at[step, phase]).wait()
    sent = owner_in.at[pl.ds(0, n_lon - 1)]
    pltpu.make_async_copy(sent, sent, own_send.at[0]).wait()
    pltpu.make_async_copy(result, out, out_sem.at[0]).wait()


def solution(mesh):
    n_lat, n_lon = mesh.shape["lat"], mesh.shape["lon"]
    msg = BLKS * COLS // n_lon
    rows = msg * FEAT // 128
    any_spec = pl.BlockSpec(memory_space=pl.ANY)
    smem = pl.BlockSpec(memory_space=pltpu.SMEM)
    dma = pltpu.SemaphoreType.DMA
    vmem = pltpu.VMEM
    scratch = [
        vmem((STEPS, EXT_R, EXT_C, FEAT), F32),
        vmem((EXT_R, EXT_C, FEAT), F32),
        vmem((EXT_R, EXT_C, 2 * LEVELS), F32),
        vmem((ROWS, WIDE, LEVELS), F32),
        vmem((ROWS, WIDE, LEVELS), F32),
        vmem((5, EXT_R, EXT_C, 128), F32),
        vmem((STEPS, 2, 2 * ROWS, FEAT), BF16),
        vmem((STEPS, 2, 2 * ROWS, FEAT), BF16),
        vmem((2, 2, ROWS, 128), F32),
        vmem((2, 2, ROWS, 128), F32),
        vmem((STEPS, 4, 8, FEAT), F32),
        vmem((STEPS, 4, 8, FEAT), F32),
        vmem((ROWS, WIDE, 384), BF16),
    ]
    scratch += [vmem((STEPS, n_lon, rows, 128), BF16)] * 8
    scratch += [
        vmem((msg // 2, 128), F32),
        vmem((n_lon, msg // 2, 128), F32),
        vmem((CELLS, CELLS), BF16),
        vmem((CELLS, CELLS), BF16),
        vmem((CELLS // 2, CELLS // 2), BF16),
        vmem((CELLS // 2, CELLS // 2), BF16),
        vmem((ROWS, WIDE, FEAT), F32),
        vmem((1, FEAT, HID), BF16),
        vmem((1, HID, HID), BF16),
        vmem((1, HID, HID), BF16),
        vmem((1, FEAT, HID), BF16),
        vmem((2 * TAIL, 2 * HID), BF16),
        vmem((2 * TAIL, 2 * HID), BF16),
        dma((7,)),
        dma((STEPS, 8)),
        dma((STEPS, 8)),
        dma((4,)),
        dma((4,)),
        dma((1,)),
        dma((1,)),
        dma((STEPS, 4)),
        dma((STEPS, 4, CLASSES)),
        dma((1,)),
    ]

    call = pl.pallas_call(
        functools.partial(kernel, n_lat, n_lon),
        out_shape=jax.ShapeDtypeStruct((ROWS, WIDE, FEAT), F32),
        in_specs=[any_spec] * 3 + [smem] * 2 + [any_spec] * 4,
        out_specs=any_spec,
        scratch_shapes=scratch,
        compiler_params=pltpu.CompilerParams(
            collective_id=0, has_side_effects=True, vmem_limit_bytes=60 * 1024 * 1024
        ),
        name="coupled_steps",
    )

    def local(fields, wind_east, wind_north, owner, counts, w_in, w_two, w_three, w_out):
        w_out = jnp.swapaxes(w_out, 1, 2)
        return call(fields, wind_east, wind_north, owner, counts, w_in, w_two, w_three, w_out)

    return jax.shard_map(
        local,
        mesh=mesh,
        in_specs=(
            P("lat", "lon", None),
            P("lat", "lon", None),
            P("lat", "lon", None),
            P("lat", "lon"),
            P("lat", "lon"),
            P("lon", None, None),
            P("lon", None, None),
            P("lon", None, None),
            P("lon", None, None),
        ),
        out_specs=P("lat", "lon", None),
        check_vma=False,
    )
```
